512 devices in a mesh: dp: 32 (over y, x, core), tensor: 16 (over z).
Axes of the slice: x: 4, y: 4, z: 16, core: 2. Of those that a mesh axis runs over, the one named last changes fastest.
Arguments:
- gradient: bfloat16 [32, 512, 8192], P('dp', 'tensor'), may hold values from -50 to 50
- feedback: float32 [32, 512, 8192], P('dp', 'tensor'), may hold values from -4 to 4
- momentum: float32 [512, 8192], P('tensor'), may hold values from -6 to 6
- q_previous: float32 [64, 8192], P(None, 'tensor'), may hold values from -6 to 6
Outputs:
- new_feedback: float32 [32, 512, 8192], P('dp', 'tensor')
- new_momentum: float32 [512, 8192], P('tensor')
- q_factor: float32 [64, 8192], P(None, 'tensor')
The draws below stay inside these ranges and needn't reach their ends.
All inputs are finite; a program needn't handle non-finite values.
Results may differ from the reference program's by a relative error of at most 0.0003.
Values sent between devices are 32-bit elements; how exact they have to be, the bound alone decides.
No kernel may reach another device: no remote copies, remote signals or barrier semaphores. Data moves between devices by JAX's collectives and lax.ppermute only.
A program may use at most 64 MiB of HBM per device.

```python
import jax
import jax.numpy as jnp
from jax import lax

D = 8192
RANK = 64
ROWS = 512
REPLICAS = 32


def draw_gradient(key, part):
    key = jax.random.fold_in(key, 11)
    first = jax.random.fold_in(key, 0)
    base = jnp.clip(jax.random.normal(first, (REPLICAS, ROWS, D), jnp.float32), -5.0, 5.0)
    ramp = jnp.arange(REPLICAS, dtype=jnp.float32) / max(REPLICAS - 1, 1)
    rep_scale = (3.0 ** ramp / jnp.sqrt(3.0)).reshape(REPLICAS, 1, 1)
    values = base * rep_scale
    return values.astype(jnp.bfloat16)


def block_levels(key, extent, shards, least, largest):
    gain = 1.0
    for position, parts in shards:
        draws = jax.random.uniform(jax.random.fold_in(jax.random.fold_in(key, 6), position), (parts,), jnp.float32, least / len(shards), largest / len(shards))
        gain = gain * jnp.repeat(jnp.exp(draws), extent[position] // parts).reshape((-1,) + (1,) * (len(extent) - 1 - position))
    return gain


def noise(key, shape, spread, reach, cuts=(), held_as=jnp.bfloat16):
    factor_of = block_levels(key, shape, cuts, -0.22, 0.18) if cuts else 1.0
    entries = jax.random.normal(key, shape, jnp.float32) * spread * factor_of
    return jnp.minimum(jnp.maximum(entries, -reach), reach).astype(held_as)


def setup_inputs(seed: int = 0) -> dict:
    streams_of = jax.random.split(jax.random.key(seed), 5)
    gradient = draw_gradient(jax.random.fold_in(streams_of[4], 71), 0)
    feedback = noise(streams_of[1], (REPLICAS, ROWS, D), 0.5, 4.0, ((0, 32), (1, 16)), jnp.float32)
    momentum = noise(streams_of[2], (ROWS, D), 1.0, 6.0, ((0, 16),), jnp.float32)
    q_previous = noise(streams_of[3], (RANK, D), 1.0, 6.0, ((1, 16),), jnp.float32)
    return {"gradient": gradient, "feedback": feedback, "momentum": momentum, "q_previous": q_previous}


BETA = 0.9
HIGH = lax.Precision.HIGHEST

def reference(gradient, feedback, momentum, q_previous):
    merged = gradient.astype(jnp.float32) + feedback
    summed = jnp.einsum('rfd,kd->fk', merged, q_previous, precision=HIGH)
    gram_matrix = jnp.dot(summed.T, summed, precision=HIGH)
    triangle = jnp.linalg.cholesky(gram_matrix)
    ortho_basis = jax.scipy.linalg.solve_triangular(triangle, summed.T, lower=True).T
    q_factor = jnp.einsum('fk,rfd->kd', ortho_basis, merged, precision=HIGH) / REPLICAS
    approx = jnp.dot(ortho_basis, q_factor, precision=HIGH)
    new_feedback = merged - approx[None]
    new_momentum = BETA * momentum + approx
    return (new_feedback, new_momentum, q_factor)
```

```python
import jax
import jax.numpy as jnp
from jax import lax
from jax.experimental import pallas as pl
from jax.experimental.pallas import tpu as pltpu
from jax.sharding import PartitionSpec as P

BETA = 0.9
HIGH = lax.Precision.HIGHEST

DP = 32
TP = 16
ROWS = 32
RANK = 64
LANES = 128
BLOCK = 16
GROUP = LANES // BLOCK
SHARD = DP * BLOCK


def dot(left, right, left_dim, right_dim):
    return lax.dot_general(
        left,
        right,
        (((left_dim,), (right_dim,)), ((), ())),
        precision=HIGH,
        preferred_element_type=jnp.float32,
    )


def swap_blocks(parts):
    parts = list(parts)
    block = lax.broadcasted_iota(jnp.int32, parts[0].shape, 1) // BLOCK
    for step in (1, 2, 4):
        upper = (block & step) != 0
        for i in range(GROUP):
            if i & step:
                continue
            a, b = parts[i], parts[i | step]
            parts[i] = jnp.where(upper, pltpu.roll(b, step * BLOCK, 1), a)
            parts[i | step] = jnp.where(upper, b, pltpu.roll(a, LANES - step * BLOCK, 1))
    return parts


def gather_blocks(matrix, lane_block):
    block = lax.broadcasted_iota(jnp.int32, (8, LANES), 1) // BLOCK
    moved = pltpu.roll(matrix, (GROUP - lane_block) % GROUP * BLOCK, 1)
    out = jnp.zeros((8, LANES), jnp.float32)
    for kh in range(GROUP):
        piece = moved[kh * 8 : (kh + 1) * 8, :]
        if kh:
            piece = pltpu.roll(piece, kh * BLOCK, 1)
        out = jnp.where(block == kh, piece, out)
    return out


def merge_kernel(gradient, feedback, out):
    for c in range(SHARD // LANES):
        for th in range(TP // GROUP):
            parts = []
            for tl in range(GROUP):
                lanes = pl.ds((th * GROUP + tl) * SHARD + c * LANES, LANES)
                parts.append(gradient[0, :, lanes].astype(jnp.float32) + feedback[0, :, lanes])
            for e, part in enumerate(swap_blocks(parts)):
                out[c * GROUP + e, th * ROWS : (th + 1) * ROWS, :] = part


def pack_q_kernel(d_ref, q_ref, out):
    d = d_ref[0]
    tile = q_ref[:, pl.ds(pl.multiple_of(d // GROUP * LANES, LANES), LANES)]
    packed = gather_blocks(tile, d % GROUP)
    for t in range(TP):
        out[t] = packed


def factor_kernel(merged, q_parts, factor_out, sum_out):
    total = merged[0]
    for r in range(1, DP):
        total = total + merged[r]
    factor = jnp.zeros((ROWS, LANES), jnp.float32)
    for th in range(TP // GROUP):
        q_rows = swap_blocks([q_parts[th * GROUP + tl] for tl in range(GROUP)])
        q_twice = jnp.concatenate(q_rows + q_rows, axis=0)
        factor = factor + dot(total[th * ROWS : (th + 1) * ROWS], q_twice, 1, 1)
    lane = lax.broadcasted_iota(jnp.int32, (ROWS // 2, LANES), 1)
    packed = jnp.where(lane < RANK, factor[: ROWS // 2], factor[ROWS // 2 :])
    for d in range(DP):
        factor_out[d] = packed
    for t in range(TP):
        sum_out[t] = total


def sum_kernel(factors, out):
    total = factors[0]
    for d in range(1, DP):
        total = total + factors[d]
    for t in range(TP):
        out[t] = total


def inverse_triangle(gram, rows_ref):
    row = lax.broadcasted_iota(jnp.int32, (RANK, LANES), 0)
    lane = lax.broadcasted_iota(jnp.int32, (RANK, LANES), 1)
    identity = jnp.where(lane == row + RANK, 1.0, 0.0)
    work = jnp.concatenate([gram, jnp.zeros_like(gram)], axis=1) + identity
    for k in range(RANK):
        pivot_row = work[k : k + 1, :]
        pivot = work[k : k + 1, k : k + 1]
        rows_ref[k : k + 1, :] = pivot_row * lax.rsqrt(pivot)
        if k + 1 < RANK:
            scaled = pivot_row * (1.0 / pivot)
            column = work[:, k : k + 1]
            work = work - jnp.where(row > k, column, 0.0) * scaled
    return rows_ref[:, RANK:]


def solve_kernel(t_ref, factors, sums, out, rows_ref):
    half = ROWS // 2
    flat = factors[...].reshape(TP * half, LANES)
    whole = jnp.concatenate([flat[:, :RANK], flat[:, RANK:]], axis=0)
    gram = dot(whole, whole, 0, 0)
    inverse = inverse_triangle(gram, rows_ref)
    own = factors[t_ref[0]]
    own = jnp.concatenate([own[:, :RANK], own[:, RANK:]], axis=0)
    basis = dot(own, inverse, 1, 1)
    t = t_ref[0]
    approx, q_tiles = [], []
    for th in range(TP // GROUP):
        columns = jnp.concatenate(
            [
                sums[:, th * ROWS + h * half : th * ROWS + (h + 1) * half, :].reshape(TP * half, LANES)
                for h in range(2)
            ],
            axis=0,
        )
        q_tile = dot(inverse, dot(whole, columns, 0, 0), 1, 0) * (1.0 / DP)
        q_tiles.append(q_tile)
        approx.append(dot(basis, q_tile, 1, 0))
    mine = jnp.where(t // GROUP == 0, q_tiles[0], q_tiles[1])
    message = jnp.concatenate(approx + [gather_blocks(mine, t % GROUP)], axis=0)
    for d in range(DP):
        out[d] = message


def finish_kernel(gradient, feedback, momentum, parts_ref, new_feedback, new_momentum, q_out):
    for c in range(SHARD // LANES):
        for th in range(TP // GROUP):
            rows = slice(th * ROWS, (th + 1) * ROWS)
            parts = swap_blocks([parts_ref[c * GROUP + e, rows, :] for e in range(GROUP)])
            for tl, part in enumerate(parts):
                lanes = pl.ds((th * GROUP + tl) * SHARD + c * LANES, LANES)
                merged = gradient[0, :, lanes].astype(jnp.float32) + feedback[0, :, lanes]
                new_feedback[0, :, lanes] = merged - part
                new_momentum[:, lanes] = BETA * momentum[:, lanes] + part
        tail = swap_blocks([parts_ref[c * GROUP + e, 2 * ROWS :, :] for e in range(GROUP)])
        q_out[:, c * LANES : (c + 1) * LANES] = jnp.concatenate(tail, axis=0)


def local(kernel, *shapes, scalars=0, inputs=1, scratch=()):
    return pl.pallas_call(
        kernel,
        out_shape=[jax.ShapeDtypeStruct(shape, jnp.float32) for shape in shapes],
        in_specs=[pl.BlockSpec(memory_space=pltpu.SMEM)] * scalars
        + [pl.BlockSpec(memory_space=pltpu.VMEM)] * inputs,
        out_specs=[pl.BlockSpec(memory_space=pltpu.VMEM)] * len(shapes),
        scratch_shapes=list(scratch),
        compiler_params=pltpu.CompilerParams(vmem_limit_bytes=32 * 1024 * 1024),
    )


def exchange(parts, axis):
    return lax.all_to_all(parts, axis, 0, 0, tiled=True)


def on_device(gradient, feedback, momentum, q_previous):
    d = lax.axis_index("dp").reshape(1)
    t = lax.axis_index("tensor").reshape(1)
    half = ROWS // 2
    (merged,) = local(merge_kernel, (DP, 2 * ROWS, LANES), inputs=2)(gradient, feedback)
    (q_parts,) = local(pack_q_kernel, (TP, 8, LANES), scalars=1)(d, q_previous)
    merged = exchange(merged, "dp")
    q_parts = exchange(q_parts, "tensor")
    factor, summed = local(
        factor_kernel, (DP, half, LANES), (TP, 2 * ROWS, LANES), inputs=2
    )(merged, q_parts)
    factor = exchange(factor, "dp")
    summed = exchange(summed, "tensor")
    (factor,) = local(sum_kernel, (TP, half, LANES))(factor)
    factor = exchange(factor, "tensor")
    (parts,) = local(
        solve_kernel,
        (DP, 2 * ROWS + 8, LANES),
        scalars=1,
        inputs=2,
        scratch=[pltpu.VMEM((RANK, LANES), jnp.float32)],
    )(t, factor, summed)
    parts = exchange(parts, "dp")
    return tuple(
        local(finish_kernel, feedback.shape, momentum.shape, q_previous.shape, inputs=4)(
            gradient, feedback, momentum, parts
        )
    )


def solution(mesh):
    placed = (
        P("dp", "tensor", None),
        P("dp", "tensor", None),
        P("tensor", None),
        P(None, "tensor"),
    )
    return jax.shard_map(
        on_device,
        mesh=mesh,
        in_specs=placed,
        out_specs=(P("dp", "tensor", None), P("tensor", None), P(None, "tensor")),
        check_vma=False,
    )
```

```python
import jax
import jax.numpy as jnp
from jax import lax
from jax.experimental import pallas as pl
from jax.experimental.pallas import tpu as pltpu
from jax.sharding import PartitionSpec as P

BETA = 0.9
HIGH = lax.Precision.HIGHEST

DP = 32
TP = 16
ROWS = 32
RANK = 64
LANES = 128
BLOCK = 16
GROUP = LANES // BLOCK
SHARD = DP * BLOCK
CHIPS = DP // 2
HALF = ROWS // 2


def dot(left, right, left_dim, right_dim):
    return lax.dot_general(
        left,
        right,
        (((left_dim,), (right_dim,)), ((), ())),
        precision=HIGH,
        preferred_element_type=jnp.float32,
    )


def swap_blocks(parts):
    parts = list(parts)
    block = lax.broadcasted_iota(jnp.int32, parts[0].shape, 1) // BLOCK
    for step in (1, 2, 4):
        upper = (block & step) != 0
        for i in range(GROUP):
            if i & step:
                continue
            a, b = parts[i], parts[i | step]
            parts[i] = jnp.where(upper, pltpu.roll(b, step * BLOCK, 1), a)
            parts[i | step] = jnp.where(upper, b, pltpu.roll(a, LANES - step * BLOCK, 1))
    return parts


def gather_blocks(matrix, lane_block):
    block = lax.broadcasted_iota(jnp.int32, (8, LANES), 1) // BLOCK
    moved = pltpu.roll(matrix, (GROUP - lane_block) % GROUP * BLOCK, 1)
    out = jnp.zeros((8, LANES), jnp.float32)
    for kh in range(GROUP):
        piece = moved[kh * 8 : (kh + 1) * 8, :]
        if kh:
            piece = pltpu.roll(piece, kh * BLOCK, 1)
        out = jnp.where(block == kh, piece, out)
    return out


def merge_kernel(core_ref, gradient, feedback, keep, send):
    first = core_ref[0] == 0
    for c in range(SHARD // LANES):
        for th in range(TP // GROUP):
            parts = []
            for tl in range(GROUP):
                lanes = pl.ds((th * GROUP + tl) * SHARD + c * LANES, LANES)
                parts.append(gradient[0, :, lanes].astype(jnp.float32) + feedback[0, :, lanes])
            parts = swap_blocks(parts)
            rows = slice(th * ROWS, (th + 1) * ROWS)
            for pair in range(GROUP // 2):
                chip = c * (GROUP // 2) + pair
                even, odd = parts[2 * pair], parts[2 * pair + 1]
                keep[chip, rows, :] = jnp.where(first, even, odd)
                send[chip, rows, :] = jnp.where(first, odd, even)


def add_kernel(left, right, out):
    out[...] = left[...] + right[...]


def pack_q_kernel(d_ref, q_ref, out):
    d = d_ref[0]
    tile = q_ref[:, pl.ds(pl.multiple_of(d // GROUP * LANES, LANES), LANES)]
    packed = gather_blocks(tile, d % GROUP)
    for t in range(TP):
        out[t] = packed


def unpack_blocks(parts, th):
    return jnp.concatenate(swap_blocks([parts[th * GROUP + tl] for tl in range(GROUP)]), axis=0)


def factor_kernel(merged, q_parts, factor_out, sum_out):
    total = merged[0]
    for chip in range(1, CHIPS):
        total = total + merged[chip]
    sum_out[...] = total
    factor = jnp.zeros((ROWS, LANES), jnp.float32)
    for th in range(TP // GROUP):
        q_tile = unpack_blocks(q_parts, th)
        q_twice = jnp.concatenate([q_tile, q_tile], axis=0)
        factor = factor + dot(total[th * ROWS : (th + 1) * ROWS], q_twice, 1, 1)
    lane = lax.broadcasted_iota(jnp.int32, (HALF, LANES), 1)
    packed = jnp.where(lane < RANK, factor[:HALF], factor[HALF:])
    for d in range(DP):
        factor_out[d] = packed


def unpack_rows(packed):
    return jnp.concatenate([packed[:, :RANK], packed[:, RANK:]], axis=0)


def project_kernel(factors, total, out):
    packed = factors[0]
    for d in range(1, DP):
        packed = packed + factors[d]
    rows = unpack_rows(packed)
    for th in range(TP // GROUP):
        term = dot(rows, total[th * ROWS : (th + 1) * ROWS, :], 0, 0)
        chunks = swap_blocks([term[kh * 8 : (kh + 1) * 8] for kh in range(GROUP)])
        for tl, chunk in enumerate(chunks):
            out[th * GROUP + tl, :HALF, :] = packed
            out[th * GROUP + tl, HALF:, :] = chunk


def chunk_kernel(parts, out):
    total = parts[0, HALF:, :]
    for t in range(1, TP):
        total = total + parts[t, HALF:, :]
    for t in range(TP):
        out[t] = total


def inverse_triangle(gram, rows_ref):
    row = lax.broadcasted_iota(jnp.int32, (RANK, LANES), 0)
    lane = lax.broadcasted_iota(jnp.int32, (RANK, LANES), 1)
    identity = jnp.where(lane == row + RANK, 1.0, 0.0)
    work = jnp.concatenate([gram, jnp.zeros_like(gram)], axis=1) + identity
    for k in range(RANK):
        pivot_row = work[k : k + 1, :]
        pivot = work[k : k + 1, k : k + 1]
        rows_ref[k : k + 1, :] = pivot_row * lax.rsqrt(pivot)
        if k + 1 < RANK:
            scaled = pivot_row * (1.0 / pivot)
            column = work[:, k : k + 1]
            work = work - jnp.where(row > k, column, 0.0) * scaled
    return rows_ref[:, RANK:]


def basis_kernel(t_ref, parts, inverse_out, basis_out, rows_ref):
    flat = parts[:, :HALF, :].reshape(TP * HALF, LANES)
    whole = unpack_rows(flat)
    inverse = inverse_triangle(dot(whole, whole, 0, 0), rows_ref)
    inverse_out[...] = inverse
    own = unpack_rows(parts[t_ref[0], :HALF, :])
    basis_out[...] = dot(own, inverse, 1, 1)


def approx_kernel(t_ref, inverse, basis, w_parts, out):
    t = t_ref[0]
    approx, q_tiles = [], []
    for th in range(TP // GROUP):
        q_tile = dot(inverse[...], unpack_blocks(w_parts, th), 1, 0) * (1.0 / DP)
        q_tiles.append(q_tile)
        approx.append(dot(basis[...], q_tile, 1, 0))
    mine = jnp.where(t // GROUP == 0, q_tiles[0], q_tiles[1])
    message = jnp.concatenate(approx + [gather_blocks(mine, t % GROUP)], axis=0)
    for chip in range(CHIPS):
        out[chip] = message


def finish_kernel(core_ref, gradient, feedback, momentum, own, other, new_feedback, new_momentum, q_out):
    first = core_ref[0] == 0

    def blocks(c, rows):
        parts = []
        for pair in range(GROUP // 2):
            chip = c * (GROUP // 2) + pair
            mine, theirs = own[chip, rows, :], other[chip, rows, :]
            parts += [jnp.where(first, mine, theirs), jnp.where(first, theirs, mine)]
        return swap_blocks(parts)

    for c in range(SHARD // LANES):
        for th in range(TP // GROUP):
            for tl, part in enumerate(blocks(c, slice(th * ROWS, (th + 1) * ROWS))):
                lanes = pl.ds((th * GROUP + tl) * SHARD + c * LANES, LANES)
                merged = gradient[0, :, lanes].astype(jnp.float32) + feedback[0, :, lanes]
                new_feedback[0, :, lanes] = merged - part
                new_momentum[:, lanes] = BETA * momentum[:, lanes] + part
        tail = blocks(c, slice(2 * ROWS, 2 * ROWS + 8))
        q_out[:, c * LANES : (c + 1) * LANES] = jnp.concatenate(tail, axis=0)


def local(kernel, *shapes, scalars=0, inputs=1, scratch=(), flops=100_000, moved=100_000):
    return pl.pallas_call(
        kernel,
        out_shape=[jax.ShapeDtypeStruct(shape, jnp.float32) for shape in shapes],
        in_specs=[pl.BlockSpec(memory_space=pltpu.SMEM)] * scalars
        + [pl.BlockSpec(memory_space=pltpu.VMEM)] * inputs,
        out_specs=[pl.BlockSpec(memory_space=pltpu.VMEM)] * len(shapes),
        scratch_shapes=list(scratch),
        cost_estimate=pl.CostEstimate(flops=flops, bytes_accessed=moved, transcendentals=0),
        compiler_params=pltpu.CompilerParams(vmem_limit_bytes=32 * 1024 * 1024),
    )


def exchange(parts, axis, groups=None):
    return lax.all_to_all(parts, axis, 0, 0, tiled=True, axis_index_groups=groups)


def swap_cores(parts):
    return lax.ppermute(parts, "dp", [(d, d ^ 1) for d in range(DP)])


def on_device(gradient, feedback, momentum, q_previous):
    d = lax.axis_index("dp").reshape(1)
    t = lax.axis_index("tensor").reshape(1)
    core = d % 2
    chips = [list(range(c, DP, 2)) for c in range(2)]
    q_parts = local(pack_q_kernel, (TP, 8, LANES), scalars=1)(d, q_previous)[0]
    q_parts = exchange(q_parts, "tensor")
    whole = (CHIPS, 2 * ROWS, LANES)
    keep, send = local(merge_kernel, whole, whole, scalars=1, inputs=2)(core, gradient, feedback)
    merged = local(add_kernel, whole, inputs=2)(keep, swap_cores(send))[0]
    merged = exchange(merged, "dp", chips)
    factor, total = local(
        factor_kernel, (DP, HALF, LANES), (2 * ROWS, LANES), inputs=2
    )(merged, q_parts)
    factor = exchange(factor, "dp")
    parts = local(project_kernel, (TP, HALF + 8, LANES), inputs=2)(factor, total)[0]
    parts = exchange(parts, "tensor")
    w_parts = local(chunk_kernel, (TP, 8, LANES))(parts)[0]
    w_parts = exchange(w_parts, "tensor")
    inverse, basis = local(
        basis_kernel,
        (RANK, RANK),
        (ROWS, RANK),
        scalars=1,
        scratch=[pltpu.VMEM((RANK, LANES), jnp.float32)],
    )(t, parts)
    own = local(approx_kernel, (CHIPS, 2 * ROWS + 8, LANES), scalars=1, inputs=3)(
        t, inverse, basis, w_parts
    )[0]
    own = exchange(own, "dp", chips)
    other = swap_cores(own)
    return tuple(
        local(
            finish_kernel, feedback.shape, momentum.shape, q_previous.shape, scalars=1, inputs=5
        )(core, gradient, feedback, momentum, own, other)
    )


def solution(mesh):
    placed = (
        P("dp", "tensor", None),
        P("dp", "tensor", None),
        P("tensor", None),
        P(None, "tensor"),
    )
    return jax.shard_map(
        on_device,
        mesh=mesh,
        in_specs=placed,
        out_specs=(P("dp", "tensor", None), P("tensor", None), P(None, "tensor")),
        check_vma=False,
    )
```

```python
import jax
import jax.numpy as jnp
from jax import lax
from jax.experimental import pallas as pl
from jax.experimental.pallas import tpu as pltpu
from jax.sharding import PartitionSpec as P

BETA = 0.9
HIGH = lax.Precision.HIGHEST

DP = 32
TP = 16
ROWS = 32
RANK = 64
LANES = 128
BLOCK = 16
GROUP = LANES // BLOCK
SHARD = DP * BLOCK
CHIPS = DP // 2
HALF = ROWS // 2


def dot(left, right, left_dim, right_dim):
    return lax.dot_general(
        left,
        right,
        (((left_dim,), (right_dim,)), ((), ())),
        precision=HIGH,
        preferred_element_type=jnp.float32,
    )


def swap_blocks(parts):
    parts = list(parts)
    block = lax.broadcasted_iota(jnp.int32, parts[0].shape, 1) // BLOCK
    for step in (1, 2, 4):
        upper = (block & step) != 0
        for i in range(GROUP):
            if i & step:
                continue
            a, b = parts[i], parts[i | step]
            parts[i] = jnp.where(upper, pltpu.roll(b, step * BLOCK, 1), a)
            parts[i | step] = jnp.where(upper, b, pltpu.roll(a, LANES - step * BLOCK, 1))
    return parts


def gather_blocks(matrix, lane_block):
    block = lax.broadcasted_iota(jnp.int32, (8, LANES), 1) // BLOCK
    moved = pltpu.roll(matrix, (GROUP - lane_block) % GROUP * BLOCK, 1)
    out = jnp.zeros((8, LANES), jnp.float32)
    for kh in range(GROUP):
        piece = moved[kh * 8 : (kh + 1) * 8, :]
        if kh:
            piece = pltpu.roll(piece, kh * BLOCK, 1)
        out = jnp.where(block == kh, piece, out)
    return out


def merge_kernel(core_ref, gradient, feedback, keep, send):
    first = core_ref[0] == 0
    for c in range(SHARD // LANES):
        for th in range(TP // GROUP):
            parts = []
            for tl in range(GROUP):
                lanes = pl.ds((th * GROUP + tl) * SHARD + c * LANES, LANES)
                parts.append(gradient[0, :, lanes].astype(jnp.float32) + feedback[0, :, lanes])
            parts = swap_blocks(parts)
            rows = slice(th * ROWS, (th + 1) * ROWS)
            for pair in range(GROUP // 2):
                chip = c * (GROUP // 2) + pair
                even, odd = parts[2 * pair], parts[2 * pair + 1]
                keep[chip, rows, :] = jnp.where(first, even, odd)
                send[chip, rows, :] = jnp.where(first, odd, even)


def copy_kernel(parts, out):
    out[...] = parts[...]


def add_kernel(left, right, q_parts, out):
    out[:, : 2 * ROWS, :] = left[...] + right[...]
    out[:, 2 * ROWS :, :] = q_parts[...]


def pack_q_kernel(core_ref, q_ref, out):
    first = core_ref[0] == 0
    for c in range(SHARD // LANES):
        lanes = slice(c * LANES, (c + 1) * LANES)
        parts = swap_blocks([q_ref[kh * 8 : (kh + 1) * 8, lanes] for kh in range(GROUP)])
        for pair in range(GROUP // 2):
            out[c * (GROUP // 2) + pair] = jnp.where(first, parts[2 * pair], parts[2 * pair + 1])


def unpack_blocks(parts, th):
    return jnp.concatenate(swap_blocks([parts[th * GROUP + tl] for tl in range(GROUP)]), axis=0)


def factor_kernel(t_ref, merged, factor_out, sum_out):
    total = merged[0, : 2 * ROWS, :]
    for chip in range(1, CHIPS):
        total = total + merged[chip, : 2 * ROWS, :]
    sum_out[...] = total
    t = t_ref[0]
    q_parts = [merged[(shard - t + TP) % TP, 2 * ROWS :, :] for shard in range(TP)]
    factor = jnp.zeros((ROWS, LANES), jnp.float32)
    for th in range(TP // GROUP):
        q_tile = unpack_blocks(q_parts, th)
        q_twice = jnp.concatenate([q_tile, q_tile], axis=0)
        factor = factor + dot(total[th * ROWS : (th + 1) * ROWS], q_twice, 1, 1)
    lane = lax.broadcasted_iota(jnp.int32, (HALF, LANES), 1)
    packed = jnp.where(lane < RANK, factor[:HALF], factor[HALF:])
    for d in range(DP):
        factor_out[d] = packed


def unpack_rows(packed):
    return jnp.concatenate([packed[:, :RANK], packed[:, RANK:]], axis=0)


def project_kernel(factors, total, out):
    packed = factors[0]
    for d in range(1, DP):
        packed = packed + factors[d]
    rows = unpack_rows(packed)
    for th in range(TP // GROUP):
        term = dot(rows, total[th * ROWS : (th + 1) * ROWS, :], 0, 0)
        chunks = swap_blocks([term[kh * 8 : (kh + 1) * 8] for kh in range(GROUP)])
        for tl, chunk in enumerate(chunks):
            out[th * GROUP + tl, :HALF, :] = packed
            out[th * GROUP + tl, HALF:, :] = chunk


def chunk_kernel(parts, out):
    total = parts[0, HALF:, :]
    for t in range(1, TP):
        total = total + parts[t, HALF:, :]
    for t in range(TP):
        out[t] = total


def inverse_triangle(gram, rows_ref):
    row = lax.broadcasted_iota(jnp.int32, (RANK, LANES), 0)
    lane = lax.broadcasted_iota(jnp.int32, (RANK, LANES), 1)
    identity = jnp.where(lane == row + RANK, 1.0, 0.0)
    work = jnp.concatenate([gram, jnp.zeros_like(gram)], axis=1) + identity
    for k in range(RANK):
        pivot_row = work[k : k + 1, :]
        pivot = work[k : k + 1, k : k + 1]
        rows_ref[k : k + 1, :] = pivot_row * lax.rsqrt(pivot)
        if k + 1 < RANK:
            scaled = pivot_row * (1.0 / pivot)
            column = work[:, k : k + 1]
            work = work - jnp.where(row > k, column, 0.0) * scaled
    return rows_ref[:, RANK:]


def basis_kernel(t_ref, parts, inverse_out, basis_out, rows_ref):
    flat = parts[:, :HALF, :].reshape(TP * HALF, LANES)
    whole = unpack_rows(flat)
    inverse = inverse_triangle(dot(whole, whole, 0, 0), rows_ref)
    inverse_out[...] = inverse
    own = unpack_rows(parts[t_ref[0], :HALF, :])
    basis_out[...] = dot(own, inverse, 1, 1)


def approx_kernel(t_ref, inverse, basis, w_parts, out):
    t = t_ref[0]
    approx, q_tiles = [], []
    for th in range(TP // GROUP):
        q_tile = dot(inverse[...], unpack_blocks(w_parts, th), 1, 0) * (1.0 / DP)
        q_tiles.append(q_tile)
        approx.append(dot(basis[...], q_tile, 1, 0))
    mine = jnp.where(t // GROUP == 0, q_tiles[0], q_tiles[1])
    message = jnp.concatenate(approx + [gather_blocks(mine, t % GROUP)], axis=0)
    for chip in range(CHIPS):
        out[chip] = message


def finish_kernel(core_ref, gradient, feedback, momentum, own, other, new_feedback, new_momentum, q_out):
    first = core_ref[0] == 0

    def blocks(c, rows):
        parts = []
        for pair in range(GROUP // 2):
            chip = c * (GROUP // 2) + pair
            mine, theirs = own[chip, rows, :], other[chip, rows, :]
            parts += [jnp.where(first, mine, theirs), jnp.where(first, theirs, mine)]
        return swap_blocks(parts)

    for c in range(SHARD // LANES):
        for th in range(TP // GROUP):
            for tl, part in enumerate(blocks(c, slice(th * ROWS, (th + 1) * ROWS))):
                lanes = pl.ds((th * GROUP + tl) * SHARD + c * LANES, LANES)
                merged = gradient[0, :, lanes].astype(jnp.float32) + feedback[0, :, lanes]
                new_feedback[0, :, lanes] = merged - part
                new_momentum[:, lanes] = BETA * momentum[:, lanes] + part
        tail = blocks(c, slice(2 * ROWS, 2 * ROWS + 8))
        q_out[:, c * LANES : (c + 1) * LANES] = jnp.concatenate(tail, axis=0)


def local(kernel, *shapes, scalars=0, inputs=1, scratch=(), flops=100_000, moved=100_000):
    return pl.pallas_call(
        kernel,
        out_shape=[jax.ShapeDtypeStruct(shape, jnp.float32) for shape in shapes],
        in_specs=[pl.BlockSpec(memory_space=pltpu.SMEM)] * scalars
        + [pl.BlockSpec(memory_space=pltpu.VMEM)] * inputs,
        out_specs=[pl.BlockSpec(memory_space=pltpu.VMEM)] * len(shapes),
        scratch_shapes=list(scratch),
        cost_estimate=pl.CostEstimate(flops=flops, bytes_accessed=moved, transcendentals=0),
        compiler_params=pltpu.CompilerParams(vmem_limit_bytes=32 * 1024 * 1024),
    )


def exchange(parts, axis, groups=None):
    return lax.all_to_all(parts, axis, 0, 0, tiled=True, axis_index_groups=groups)


def swap_cores(parts):
    return lax.ppermute(parts, "dp", [(d, d ^ 1) for d in range(DP)])


def fetch_shards(parts):
    pairs = [(d * TP + (t + d // 2) % TP, d * TP + t) for d in range(DP) for t in range(TP)]
    return lax.ppermute(parts, ("dp", "tensor"), pairs)


def on_device(gradient, feedback, momentum, q_previous):
    core = (lax.axis_index("dp") & 1).reshape(1)
    t = lax.axis_index("tensor").reshape(1)
    chips = [list(range(c, DP, 2)) for c in range(2)]
    whole = (CHIPS, 2 * ROWS, LANES)
    q_parts = local(pack_q_kernel, (CHIPS, 8, LANES), scalars=1)(core, q_previous)[0]
    q_parts = fetch_shards(q_parts)
    q_parts = local(copy_kernel, (CHIPS, 8, LANES), flops=10_000_000_000)(q_parts)[0]
    keep, send = local(merge_kernel, whole, whole, scalars=1, inputs=2)(core, gradient, feedback)
    merged = local(add_kernel, (CHIPS, 2 * ROWS + 8, LANES), inputs=3)(
        keep, swap_cores(send), q_parts
    )[0]
    merged = exchange(merged, "dp", chips)
    factor, total = local(factor_kernel, (DP, HALF, LANES), (2 * ROWS, LANES), scalars=1)(t, merged)
    factor = exchange(factor, "dp")
    parts = local(project_kernel, (TP, HALF + 8, LANES), inputs=2)(factor, total)[0]
    parts = exchange(parts, "tensor")
    w_parts = local(chunk_kernel, (TP, 8, LANES))(parts)[0]
    w_parts = exchange(w_parts, "tensor")
    inverse, basis = local(
        basis_kernel,
        (RANK, RANK),
        (ROWS, RANK),
        scalars=1,
        scratch=[pltpu.VMEM((RANK, LANES), jnp.float32)],
    )(t, parts)
    own = local(approx_kernel, (CHIPS, 2 * ROWS + 8, LANES), scalars=1, inputs=3)(
        t, inverse, basis, w_parts
    )[0]
    own = exchange(own, "dp", chips)
    other = swap_cores(own)
    return tuple(
        local(
            finish_kernel, feedback.shape, momentum.shape, q_previous.shape, scalars=1, inputs=5
        )(core, gradient, feedback, momentum, own, other)
    )


def solution(mesh):
    placed = (
        P("dp", "tensor", None),
        P("dp", "tensor", None),
        P("tensor", None),
        P(None, "tensor"),
    )
    return jax.shard_map(
        on_device,
        mesh=mesh,
        in_specs=placed,
        out_specs=(P("dp", "tensor", None), P("tensor", None), P(None, "tensor")),
        check_vma=False,
    )
```

```python
import jax
import jax.numpy as jnp
from jax import lax
from jax.experimental import pallas as pl
from jax.experimental.pallas import tpu as pltpu
from jax.sharding import PartitionSpec as P

BETA = 0.9
HIGH = lax.Precision.HIGHEST

DP = 32
TP = 16
ROWS = 32
RANK = 64
LANES = 128
BLOCK = 16
GROUP = LANES // BLOCK
SHARD = DP * BLOCK
CHIPS = DP // 2
HALF = ROWS // 2


def dot(left, right, left_dim, right_dim):
    return lax.dot_general(
        left,
        right,
        (((left_dim,), (right_dim,)), ((), ())),
        precision=HIGH,
        preferred_element_type=jnp.float32,
    )


def swap_blocks(parts):
    parts = list(parts)
    block = lax.broadcasted_iota(jnp.int32, parts[0].shape, 1) // BLOCK
    for step in (1, 2, 4):
        upper = (block & step) != 0
        for i in range(GROUP):
            if i & step:
                continue
            a, b = parts[i], parts[i | step]
            parts[i] = jnp.where(upper, pltpu.roll(b, step * BLOCK, 1), a)
            parts[i | step] = jnp.where(upper, b, pltpu.roll(a, LANES - step * BLOCK, 1))
    return parts


def gather_blocks(matrix, lane_block):
    block = lax.broadcasted_iota(jnp.int32, (8, LANES), 1) // BLOCK
    moved = pltpu.roll(matrix, (GROUP - lane_block) % GROUP * BLOCK, 1)
    out = jnp.zeros((8, LANES), jnp.float32)
    for kh in range(GROUP):
        piece = moved[kh * 8 : (kh + 1) * 8, :]
        if kh:
            piece = pltpu.roll(piece, kh * BLOCK, 1)
        out = jnp.where(block == kh, piece, out)
    return out


def merge_kernel(core_ref, gradient, feedback, keep, send):
    first = core_ref[0] == 0
    for c in range(SHARD // LANES):
        for th in range(TP // GROUP):
            parts = []
            for tl in range(GROUP):
                lanes = pl.ds((th * GROUP + tl) * SHARD + c * LANES, LANES)
                parts.append(gradient[0, :, lanes].astype(jnp.float32) + feedback[0, :, lanes])
            parts = swap_blocks(parts)
            rows = slice(th * ROWS, (th + 1) * ROWS)
            for pair in range(GROUP // 2):
                chip = c * (GROUP // 2) + pair
                even, odd = parts[2 * pair], parts[2 * pair + 1]
                keep[chip, rows, :] = jnp.where(first, even, odd)
                send[chip, rows, :] = jnp.where(first, odd, even)


def add_kernel(core_ref, t_ref, left, right, out):
    for chip in range(CHIPS):
        out[chip, : 2 * ROWS, :] = left[chip] + right[chip]
    for th in range(TP // GROUP):
        rows = slice(th * ROWS, (th + 1) * ROWS)
        for h in range(2):
            parts = [out[h * GROUP + k // 2 + k % 2 * (GROUP // 2), rows, :] for k in range(GROUP)]
            for tl, part in enumerate(swap_blocks(parts)):
                shard = th * GROUP + tl
                chip = (shard - t_ref[0] + (2 - core_ref[0]) * (TP // 2)) % TP
                out[chip, (2 + h) * ROWS : (3 + h) * ROWS, :] = part


def pack_q_kernel(core_ref, q_ref, out):
    first = core_ref[0] == 0
    even = (lax.broadcasted_iota(jnp.int32, (RANK, LANES), 1) // BLOCK) % 2 == 0
    for h in range(2):
        left = q_ref[:, 2 * h * LANES : (2 * h + 1) * LANES]
        right = q_ref[:, (2 * h + 1) * LANES : (2 * h + 2) * LANES]
        for_first = jnp.where(even, left, pltpu.roll(right, BLOCK, 1))
        for_second = jnp.where(even, pltpu.roll(left, LANES - BLOCK, 1), right)
        out[h] = jnp.where(first, for_first, for_second)


def twice_kernel(q_parts, out):
    out[:, :RANK, :] = q_parts[...]
    out[:, RANK:, :] = q_parts[...]


def unpack_blocks(parts, th):
    return jnp.concatenate(swap_blocks([parts[th * GROUP + tl] for tl in range(GROUP)]), axis=0)


def factor_kernel(merged, q_twice, factor_out, sum_out):
    total = merged[0]
    for chip in range(1, CHIPS):
        total = total + merged[chip]
    sum_out[...] = total[: 2 * ROWS]
    factor = jnp.zeros((ROWS, LANES), jnp.float32)
    for h in range(2):
        factor = factor + dot(total[(2 + h) * ROWS : (3 + h) * ROWS], q_twice[h], 1, 1)
    lane = lax.broadcasted_iota(jnp.int32, (HALF, LANES), 1)
    packed = jnp.where(lane < RANK, factor[:HALF], factor[HALF:])
    for d in range(DP):
        factor_out[d] = packed


def unpack_rows(packed):
    return jnp.concatenate([packed[:, :RANK], packed[:, RANK:]], axis=0)


def project_kernel(factors, total, out):
    packed = factors[0]
    for d in range(1, DP):
        packed = packed + factors[d]
    rows = unpack_rows(packed)
    for th in range(TP // GROUP):
        term = dot(rows, total[th * ROWS : (th + 1) * ROWS, :], 0, 0)
        chunks = swap_blocks([term[kh * 8 : (kh + 1) * 8] for kh in range(GROUP)])
        for tl, chunk in enumerate(chunks):
            out[th * GROUP + tl, :HALF, :] = packed
            out[th * GROUP + tl, HALF:, :] = chunk


def chunk_kernel(parts, out):
    total = parts[0, HALF:, :]
    for t in range(1, TP):
        total = total + parts[t, HALF:, :]
    for t in range(TP):
        out[t] = total


def inverse_triangle(gram, rows_ref):
    row = lax.broadcasted_iota(jnp.int32, (RANK, LANES), 0)
    lane = lax.broadcasted_iota(jnp.int32, (RANK, LANES), 1)
    identity = jnp.where(lane == row + RANK, 1.0, 0.0)
    work = jnp.concatenate([gram, jnp.zeros_like(gram)], axis=1) + identity
    for k in range(RANK):
        pivot_row = work[k : k + 1, :]
        pivot = work[k : k + 1, k : k + 1]
        rows_ref[k : k + 1, :] = pivot_row * lax.rsqrt(pivot)
        if k + 1 < RANK:
            scaled = pivot_row * (1.0 / pivot)
            column = work[:, k : k + 1]
            work = work - jnp.where(row > k, column, 0.0) * scaled
    return rows_ref[:, RANK:]


def basis_kernel(t_ref, parts, inverse_out, basis_out, rows_ref):
    flat = parts[:, :HALF, :].reshape(TP * HALF, LANES)
    whole = unpack_rows(flat)
    inverse = inverse_triangle(dot(whole, whole, 0, 0), rows_ref)
    inverse_out[...] = inverse
    own = unpack_rows(parts[t_ref[0], :HALF, :])
    basis_out[...] = dot(own, inverse, 1, 1)


def approx_kernel(t_ref, inverse, basis, w_parts, out):
    t = t_ref[0]
    approx, q_tiles = [], []
    for th in range(TP // GROUP):
        q_tile = dot(inverse[...], unpack_blocks(w_parts, th), 1, 0) * (1.0 / DP)
        q_tiles.append(q_tile)
        approx.append(dot(basis[...], q_tile, 1, 0))
    mine = jnp.where(t // GROUP == 0, q_tiles[0], q_tiles[1])
    message = jnp.concatenate(approx + [gather_blocks(mine, t % GROUP)], axis=0)
    for chip in range(CHIPS):
        out[chip] = message


def finish_kernel(core_ref, gradient, feedback, momentum, own, other, new_feedback, new_momentum, q_out):
    first = core_ref[0] == 0

    def blocks(c, rows):
        parts = []
        for pair in range(GROUP // 2):
            chip = c * (GROUP // 2) + pair
            mine, theirs = own[chip, rows, :], other[chip, rows, :]
            parts += [jnp.where(first, mine, theirs), jnp.where(first, theirs, mine)]
        return swap_blocks(parts)

    for c in range(SHARD // LANES):
        for th in range(TP // GROUP):
            for tl, part in enumerate(blocks(c, slice(th * ROWS, (th + 1) * ROWS))):
                lanes = pl.ds((th * GROUP + tl) * SHARD + c * LANES, LANES)
                merged = gradient[0, :, lanes].astype(jnp.float32) + feedback[0, :, lanes]
                new_feedback[0, :, lanes] = merged - part
                new_momentum[:, lanes] = BETA * momentum[:, lanes] + part
        tail = blocks(c, slice(2 * ROWS, 2 * ROWS + 8))
        q_out[:, c * LANES : (c + 1) * LANES] = jnp.concatenate(tail, axis=0)


def local(kernel, *shapes, scalars=0, inputs=1, scratch=(), flops=100_000, moved=100_000):
    return pl.pallas_call(
        kernel,
        out_shape=[jax.ShapeDtypeStruct(shape, jnp.float32) for shape in shapes],
        in_specs=[pl.BlockSpec(memory_space=pltpu.SMEM)] * scalars
        + [pl.BlockSpec(memory_space=pltpu.VMEM)] * inputs,
        out_specs=[pl.BlockSpec(memory_space=pltpu.VMEM)] * len(shapes),
        scratch_shapes=list(scratch),
        cost_estimate=pl.CostEstimate(flops=flops, bytes_accessed=moved, transcendentals=0),
        compiler_params=pltpu.CompilerParams(vmem_limit_bytes=32 * 1024 * 1024),
    )


def exchange(parts, axis, groups=None):
    return lax.all_to_all(parts, axis, 0, 0, tiled=True, axis_index_groups=groups)


def swap_cores(parts):
    return lax.ppermute(parts, "dp", [(d, d ^ 1) for d in range(DP)])


def fetch_shards(parts):
    pairs = [
        (d * TP + (t + d // 2 + d % 2 * (TP // 2)) % TP, d * TP + t)
        for d in range(DP)
        for t in range(TP)
    ]
    return lax.ppermute(parts, ("dp", "tensor"), pairs)


def on_device(gradient, feedback, momentum, q_previous):
    core = (lax.axis_index("dp") & 1).reshape(1)
    t = lax.axis_index("tensor").reshape(1)
    chips = [list(range(c, DP, 2)) for c in range(2)]
    whole = (CHIPS, 2 * ROWS, LANES)
    q_parts = local(pack_q_kernel, (2, RANK, LANES), scalars=1)(core, q_previous)[0]
    q_parts = fetch_shards(q_parts)
    q_parts = local(twice_kernel, (2, 2 * RANK, LANES), flops=10_000_000_000)(q_parts)[0]
    keep, send = local(merge_kernel, whole, whole, scalars=1, inputs=2)(core, gradient, feedback)
    merged = local(add_kernel, (CHIPS, 4 * ROWS, LANES), scalars=2, inputs=2)(
        core, t, keep, swap_cores(send)
    )[0]
    merged = exchange(merged, "dp", chips)
    factor, total = local(factor_kernel, (DP, HALF, LANES), (2 * ROWS, LANES), inputs=2)(
        merged, q_parts
    )
    factor = exchange(factor, "dp")
    parts = local(project_kernel, (TP, HALF + 8, LANES), inputs=2)(factor, total)[0]
    parts = exchange(parts, "tensor")
    w_parts = local(chunk_kernel, (TP, 8, LANES))(parts)[0]
    w_parts = exchange(w_parts, "tensor")
    inverse, basis = local(
        basis_kernel,
        (RANK, RANK),
        (ROWS, RANK),
        scalars=1,
        scratch=[pltpu.VMEM((RANK, LANES), jnp.float32)],
    )(t, parts)
    own = local(approx_kernel, (CHIPS, 2 * ROWS + 8, LANES), scalars=1, inputs=3)(
        t, inverse, basis, w_parts
    )[0]
    own = exchange(own, "dp", chips)
    other = swap_cores(own)
    return tuple(
        local(
            finish_kernel, feedback.shape, momentum.shape, q_previous.shape, scalars=1, inputs=5
        )(core, gradient, feedback, momentum, own, other)
    )


def solution(mesh):
    placed = (
        P("dp", "tensor", None),
        P("dp", "tensor", None),
        P("tensor", None),
        P(None, "tensor"),
    )
    return jax.shard_map(
        on_device,
        mesh=mesh,
        in_specs=placed,
        out_specs=(P("dp", "tensor", None), P("tensor", None), P(None, "tensor")),
        check_vma=False,
    )
```

```python
import jax
import jax.numpy as jnp
from jax import lax
from jax.experimental import pallas as pl
from jax.experimental.pallas import tpu as pltpu
from jax.sharding import PartitionSpec as P

BETA = 0.9
HIGH = lax.Precision.HIGHEST

DP = 32
TP = 16
ROWS = 32
RANK = 64
LANES = 128
BLOCK = 16
GROUP = LANES // BLOCK
SPAN = BLOCK * TP
SHARD = DP * BLOCK
CHIPS = DP // 2
HALF = ROWS // 2


def dot(left, right, left_dim, right_dim):
    return lax.dot_general(
        left,
        right,
        (((left_dim,), (right_dim,)), ((), ())),
        precision=HIGH,
        preferred_element_type=jnp.float32,
    )


def swap_blocks(parts):
    parts = list(parts)
    block = lax.broadcasted_iota(jnp.int32, parts[0].shape, 1) // BLOCK
    for step in (1, 2, 4):
        upper = (block & step) != 0
        for i in range(GROUP):
            if i & step:
                continue
            a, b = parts[i], parts[i | step]
            parts[i] = jnp.where(upper, pltpu.roll(b, step * BLOCK, 1), a)
            parts[i | step] = jnp.where(upper, b, pltpu.roll(a, LANES - step * BLOCK, 1))
    return parts


def merge_kernel(core_ref, t_ref, gradient, feedback, keep, send):
    core, t = core_ref[0], t_ref[0]
    for shard in range(TP):
        for out, half in ((keep, core), (send, 1 - core)):
            lanes = pl.ds(pl.multiple_of(shard * SHARD + half * SPAN, SPAN), SPAN)
            chip = (shard - t + (4 - half) * (TP // 2)) % TP
            out[chip] = gradient[0, :, lanes].astype(jnp.float32) + feedback[0, :, lanes]


def add_kernel(left, right, out):
    out[...] = left[...] + right[...]


def half_kernel(core_ref, q_ref, out):
    out[...] = jnp.where(core_ref[0] == 0, q_ref[:, :SPAN], q_ref[:, SPAN:])


def twice_kernel(q_part, out):
    out[:RANK, :] = q_part[...]
    out[RANK:, :] = q_part[...]


def unpack_blocks(parts, th):
    return jnp.concatenate(swap_blocks([parts[th * GROUP + tl] for tl in range(GROUP)]), axis=0)


def factor_kernel(merged, q_twice, factor_out, sum_out):
    total = merged[0]
    for chip in range(1, CHIPS):
        total = total + merged[chip]
    sum_out[...] = total
    factor = dot(total, q_twice[...], 1, 1)
    lane = lax.broadcasted_iota(jnp.int32, (HALF, LANES), 1)
    packed = jnp.where(lane < RANK, factor[:HALF], factor[HALF:])
    for d in range(DP):
        factor_out[d] = packed


def unpack_rows(packed):
    return jnp.concatenate([packed[:, :RANK], packed[:, RANK:]], axis=0)


def project_kernel(factors, total, out):
    packed = factors[0]
    for d in range(1, DP):
        packed = packed + factors[d]
    rows = unpack_rows(packed)
    for th in range(TP // GROUP):
        term = dot(rows, total[:, th * LANES : (th + 1) * LANES], 0, 0)
        chunks = swap_blocks([term[kh * 8 : (kh + 1) * 8] for kh in range(GROUP)])
        for tl, chunk in enumerate(chunks):
            out[th * GROUP + tl, :HALF, :] = packed
            out[th * GROUP + tl, HALF:, :] = chunk


def chunk_kernel(parts, out, chunk_out):
    total = parts[0, HALF:, :]
    for t in range(1, TP):
        total = total + parts[t, HALF:, :]
    chunk_out[...] = total
    for t in range(TP):
        out[t] = total


def inverse_triangle(gram, rows_ref):
    row = lax.broadcasted_iota(jnp.int32, (RANK, LANES), 0)
    lane = lax.broadcasted_iota(jnp.int32, (RANK, LANES), 1)
    identity = jnp.where(lane == row + RANK, 1.0, 0.0)
    work = jnp.concatenate([gram, jnp.zeros_like(gram)], axis=1) + identity
    for k in range(RANK):
        pivot_row = work[k : k + 1, :]
        pivot = work[k : k + 1, k : k + 1]
        rows_ref[k : k + 1, :] = pivot_row * lax.rsqrt(pivot)
        if k + 1 < RANK:
            scaled = pivot_row * (1.0 / pivot)
            column = work[:, k : k + 1]
            work = work - jnp.where(row > k, column, 0.0) * scaled
    return rows_ref[:, RANK:]


def basis_kernel(t_ref, parts, inverse_out, basis_out, rows_ref):
    flat = parts[:, :HALF, :].reshape(TP * HALF, LANES)
    whole = unpack_rows(flat)
    inverse = inverse_triangle(dot(whole, whole, 0, 0), rows_ref)
    inverse_out[...] = inverse
    own = unpack_rows(parts[t_ref[0], :HALF, :])
    basis_out[...] = dot(own, inverse, 1, 1)


def approx_kernel(inverse, basis, w_parts, chunk, out):
    approx = []
    for th in range(TP // GROUP):
        q_tile = dot(inverse[...], unpack_blocks(w_parts, th), 1, 0) * (1.0 / DP)
        approx.append(dot(basis[...], q_tile, 1, 0))
    message = jnp.concatenate(approx + [chunk[...]], axis=0)
    for chip in range(CHIPS):
        out[chip] = message


def finish_kernel(
    core_ref, gradient, feedback, momentum, inverse, own, other, new_feedback, new_momentum, q_out
):
    first = core_ref[0] == 0
    for half in range(2):
        mine = first if half == 0 else jnp.logical_not(first)
        for shard in range(TP):
            for th in range(TP // GROUP):
                rows = slice(th * ROWS, (th + 1) * ROWS)
                part = jnp.where(mine, own[shard, rows, :], other[shard, rows, :])
                start = shard * SHARD + half * SPAN + th * LANES
                lanes = slice(start, start + LANES)
                merged = gradient[0, :, lanes].astype(jnp.float32) + feedback[0, :, lanes]
                new_feedback[0, :, lanes] = merged - part
                new_momentum[:, lanes] = BETA * momentum[:, lanes] + part
        for th in range(TP // GROUP):
            chunks = [
                jnp.where(mine, own[chip, 2 * ROWS :, :], other[chip, 2 * ROWS :, :])
                for chip in range(th * GROUP, (th + 1) * GROUP)
            ]
            w_tile = jnp.concatenate(swap_blocks(chunks), axis=0)
            start = half * SPAN + th * LANES
            q_out[:, start : start + LANES] = dot(inverse[...], w_tile, 1, 0) * (1.0 / DP)


def local(kernel, *shapes, scalars=0, inputs=1, scratch=(), flops=100_000, moved=100_000):
    return pl.pallas_call(
        kernel,
        out_shape=[jax.ShapeDtypeStruct(shape, jnp.float32) for shape in shapes],
        in_specs=[pl.BlockSpec(memory_space=pltpu.SMEM)] * scalars
        + [pl.BlockSpec(memory_space=pltpu.VMEM)] * inputs,
        out_specs=[pl.BlockSpec(memory_space=pltpu.VMEM)] * len(shapes),
        scratch_shapes=list(scratch),
        cost_estimate=pl.CostEstimate(flops=flops, bytes_accessed=moved, transcendentals=0),
        compiler_params=pltpu.CompilerParams(vmem_limit_bytes=32 * 1024 * 1024),
    )


def exchange(parts, axis, groups=None):
    return lax.all_to_all(parts, axis, 0, 0, tiled=True, axis_index_groups=groups)


def swap_cores(parts):
    return lax.ppermute(parts, "dp", [(d, d ^ 1) for d in range(DP)])


def permute(parts, target):
    pairs = []
    for d in range(DP):
        for t in range(TP):
            chip, plane = target(d // 2, d % 2, t)
            pairs.append((d * TP + t, (chip * 2 + d % 2) * TP + plane))
    return lax.ppermute(parts, ("dp", "tensor"), pairs)


def on_device(gradient, feedback, momentum, q_previous):
    core = (lax.axis_index("dp") & 1).reshape(1)
    t = lax.axis_index("tensor").reshape(1)
    chips = [list(range(c, DP, 2)) for c in range(2)]
    q_part = local(half_kernel, (RANK, SPAN), scalars=1)(core, q_previous)[0]
    q_part = permute(q_part, lambda chip, c, plane: (chip, (plane - chip - c * (TP // 2)) % TP))
    q_part = local(twice_kernel, (2 * RANK, SPAN), flops=10_000_000_000)(q_part)[0]
    whole = (CHIPS, ROWS, SPAN)
    keep, send = local(merge_kernel, whole, whole, scalars=2, inputs=2)(
        core, t, gradient, feedback
    )
    merged = local(add_kernel, whole, inputs=2)(keep, swap_cores(send))[0]
    merged = exchange(merged, "dp", chips)
    factor, total = local(factor_kernel, (DP, HALF, LANES), (ROWS, SPAN), inputs=2)(merged, q_part)
    total = permute(total, lambda chip, c, plane: ((plane + chip + c * (TP // 2)) % TP, plane))
    factor = exchange(factor, "dp")
    parts = local(project_kernel, (TP, HALF + 8, LANES), inputs=2)(factor, total)[0]
    parts = exchange(parts, "tensor")
    w_parts, chunk = local(chunk_kernel, (TP, 8, LANES), (8, LANES))(parts)
    w_parts = exchange(w_parts, "tensor")
    chunk = permute(chunk, lambda chip, c, plane: (plane, chip))
    inverse, basis = local(
        basis_kernel,
        (RANK, RANK),
        (ROWS, RANK),
        scalars=1,
        scratch=[pltpu.VMEM((RANK, LANES), jnp.float32)],
    )(t, parts)
    own = local(approx_kernel, (CHIPS, 2 * ROWS + 8, LANES), inputs=4)(
        inverse, basis, w_parts, chunk
    )[0]
    own = exchange(own, "dp", chips)
    other = swap_cores(own)
    return tuple(
        local(
            finish_kernel, feedback.shape, momentum.shape, q_previous.shape, scalars=1, inputs=6
        )(core, gradient, feedback, momentum, inverse, own, other)
    )


def solution(mesh):
    placed = (
        P("dp", "tensor", None),
        P("dp", "tensor", None),
        P("tensor", None),
        P(None, "tensor"),
    )
    return jax.shard_map(
        on_device,
        mesh=mesh,
        in_specs=placed,
        out_specs=(P("dp", "tensor", None), P("tensor", None), P(None, "tensor")),
        check_vma=False,
    )
```

```python
import jax
import jax.numpy as jnp
from jax import lax
from jax.experimental import pallas as pl
from jax.experimental.pallas import tpu as pltpu
from jax.sharding import PartitionSpec as P

BETA = 0.9
HIGH = lax.Precision.HIGHEST

DP = 32
TP = 16
ROWS = 32
RANK = 64
LANES = 128
BLOCK = 16
GROUP = LANES // BLOCK
SPAN = BLOCK * TP
SHARD = DP * BLOCK
CHIPS = DP // 2
HALF = ROWS // 2


def dot(left, right, left_dim, right_dim):
    return lax.dot_general(
        left,
        right,
        (((left_dim,), (right_dim,)), ((), ())),
        precision=HIGH,
        preferred_element_type=jnp.float32,
    )


def swap_blocks(parts):
    parts = list(parts)
    block = lax.broadcasted_iota(jnp.int32, parts[0].shape, 1) // BLOCK
    for step in (1, 2, 4):
        upper = (block & step) != 0
        for i in range(GROUP):
            if i & step:
                continue
            a, b = parts[i], parts[i | step]
            parts[i] = jnp.where(upper, pltpu.roll(b, step * BLOCK, 1), a)
            parts[i | step] = jnp.where(upper, b, pltpu.roll(a, LANES - step * BLOCK, 1))
    return parts


def merge_kernel(core_ref, t_ref, gradient, feedback, keep, send):
    core, t = core_ref[0], t_ref[0]
    for shard in range(TP):
        for out, half in ((keep, core), (send, 1 - core)):
            lanes = pl.ds(pl.multiple_of(shard * SHARD + half * SPAN, SPAN), SPAN)
            chip = (shard - t + (4 - half) * (TP // 2)) % TP
            out[chip] = gradient[0, :, lanes].astype(jnp.float32) + feedback[0, :, lanes]


def add_kernel(left, right, out):
    out[...] = left[...] + right[...]


def half_kernel(core_ref, q_ref, out):
    out[...] = jnp.where(core_ref[0] == 0, q_ref[:, :SPAN], q_ref[:, SPAN:])


def twice_kernel(q_part, out):
    out[:RANK, :] = q_part[...]
    out[RANK:, :] = q_part[...]


def unpack_blocks(parts, th):
    return jnp.concatenate(swap_blocks([parts[th * GROUP + tl] for tl in range(GROUP)]), axis=0)


def factor_kernel(merged, q_twice, out):
    total = merged[0]
    for chip in range(1, CHIPS):
        total = total + merged[chip]
    factor = dot(total, q_twice[...], 1, 1)
    lane = lax.broadcasted_iota(jnp.int32, (HALF, LANES), 1)
    packed = jnp.where(lane < RANK, factor[:HALF], factor[HALF:])
    pieces = swap_blocks(
        [
            total[g * 8 : (g + 1) * 8, h * LANES : (h + 1) * LANES]
            for h in range(2)
            for g in range(ROWS // 8)
        ]
    )
    for d in range(DP):
        out[d, :HALF, :] = packed
        out[d, HALF:, :] = pieces[d // 2 % GROUP]


def unpack_rows(packed):
    return jnp.concatenate([packed[:, :RANK], packed[:, RANK:]], axis=0)


def project_kernel(core_ref, chip_ref, t_ref, parts, out):
    packed = parts[0, :HALF, :]
    for d in range(1, DP):
        packed = packed + parts[d, :HALF, :]
    rows = unpack_rows(packed)
    low = chip_ref[0] < GROUP
    for th in range(TP // GROUP):
        pieces = []
        for tl in range(GROUP):
            source = (th * GROUP + tl - t_ref[0] + (4 - core_ref[0]) * (TP // 2)) % TP
            pieces.append(parts[source * 2 + core_ref[0], HALF:, :])
        pieces = swap_blocks(pieces)
        total = jnp.concatenate(
            [jnp.where(low, pieces[g], pieces[g + ROWS // 8]) for g in range(ROWS // 8)], axis=0
        )
        term = dot(rows, total, 0, 0)
        chunks = swap_blocks([term[kh * 8 : (kh + 1) * 8] for kh in range(GROUP)])
        for tl, chunk in enumerate(chunks):
            out[th * GROUP + tl, :HALF, :] = packed
            out[th * GROUP + tl, HALF:, :] = chunk


def chunk_kernel(parts, out, chunk_out):
    total = parts[0, HALF:, :]
    for t in range(1, TP):
        total = total + parts[t, HALF:, :]
    chunk_out[...] = total
    for t in range(TP):
        out[t] = total


def inverse_triangle(gram, rows_ref):
    row = lax.broadcasted_iota(jnp.int32, (RANK, LANES), 0)
    lane = lax.broadcasted_iota(jnp.int32, (RANK, LANES), 1)
    identity = jnp.where(lane == row + RANK, 1.0, 0.0)
    work = jnp.concatenate([gram, jnp.zeros_like(gram)], axis=1) + identity
    for k in range(RANK):
        pivot_row = work[k : k + 1, :]
        pivot = work[k : k + 1, k : k + 1]
        rows_ref[k : k + 1, :] = pivot_row * lax.rsqrt(pivot)
        if k + 1 < RANK:
            scaled = pivot_row * (1.0 / pivot)
            column = work[:, k : k + 1]
            work = work - jnp.where(row > k, column, 0.0) * scaled
    return rows_ref[:, RANK:]


def basis_kernel(t_ref, parts, inverse_out, basis_out, rows_ref):
    flat = parts[:, :HALF, :].reshape(TP * HALF, LANES)
    whole = unpack_rows(flat)
    inverse = inverse_triangle(dot(whole, whole, 0, 0), rows_ref)
    inverse_out[...] = inverse
    own = unpack_rows(parts[t_ref[0], :HALF, :])
    basis_out[...] = dot(own, inverse, 1, 1)


def approx_kernel(inverse, basis, w_parts, chunk, out):
    approx = []
    for th in range(TP // GROUP):
        q_tile = dot(inverse[...], unpack_blocks(w_parts, th), 1, 0) * (1.0 / DP)
        approx.append(dot(basis[...], q_tile, 1, 0))
    message = jnp.concatenate(approx + [chunk[...]], axis=0)
    for chip in range(CHIPS):
        out[chip] = message


def finish_kernel(
    core_ref, gradient, feedback, momentum, inverse, own, other, new_feedback, new_momentum, q_out
):
    first = core_ref[0] == 0
    for half in range(2):
        mine = first if half == 0 else jnp.logical_not(first)
        for th in range(TP // GROUP):
            rows = slice(th * ROWS, (th + 1) * ROWS)
            for group in range(CHIPS // GROUP):
                parts = [
                    jnp.where(mine, own[chip, rows, :], other[chip, rows, :])
                    for chip in range(group * GROUP, (group + 1) * GROUP)
                ]
                for tl, part in enumerate(swap_blocks(parts)):
                    start = (th * GROUP + tl) * SHARD + half * SPAN + group * LANES
                    lanes = slice(start, start + LANES)
                    merged = gradient[0, :, lanes].astype(jnp.float32) + feedback[0, :, lanes]
                    new_feedback[0, :, lanes] = merged - part
                    new_momentum[:, lanes] = BETA * momentum[:, lanes] + part
        for th in range(TP // GROUP):
            chunks = [
                jnp.where(mine, own[chip, 2 * ROWS :, :], other[chip, 2 * ROWS :, :])
                for chip in range(th * GROUP, (th + 1) * GROUP)
            ]
            w_tile = jnp.concatenate(swap_blocks(chunks), axis=0)
            start = half * SPAN + th * LANES
            q_out[:, start : start + LANES] = dot(inverse[...], w_tile, 1, 0) * (1.0 / DP)


def local(kernel, *shapes, scalars=0, inputs=1, scratch=(), flops=100_000, moved=100_000):
    return pl.pallas_call(
        kernel,
        out_shape=[jax.ShapeDtypeStruct(shape, jnp.float32) for shape in shapes],
        in_specs=[pl.BlockSpec(memory_space=pltpu.SMEM)] * scalars
        + [pl.BlockSpec(memory_space=pltpu.VMEM)] * inputs,
        out_specs=[pl.BlockSpec(memory_space=pltpu.VMEM)] * len(shapes),
        scratch_shapes=list(scratch),
        cost_estimate=pl.CostEstimate(flops=flops, bytes_accessed=moved, transcendentals=0),
        compiler_params=pltpu.CompilerParams(vmem_limit_bytes=32 * 1024 * 1024),
    )


def exchange(parts, axis, groups=None):
    return lax.all_to_all(parts, axis, 0, 0, tiled=True, axis_index_groups=groups)


def swap_cores(parts):
    return lax.ppermute(parts, "dp", [(d, d ^ 1) for d in range(DP)])


def permute(parts, target):
    pairs = []
    for d in range(DP):
        for t in range(TP):
            chip, plane = target(d // 2, d % 2, t)
            pairs.append((d * TP + t, (chip * 2 + d % 2) * TP + plane))
    return lax.ppermute(parts, ("dp", "tensor"), pairs)


def on_device(gradient, feedback, momentum, q_previous):
    d = lax.axis_index("dp").reshape(1)
    core, chip = d & 1, d >> 1
    t = lax.axis_index("tensor").reshape(1)
    chips = [list(range(c, DP, 2)) for c in range(2)]
    q_part = local(half_kernel, (RANK, SPAN), scalars=1)(core, q_previous)[0]
    q_part = permute(q_part, lambda chip, c, plane: (chip, (plane - chip - c * (TP // 2)) % TP))
    q_part = local(twice_kernel, (2 * RANK, SPAN))(q_part)[0]
    whole = (CHIPS, ROWS, SPAN)
    keep, send = local(merge_kernel, whole, whole, scalars=2, inputs=2)(
        core, t, gradient, feedback
    )
    merged = local(add_kernel, whole, inputs=2)(keep, swap_cores(send))[0]
    merged = exchange(merged, "dp", chips)
    factor = local(factor_kernel, (DP, HALF + 8, LANES), inputs=2)(merged, q_part)[0]
    factor = exchange(factor, "dp")
    parts = local(project_kernel, (TP, HALF + 8, LANES), scalars=3)(core, chip, t, factor)[0]
    parts = exchange(parts, "tensor")
    w_parts, chunk = local(chunk_kernel, (TP, 8, LANES), (8, LANES))(parts)
    w_parts = exchange(w_parts, "tensor")
    inverse, basis = local(
        basis_kernel,
        (RANK, RANK),
        (ROWS, RANK),
        scalars=1,
        scratch=[pltpu.VMEM((RANK, LANES), jnp.float32)],
    )(t, parts)
    own = local(approx_kernel, (CHIPS, 2 * ROWS + 8, LANES), inputs=4)(
        inverse, basis, w_parts, chunk
    )[0]
    own = exchange(own, "dp", chips)
    other = swap_cores(own)
    return tuple(
        local(
            finish_kernel, feedback.shape, momentum.shape, q_previous.shape, scalars=1, inputs=6
        )(core, gradient, feedback, momentum, inverse, own, other)
    )


def solution(mesh):
    placed = (
        P("dp", "tensor", None),
        P("dp", "tensor", None),
        P("tensor", None),
        P(None, "tensor"),
    )
    return jax.shard_map(
        on_device,
        mesh=mesh,
        in_specs=placed,
        out_specs=(P("dp", "tensor", None), P("tensor", None), P(None, "tensor")),
        check_vma=False,
    )
```

```python
import functools

import jax
import jax.numpy as jnp
from jax import lax
from jax.experimental import pallas as pl
from jax.experimental.pallas import tpu as pltpu
from jax.sharding import PartitionSpec as P

BETA = 0.9
HIGH = lax.Precision.HIGHEST

DP = 32
TP = 16
ROWS = 32
RANK = 64
LANES = 128
BLOCK = 16
GROUP = LANES // BLOCK
SPAN = BLOCK * TP
SHARD = DP * BLOCK
CHIPS = DP // 2
HALF = ROWS // 2


def dot(left, right, left_dim, right_dim):
    return lax.dot_general(
        left,
        right,
        (((left_dim,), (right_dim,)), ((), ())),
        precision=HIGH,
        preferred_element_type=jnp.float32,
    )


def swap_blocks(parts):
    parts = list(parts)
    block = lax.broadcasted_iota(jnp.int32, parts[0].shape, 1) // BLOCK
    for step in (1, 2, 4):
        upper = (block & step) != 0
        for i in range(GROUP):
            if i & step:
                continue
            a, b = parts[i], parts[i | step]
            parts[i] = jnp.where(upper, pltpu.roll(b, step * BLOCK, 1), a)
            parts[i | step] = jnp.where(upper, b, pltpu.roll(a, LANES - step * BLOCK, 1))
    return parts


def columns(shard, half):
    return pl.ds(pl.multiple_of(shard * SHARD + half * SPAN, SPAN), SPAN)


def merge_kernel(half_ref, t_ref, gradient, feedback, out, gradient_part, feedback_part, sems):
    half, t = half_ref[0], t_ref[0]
    copies = []
    for shard in range(TP):
        lanes = columns(shard, half)
        copies.append(
            [
                pltpu.make_async_copy(source.at[0, :, lanes], target.at[shard], sems.at[i, shard])
                for i, (source, target) in enumerate(
                    ((gradient, gradient_part), (feedback, feedback_part))
                )
            ]
        )
    for pair in copies:
        for copy in pair:
            copy.start()
    for shard in range(TP):
        for copy in copies[shard]:
            copy.wait()
        chip = (shard - t + (4 - half) * (TP // 2)) % TP
        out[chip] = gradient_part[shard].astype(jnp.float32) + feedback_part[shard]


def add_kernel(left, right, out, left_part, sems):
    copies = [
        pltpu.make_async_copy(left.at[chip], left_part.at[chip], sems.at[0, chip])
        for chip in range(CHIPS)
    ]
    for copy in copies:
        copy.start()
    results = []
    for chip in range(CHIPS):
        copies[chip].wait()
        left_part[chip] = left_part[chip] + right[chip]
        results.append(pltpu.make_async_copy(left_part.at[chip], out.at[chip], sems.at[1, chip]))
        results[chip].start()
    for copy in results:
        copy.wait()


def half_kernel(core_ref, q_ref, out):
    out[...] = jnp.where(core_ref[0] == 0, q_ref[:, :SPAN], q_ref[:, SPAN:])


def twice_kernel(q_part, out):
    out[:RANK, :] = q_part[...]
    out[RANK:, :] = q_part[...]


def unpack_blocks(parts, th):
    return jnp.concatenate(swap_blocks([parts[th * GROUP + tl] for tl in range(GROUP)]), axis=0)


def factor_kernel(merged, q_twice, out):
    total = merged[0]
    for chip in range(1, CHIPS):
        total = total + merged[chip]
    factor = dot(total, q_twice[...], 1, 1)
    lane = lax.broadcasted_iota(jnp.int32, (HALF, LANES), 1)
    packed = jnp.where(lane < RANK, factor[:HALF], factor[HALF:])
    pieces = swap_blocks(
        [
            total[g * 8 : (g + 1) * 8, h * LANES : (h + 1) * LANES]
            for h in range(2)
            for g in range(ROWS // 8)
        ]
    )
    for d in range(DP):
        out[d, :HALF, :] = packed
        out[d, HALF:, :] = pieces[d // 2 % GROUP]


def unpack_rows(packed):
    return jnp.concatenate([packed[:, :RANK], packed[:, RANK:]], axis=0)


def project_kernel(core_ref, chip_ref, t_ref, parts, out):
    packed = parts[0, :HALF, :]
    for d in range(1, DP):
        packed = packed + parts[d, :HALF, :]
    rows = unpack_rows(packed)
    low = chip_ref[0] < GROUP
    for th in range(TP // GROUP):
        pieces = []
        for tl in range(GROUP):
            source = (th * GROUP + tl - t_ref[0] + (4 - core_ref[0]) * (TP // 2)) % TP
            pieces.append(parts[source * 2 + core_ref[0], HALF:, :])
        pieces = swap_blocks(pieces)
        total = jnp.concatenate(
            [jnp.where(low, pieces[g], pieces[g + ROWS // 8]) for g in range(ROWS // 8)], axis=0
        )
        term = dot(rows, total, 0, 0)
        chunks = swap_blocks([term[kh * 8 : (kh + 1) * 8] for kh in range(GROUP)])
        for tl, chunk in enumerate(chunks):
            out[th * GROUP + tl, :HALF, :] = packed
            out[th * GROUP + tl, HALF:, :] = chunk


def chunk_kernel(parts, out, chunk_out):
    total = parts[0, HALF:, :]
    for t in range(1, TP):
        total = total + parts[t, HALF:, :]
    chunk_out[...] = total
    for t in range(TP):
        out[t] = total


def inverse_triangle(gram, rows_ref):
    row = lax.broadcasted_iota(jnp.int32, (RANK, LANES), 0)
    lane = lax.broadcasted_iota(jnp.int32, (RANK, LANES), 1)
    identity = jnp.where(lane == row + RANK, 1.0, 0.0)
    work = jnp.concatenate([gram, jnp.zeros_like(gram)], axis=1) + identity
    for k in range(RANK):
        pivot_row = work[k : k + 1, :]
        pivot = work[k : k + 1, k : k + 1]
        rows_ref[k : k + 1, :] = pivot_row * lax.rsqrt(pivot)
        if k + 1 < RANK:
            scaled = pivot_row * (1.0 / pivot)
            column = work[:, k : k + 1]
            work = work - jnp.where(row > k, column, 0.0) * scaled
    return rows_ref[:, RANK:]


def basis_kernel(t_ref, parts, inverse_out, basis_out, rows_ref):
    flat = parts[:, :HALF, :].reshape(TP * HALF, LANES)
    whole = unpack_rows(flat)
    inverse = inverse_triangle(dot(whole, whole, 0, 0), rows_ref)
    inverse_out[...] = inverse
    own = unpack_rows(parts[t_ref[0], :HALF, :])
    basis_out[...] = dot(own, inverse, 1, 1)


def approx_kernel(inverse, basis, w_parts, chunk, out):
    approx = []
    for th in range(TP // GROUP):
        q_tile = dot(inverse[...], unpack_blocks(w_parts, th), 1, 0) * (1.0 / DP)
        approx.append(dot(basis[...], q_tile, 1, 0))
    message = jnp.concatenate(approx + [chunk[...]], axis=0)
    for chip in range(CHIPS):
        out[chip] = message


def finish_half(half_ref, gradient, feedback, momentum, inverse, parts, outs, scratch, sems):
    half = half_ref[0]
    new_feedback, new_momentum, q_out = outs
    feedback_part, momentum_part, q_part = scratch
    copies = []
    for th in range(TP // GROUP):
        rows = slice(th * ROWS, (th + 1) * ROWS)
        for group in range(CHIPS // GROUP):
            chips = range(group * GROUP, (group + 1) * GROUP)
            place = slice(group * LANES, (group + 1) * LANES)
            for tl, part in enumerate(swap_blocks([parts[chip, rows, :] for chip in chips])):
                shard = th * GROUP + tl
                start = shard * SHARD + half * SPAN + group * LANES
                lanes = pl.ds(pl.multiple_of(start, LANES), LANES)
                merged = gradient[0, :, lanes].astype(jnp.float32) + feedback[0, :, lanes]
                feedback_part[shard, :, place] = merged - part
                momentum_part[shard, :, place] = BETA * momentum[:, lanes] + part
        for shard in range(th * GROUP, (th + 1) * GROUP):
            lanes = columns(shard, half)
            copies += [
                pltpu.make_async_copy(
                    feedback_part.at[shard], new_feedback.at[0, :, lanes], sems.at[0, shard]
                ),
                pltpu.make_async_copy(
                    momentum_part.at[shard], new_momentum.at[:, lanes], sems.at[1, shard]
                ),
            ]
            copies[-2].start()
            copies[-1].start()
    for group in range(CHIPS // GROUP):
        chips = range(group * GROUP, (group + 1) * GROUP)
        w_tile = jnp.concatenate(swap_blocks([parts[chip, 2 * ROWS :, :] for chip in chips]), axis=0)
        place = slice(group * LANES, (group + 1) * LANES)
        q_part[:, place] = dot(inverse[...], w_tile, 1, 0) * (1.0 / DP)
    copies.append(pltpu.make_async_copy(q_part, q_out.at[:, columns(0, half)], sems.at[2, 0]))
    copies[-1].start()
    for copy in copies:
        copy.wait()


def finish_own_kernel(half_ref, gradient, feedback, momentum, inverse, parts, *refs):
    finish_half(half_ref, gradient, feedback, momentum, inverse, parts, refs[:3], refs[3:6], refs[6])


def finish_other_kernel(half_ref, gradient, feedback, momentum, inverse, parts, *refs):
    finish_half(half_ref, gradient, feedback, momentum, inverse, parts, refs[3:6], refs[6:9], refs[9])


def local(kernel, *shapes, scalars=0, inputs=1, scratch=(), flops=100_000, far=(), far_out=False, alias=None, room=32):
    vmem, anywhere = pl.BlockSpec(memory_space=pltpu.VMEM), pl.BlockSpec(memory_space=pltpu.HBM)
    return pl.pallas_call(
        kernel,
        out_shape=[jax.ShapeDtypeStruct(shape, jnp.float32) for shape in shapes],
        in_specs=[pl.BlockSpec(memory_space=pltpu.SMEM)] * scalars
        + [anywhere if i in far else vmem for i in range(inputs)],
        out_specs=[anywhere if far_out else vmem] * len(shapes),
        scratch_shapes=list(scratch),
        input_output_aliases=alias or {},
        cost_estimate=pl.CostEstimate(flops=flops, bytes_accessed=100_000, transcendentals=0),
        compiler_params=pltpu.CompilerParams(vmem_limit_bytes=room * 1024 * 1024),
    )


def exchange(parts, axis, groups=None):
    return lax.all_to_all(parts, axis, 0, 0, tiled=True, axis_index_groups=groups)


def swap_cores(parts):
    return lax.ppermute(parts, "dp", [(d, d ^ 1) for d in range(DP)])


def permute(parts, target):
    pairs = []
    for d in range(DP):
        for t in range(TP):
            chip, plane = target(d // 2, d % 2, t)
            pairs.append((d * TP + t, (chip * 2 + d % 2) * TP + plane))
    return lax.ppermute(parts, ("dp", "tensor"), pairs)


def on_device(gradient, feedback, momentum, q_previous):
    d = lax.axis_index("dp").reshape(1)
    core, chip = d & 1, d >> 1
    t = lax.axis_index("tensor").reshape(1)
    chips = [list(range(c, DP, 2)) for c in range(2)]
    q_part = local(half_kernel, (RANK, SPAN), scalars=1)(core, q_previous)[0]
    q_part = permute(q_part, lambda chip, c, plane: (chip, (plane - chip - c * (TP // 2)) % TP))
    q_part = local(twice_kernel, (2 * RANK, SPAN), flops=10_000_000_000)(q_part)[0]
    whole = (CHIPS, ROWS, SPAN)
    merge = functools.partial(
        local,
        merge_kernel,
        whole,
        scalars=2,
        inputs=2,
        far=(0, 1),
        scratch=[
            pltpu.VMEM((TP, ROWS, SPAN), jnp.bfloat16),
            pltpu.VMEM((TP, ROWS, SPAN), jnp.float32),
            pltpu.SemaphoreType.DMA((2, TP)),
        ],
    )
    send = merge(room=60)(1 - core, t, gradient, feedback)[0]
    keep = merge(room=32)(core, t, gradient, feedback)[0]
    merged = local(
        add_kernel,
        whole,
        inputs=2,
        far=(0,),
        far_out=True,
        room=32,
        scratch=[pltpu.VMEM(whole, jnp.float32), pltpu.SemaphoreType.DMA((2, CHIPS))],
    )(keep, swap_cores(send))[0]
    merged = exchange(merged, "dp", chips)
    factor = local(factor_kernel, (DP, HALF + 8, LANES), inputs=2)(merged, q_part)[0]
    factor = exchange(factor, "dp")
    parts = local(project_kernel, (TP, HALF + 8, LANES), scalars=3)(core, chip, t, factor)[0]
    parts = exchange(parts, "tensor")
    w_parts, chunk = local(chunk_kernel, (TP, 8, LANES), (8, LANES))(parts)
    w_parts = exchange(w_parts, "tensor")
    inverse, basis = local(
        basis_kernel,
        (RANK, RANK),
        (ROWS, RANK),
        scalars=1,
        scratch=[pltpu.VMEM((RANK, LANES), jnp.float32)],
    )(t, parts)
    own = local(approx_kernel, (CHIPS, 2 * ROWS + 8, LANES), inputs=4)(
        inverse, basis, w_parts, chunk
    )[0]
    own = exchange(own, "dp", chips)
    other = swap_cores(own)
    shapes = (feedback.shape, momentum.shape, q_previous.shape)
    scratch = [
        pltpu.VMEM((TP, ROWS, SPAN), jnp.float32),
        pltpu.VMEM((TP, ROWS, SPAN), jnp.float32),
        pltpu.VMEM((RANK, SPAN), jnp.float32),
        pltpu.SemaphoreType.DMA((3, TP)),
    ]
    outs = local(
        finish_own_kernel, *shapes, scalars=1, inputs=5, scratch=scratch, far_out=True
    )(core, gradient, feedback, momentum, inverse, own)
    outs = local(
        finish_other_kernel,
        *shapes,
        scalars=1,
        inputs=8,
        scratch=scratch,
        far=(5, 6, 7),
        far_out=True,
        alias={6: 0, 7: 1, 8: 2},
    )(1 - core, gradient, feedback, momentum, inverse, other, *outs)
    return tuple(outs)


def solution(mesh):
    placed = (
        P("dp", "tensor", None),
        P("dp", "tensor", None),
        P("tensor", None),
        P(None, "tensor"),
    )
    return jax.shard_map(
        on_device,
        mesh=mesh,
        in_specs=placed,
        out_specs=(P("dp", "tensor", None), P("tensor", None), P(None, "tensor")),
        check_vma=False,
    )
```

```python
import functools

import jax
import jax.numpy as jnp
from jax import lax
from jax.experimental import pallas as pl
from jax.experimental.pallas import tpu as pltpu
from jax.sharding import PartitionSpec as P

BETA = 0.9
HIGH = lax.Precision.HIGHEST

DP = 32
TP = 16
ROWS = 32
RANK = 64
LANES = 128
BLOCK = 16
GROUP = LANES // BLOCK
SPAN = BLOCK * TP
CHUNKS = 4
SHARD = DP * BLOCK
CHIPS = DP // 2
HALF = ROWS // 2


def dot(left, right, left_dim, right_dim):
    return lax.dot_general(
        left,
        right,
        (((left_dim,), (right_dim,)), ((), ())),
        precision=HIGH,
        preferred_element_type=jnp.float32,
    )


def swap_blocks(parts):
    parts = list(parts)
    block = lax.broadcasted_iota(jnp.int32, parts[0].shape, 1) // BLOCK
    for step in (1, 2, 4):
        upper = (block & step) != 0
        for i in range(GROUP):
            if i & step:
                continue
            a, b = parts[i], parts[i | step]
            parts[i] = jnp.where(upper, pltpu.roll(b, step * BLOCK, 1), a)
            parts[i | step] = jnp.where(upper, b, pltpu.roll(a, LANES - step * BLOCK, 1))
    return parts


def columns(shard, half):
    return pl.ds(pl.multiple_of(shard * SHARD + half * SPAN, SPAN), SPAN)


def merge_kernel(t_ref, gradient, feedback, out, gradient_part, feedback_part, merged, sems):
    t = t_ref[0]
    wide = TP // CHUNKS * SHARD
    copies = []
    for chunk in range(CHUNKS):
        lanes = pl.ds(chunk * wide, wide)
        copies.append(
            [
                pltpu.make_async_copy(source.at[0, :, lanes], target.at[:, lanes], sems.at[i, chunk])
                for i, (source, target) in enumerate(
                    ((gradient, gradient_part), (feedback, feedback_part))
                )
            ]
        )
        for copy in copies[chunk]:
            copy.start()
    results = []
    for shard in range(TP):
        if shard % (TP // CHUNKS) == 0:
            for copy in copies[shard // (TP // CHUNKS)]:
                copy.wait()
        for half in range(2):
            start = shard * SHARD + half * SPAN
            lanes = slice(start, start + SPAN)
            place = shard * 2 + half
            merged[place] = gradient_part[:, lanes].astype(jnp.float32) + feedback_part[:, lanes]
            chip = (shard - t + (4 - half) * (TP // 2)) % TP
            results.append(
                pltpu.make_async_copy(merged.at[place], out.at[chip * 2 + half], sems.at[2, place])
            )
            results[place].start()
    for copy in results:
        copy.wait()


def half_kernel(core_ref, q_ref, out):
    out[...] = jnp.where(core_ref[0] == 0, q_ref[:, :SPAN], q_ref[:, SPAN:])


def twice_kernel(q_part, out):
    out[:RANK, :] = q_part[...]
    out[RANK:, :] = q_part[...]


def unpack_blocks(parts, th):
    return jnp.concatenate(swap_blocks([parts[th * GROUP + tl] for tl in range(GROUP)]), axis=0)


def factor_kernel(merged, q_twice, out):
    total = merged[0]
    for d in range(1, DP):
        total = total + merged[d]
    factor = dot(total, q_twice[...], 1, 1)
    lane = lax.broadcasted_iota(jnp.int32, (HALF, LANES), 1)
    packed = jnp.where(lane < RANK, factor[:HALF], factor[HALF:])
    pieces = swap_blocks(
        [
            total[g * 8 : (g + 1) * 8, h * LANES : (h + 1) * LANES]
            for h in range(2)
            for g in range(ROWS // 8)
        ]
    )
    for d in range(DP):
        out[d, :HALF, :] = packed
        out[d, HALF:, :] = pieces[d // 2 % GROUP]


def unpack_rows(packed):
    return jnp.concatenate([packed[:, :RANK], packed[:, RANK:]], axis=0)


def project_kernel(core_ref, chip_ref, t_ref, parts, out):
    packed = parts[0, :HALF, :]
    for d in range(1, DP):
        packed = packed + parts[d, :HALF, :]
    rows = unpack_rows(packed)
    low = chip_ref[0] < GROUP
    for th in range(TP // GROUP):
        pieces = []
        for tl in range(GROUP):
            source = (th * GROUP + tl - t_ref[0] + (4 - core_ref[0]) * (TP // 2)) % TP
            pieces.append(parts[source * 2 + core_ref[0], HALF:, :])
        pieces = swap_blocks(pieces)
        total = jnp.concatenate(
            [jnp.where(low, pieces[g], pieces[g + ROWS // 8]) for g in range(ROWS // 8)], axis=0
        )
        term = dot(rows, total, 0, 0)
        chunks = swap_blocks([term[kh * 8 : (kh + 1) * 8] for kh in range(GROUP)])
        for tl, chunk in enumerate(chunks):
            out[th * GROUP + tl, :HALF, :] = packed
            out[th * GROUP + tl, HALF:, :] = chunk


def chunk_kernel(parts, out, chunk_out):
    total = parts[0, HALF:, :]
    for t in range(1, TP):
        total = total + parts[t, HALF:, :]
    chunk_out[...] = total
    for t in range(TP):
        out[t] = total


def inverse_triangle(gram, rows_ref):
    row = lax.broadcasted_iota(jnp.int32, (RANK, LANES), 0)
    lane = lax.broadcasted_iota(jnp.int32, (RANK, LANES), 1)
    identity = jnp.where(lane == row + RANK, 1.0, 0.0)
    work = jnp.concatenate([gram, jnp.zeros_like(gram)], axis=1) + identity
    for k in range(RANK):
        pivot_row = work[k : k + 1, :]
        pivot = work[k : k + 1, k : k + 1]
        rows_ref[k : k + 1, :] = pivot_row * lax.rsqrt(pivot)
        if k + 1 < RANK:
            scaled = pivot_row * (1.0 / pivot)
            column = work[:, k : k + 1]
            work = work - jnp.where(row > k, column, 0.0) * scaled
    return rows_ref[:, RANK:]


def basis_kernel(t_ref, parts, inverse_out, basis_out, rows_ref):
    flat = parts[:, :HALF, :].reshape(TP * HALF, LANES)
    whole = unpack_rows(flat)
    inverse = inverse_triangle(dot(whole, whole, 0, 0), rows_ref)
    inverse_out[...] = inverse
    own = unpack_rows(parts[t_ref[0], :HALF, :])
    basis_out[...] = dot(own, inverse, 1, 1)


def approx_kernel(inverse, basis, w_parts, chunk, out):
    approx = []
    for th in range(TP // GROUP):
        q_tile = dot(inverse[...], unpack_blocks(w_parts, th), 1, 0) * (1.0 / DP)
        approx.append(dot(basis[...], q_tile, 1, 0))
    message = jnp.concatenate(approx + [chunk[...]], axis=0)
    for chip in range(CHIPS):
        out[chip] = message


def finish_half(half_ref, gradient, feedback, momentum, inverse, parts, outs, scratch, sems):
    half = half_ref[0]
    new_feedback, new_momentum, q_out = outs
    feedback_part, momentum_part, q_part = scratch
    for group in range(CHIPS // GROUP):
        chips = range(group * GROUP, (group + 1) * GROUP)
        w_tile = jnp.concatenate(swap_blocks([parts[chip, 2 * ROWS :, :] for chip in chips]), axis=0)
        place = slice(group * LANES, (group + 1) * LANES)
        q_part[:, place] = dot(inverse[...], w_tile, 1, 0) * (1.0 / DP)
    copies = [pltpu.make_async_copy(q_part, q_out.at[:, columns(0, half)], sems.at[2, 0])]
    copies[0].start()
    for th in range(TP // GROUP):
        rows = slice(th * ROWS, (th + 1) * ROWS)
        for group in range(CHIPS // GROUP):
            chips = range(group * GROUP, (group + 1) * GROUP)
            place = slice(group * LANES, (group + 1) * LANES)
            for tl, part in enumerate(swap_blocks([parts[chip, rows, :] for chip in chips])):
                shard = th * GROUP + tl
                start = shard * SHARD + half * SPAN + group * LANES
                lanes = pl.ds(pl.multiple_of(start, LANES), LANES)
                merged = gradient[0, :, lanes].astype(jnp.float32) + feedback[0, :, lanes]
                feedback_part[shard, :, place] = merged - part
                momentum_part[shard, :, place] = BETA * momentum[:, lanes] + part
        for shard in range(th * GROUP, (th + 1) * GROUP):
            lanes = columns(shard, half)
            copies += [
                pltpu.make_async_copy(
                    feedback_part.at[shard], new_feedback.at[0, :, lanes], sems.at[0, shard]
                ),
                pltpu.make_async_copy(
                    momentum_part.at[shard], new_momentum.at[:, lanes], sems.at[1, shard]
                ),
            ]
            copies[-2].start()
            copies[-1].start()
    for copy in copies:
        copy.wait()


def finish_own_kernel(half_ref, gradient, feedback, momentum, inverse, parts, *refs):
    finish_half(half_ref, gradient, feedback, momentum, inverse, parts, refs[:3], refs[3:6], refs[6])


def finish_other_kernel(half_ref, gradient, feedback, momentum, inverse, parts, *refs):
    finish_half(half_ref, gradient, feedback, momentum, inverse, parts, refs[3:6], refs[6:9], refs[9])


def local(kernel, *shapes, scalars=0, inputs=1, scratch=(), flops=100_000, far=(), far_out=False, alias=None, room=32):
    vmem, anywhere = pl.BlockSpec(memory_space=pltpu.VMEM), pl.BlockSpec(memory_space=pltpu.HBM)
    return pl.pallas_call(
        kernel,
        out_shape=[jax.ShapeDtypeStruct(shape, jnp.float32) for shape in shapes],
        in_specs=[pl.BlockSpec(memory_space=pltpu.SMEM)] * scalars
        + [anywhere if i in far else vmem for i in range(inputs)],
        out_specs=[anywhere if far_out else vmem] * len(shapes),
        scratch_shapes=list(scratch),
        input_output_aliases=alias or {},
        cost_estimate=pl.CostEstimate(flops=flops, bytes_accessed=100_000, transcendentals=0),
        compiler_params=pltpu.CompilerParams(vmem_limit_bytes=room * 1024 * 1024),
    )


def exchange(parts, axis, groups=None):
    return lax.all_to_all(parts, axis, 0, 0, tiled=True, axis_index_groups=groups)


def swap_cores(parts):
    return lax.ppermute(parts, "dp", [(d, d ^ 1) for d in range(DP)])


def permute(parts, target):
    pairs = []
    for d in range(DP):
        for t in range(TP):
            chip, plane = target(d // 2, d % 2, t)
            pairs.append((d * TP + t, (chip * 2 + d % 2) * TP + plane))
    return lax.ppermute(parts, ("dp", "tensor"), pairs)


def on_device(gradient, feedback, momentum, q_previous):
    d = lax.axis_index("dp").reshape(1)
    core, chip = d & 1, d >> 1
    t = lax.axis_index("tensor").reshape(1)
    chips = [list(range(c, DP, 2)) for c in range(2)]
    q_part = local(half_kernel, (RANK, SPAN), scalars=1)(core, q_previous)[0]
    q_part = permute(q_part, lambda chip, c, plane: (chip, (plane - chip - c * (TP // 2)) % TP))
    q_part = local(twice_kernel, (2 * RANK, SPAN), flops=100_000)(q_part)[0]
    merged = local(
        merge_kernel,
        (DP, ROWS, SPAN),
        scalars=1,
        inputs=2,
        far=(0, 1),
        far_out=True,
        room=60,
        scratch=[
            pltpu.VMEM(gradient.shape[1:], jnp.bfloat16),
            pltpu.VMEM(feedback.shape[1:], jnp.float32),
            pltpu.VMEM((DP, ROWS, SPAN), jnp.float32),
            pltpu.SemaphoreType.DMA((3, DP)),
        ],
    )(t, gradient, feedback)[0]
    merged = exchange(merged, "dp")
    factor = local(factor_kernel, (DP, HALF + 8, LANES), inputs=2)(merged, q_part)[0]
    factor = exchange(factor, "dp")
    parts = local(project_kernel, (TP, HALF + 8, LANES), scalars=3)(core, chip, t, factor)[0]
    parts = exchange(parts, "tensor")
    w_parts, chunk = local(chunk_kernel, (TP, 8, LANES), (8, LANES))(parts)
    w_parts = exchange(w_parts, "tensor")
    inverse, basis = local(
        basis_kernel,
        (RANK, RANK),
        (ROWS, RANK),
        scalars=1,
        scratch=[pltpu.VMEM((RANK, LANES), jnp.float32)],
    )(t, parts)
    own = local(approx_kernel, (CHIPS, 2 * ROWS + 8, LANES), inputs=4)(
        inverse, basis, w_parts, chunk
    )[0]
    own = exchange(own, "dp", chips)
    other = swap_cores(own)
    shapes = (feedback.shape, momentum.shape, q_previous.shape)
    scratch = [
        pltpu.VMEM((TP, ROWS, SPAN), jnp.float32),
        pltpu.VMEM((TP, ROWS, SPAN), jnp.float32),
        pltpu.VMEM((RANK, SPAN), jnp.float32),
        pltpu.SemaphoreType.DMA((3, TP)),
    ]
    outs = local(
        finish_own_kernel, *shapes, scalars=1, inputs=5, scratch=scratch, far_out=True
    )(core, gradient, feedback, momentum, inverse, own)
    outs = local(
        finish_other_kernel,
        *shapes,
        scalars=1,
        inputs=8,
        scratch=scratch,
        far=(5, 6, 7),
        far_out=True,
        alias={6: 0, 7: 1, 8: 2},
    )(1 - core, gradient, feedback, momentum, inverse, other, *outs)
    return tuple(outs)


def solution(mesh):
    placed = (
        P("dp", "tensor", None),
        P("dp", "tensor", None),
        P("tensor", None),
        P(None, "tensor"),
    )
    return jax.shard_map(
        on_device,
        mesh=mesh,
        in_specs=placed,
        out_specs=(P("dp", "tensor", None), P("tensor", None), P(None, "tensor")),
        check_vma=False,
    )
```

```python
import functools

import jax
import jax.numpy as jnp
from jax import lax
from jax.experimental import pallas as pl
from jax.experimental.pallas import tpu as pltpu
from jax.sharding import PartitionSpec as P

BETA = 0.9
HIGH = lax.Precision.HIGHEST

DP = 32
TP = 16
ROWS = 32
RANK = 64
LANES = 128
BLOCK = 16
GROUP = LANES // BLOCK
SPAN = BLOCK * TP
CHUNKS = 4
SHARD = DP * BLOCK
CHIPS = DP // 2
HALF = ROWS // 2


def dot(left, right, left_dim, right_dim):
    return lax.dot_general(
        left,
        right,
        (((left_dim,), (right_dim,)), ((), ())),
        precision=HIGH,
        preferred_element_type=jnp.float32,
    )


def swap_blocks(parts):
    parts = list(parts)
    block = lax.broadcasted_iota(jnp.int32, parts[0].shape, 1) // BLOCK
    for step in (1, 2, 4):
        upper = (block & step) != 0
        for i in range(GROUP):
            if i & step:
                continue
            a, b = parts[i], parts[i | step]
            parts[i] = jnp.where(upper, pltpu.roll(b, step * BLOCK, 1), a)
            parts[i | step] = jnp.where(upper, b, pltpu.roll(a, LANES - step * BLOCK, 1))
    return parts


def gather_blocks(matrix, lane_block):
    block = lax.broadcasted_iota(jnp.int32, (8, LANES), 1) // BLOCK
    moved = pltpu.roll(matrix, (GROUP - lane_block) % GROUP * BLOCK, 1)
    out = jnp.zeros((8, LANES), jnp.float32)
    for kh in range(GROUP):
        piece = moved[kh * 8 : (kh + 1) * 8, :]
        if kh:
            piece = pltpu.roll(piece, kh * BLOCK, 1)
        out = jnp.where(block == kh, piece, out)
    return out


def columns(shard, half):
    return pl.ds(pl.multiple_of(shard * SHARD + half * SPAN, SPAN), SPAN)


def merge_kernel(t_ref, gradient, feedback, out, gradient_part, feedback_part, merged, sems):
    t = t_ref[0]
    wide = TP // CHUNKS * SHARD
    copies = []
    for chunk in range(CHUNKS):
        lanes = pl.ds(chunk * wide, wide)
        copies.append(
            [
                pltpu.make_async_copy(source.at[0, :, lanes], target.at[:, lanes], sems.at[i, chunk])
                for i, (source, target) in enumerate(
                    ((gradient, gradient_part), (feedback, feedback_part))
                )
            ]
        )
        for copy in copies[chunk]:
            copy.start()
    results = []
    for shard in range(TP):
        if shard % (TP // CHUNKS) == 0:
            for copy in copies[shard // (TP // CHUNKS)]:
                copy.wait()
        for half in range(2):
            start = shard * SHARD + half * SPAN
            lanes = slice(start, start + SPAN)
            place = shard * 2 + half
            merged[place] = gradient_part[:, lanes].astype(jnp.float32) + feedback_part[:, lanes]
            chip = (shard - t + (4 - half) * (TP // 2)) % TP
            results.append(
                pltpu.make_async_copy(merged.at[place], out.at[chip * 2 + half], sems.at[2, place])
            )
            results[place].start()
    for copy in results:
        copy.wait()


def half_kernel(core_ref, q_ref, out):
    out[...] = jnp.where(core_ref[0] == 0, q_ref[:, :SPAN], q_ref[:, SPAN:])


def twice_kernel(q_part, out):
    out[:RANK, :] = q_part[...]
    out[RANK:, :] = q_part[...]


def factor_kernel(merged, q_twice, out):
    total = merged[0]
    for d in range(1, DP):
        total = total + merged[d]
    factor = dot(total, q_twice[...], 1, 1)
    lane = lax.broadcasted_iota(jnp.int32, (HALF, LANES), 1)
    packed = jnp.where(lane < RANK, factor[:HALF], factor[HALF:])
    pieces = swap_blocks(
        [
            total[g * 8 : (g + 1) * 8, h * LANES : (h + 1) * LANES]
            for h in range(2)
            for g in range(ROWS // 8)
        ]
    )
    for d in range(DP):
        out[d, :HALF, :] = packed
        out[d, HALF:, :] = pieces[d // 2 % GROUP]


def unpack_rows(packed):
    return jnp.concatenate([packed[:, :RANK], packed[:, RANK:]], axis=0)


def project_kernel(core_ref, chip_ref, t_ref, parts, out):
    packed = parts[0, :HALF, :]
    for d in range(1, DP):
        packed = packed + parts[d, :HALF, :]
    out[:HALF, :] = packed
    low = chip_ref[0] < GROUP
    for th in range(TP // GROUP):
        pieces = []
        for tl in range(GROUP):
            source = (th * GROUP + tl - t_ref[0] + (4 - core_ref[0]) * (TP // 2)) % TP
            pieces.append(parts[source * 2 + core_ref[0], HALF:, :])
        pieces = swap_blocks(pieces)
        start = HALF + th * ROWS
        for g in range(ROWS // 8):
            out[start + g * 8 : start + (g + 1) * 8, :] = jnp.where(
                low, pieces[g], pieces[g + ROWS // 8]
            )


def inverse_triangle(gram):
    size = 8
    count = RANK // size
    row = lax.broadcasted_iota(jnp.int32, (RANK, LANES), 0)
    lane = lax.broadcasted_iota(jnp.int32, (RANK, LANES), 1)
    identity = jnp.where(lane == row + RANK, 1.0, 0.0)
    work = jnp.concatenate([gram, jnp.zeros_like(gram)], axis=1) + identity
    work = [work[g * size : (g + 1) * size, :] for g in range(count)]
    row = lax.broadcasted_iota(jnp.int32, (size, LANES), 0)
    for b in range(count):
        spread = {
            g: [
                jnp.broadcast_to(work[g][:, b * size + k : b * size + k + 1], (size, LANES))
                for k in range(size)
            ]
            for g in range(b, count)
        }
        pivots = jnp.zeros((size, LANES), jnp.float32)
        for k in range(size):
            pivot_row = work[b][k : k + 1, :]
            heads = [spread[b][j][k : k + 1, :] for j in range(size)]
            pivots = jnp.where(row == k, heads[k], pivots)
            reciprocal = 1.0 / heads[k]
            for g in range(b, count):
                factor = spread[g][k] * reciprocal
                if g == b:
                    factor = jnp.where(row > k, factor, 0.0)
                work[g] = work[g] - factor * pivot_row
                for j in range(k + 1, size):
                    spread[g][j] = spread[g][j] - factor * heads[j]
        work[b] = work[b] * lax.rsqrt(pivots)
    return jnp.concatenate(work, axis=0)[:, RANK:]


def solve_kernel(t_ref, parts, out):
    t = t_ref[0]
    whole = unpack_rows(parts[:, :HALF, :].reshape(TP * HALF, LANES))
    whole_t = whole.T
    inverse = inverse_triangle(dot(whole_t, whole, 1, 0))
    basis = dot(unpack_rows(parts[t, :HALF, :]), inverse, 1, 1)
    approx, q_tiles = [], []
    for th in range(TP // GROUP):
        start = HALF + th * ROWS
        sums = jnp.concatenate(
            [
                parts[:, start + h * HALF : start + (h + 1) * HALF, :].reshape(TP * HALF, LANES)
                for h in range(2)
            ],
            axis=0,
        )
        q_tiles.append(dot(inverse, dot(whole_t, sums, 1, 0), 1, 0) * (1.0 / DP))
        approx.append(dot(basis, q_tiles[th], 1, 0))
    mine = jnp.where(t // GROUP == 0, q_tiles[0], q_tiles[1])
    message = jnp.concatenate(approx + [gather_blocks(mine, t % GROUP)], axis=0)
    for chip in range(CHIPS):
        out[chip] = message


def finish_half(half_ref, gradient, feedback, momentum, parts, outs, scratch, sems):
    half = half_ref[0]
    new_feedback, new_momentum, q_out = outs
    feedback_part, momentum_part, q_part = scratch
    for group in range(CHIPS // GROUP):
        chips = range(group * GROUP, (group + 1) * GROUP)
        chunks = swap_blocks([parts[chip, 2 * ROWS :, :] for chip in chips])
        q_part[:, group * LANES : (group + 1) * LANES] = jnp.concatenate(chunks, axis=0)
    copies = [pltpu.make_async_copy(q_part, q_out.at[:, columns(0, half)], sems.at[2, 0])]
    copies[0].start()
    for th in range(TP // GROUP):
        rows = slice(th * ROWS, (th + 1) * ROWS)
        for group in range(CHIPS // GROUP):
            chips = range(group * GROUP, (group + 1) * GROUP)
            place = slice(group * LANES, (group + 1) * LANES)
            for tl, part in enumerate(swap_blocks([parts[chip, rows, :] for chip in chips])):
                shard = th * GROUP + tl
                start = shard * SHARD + half * SPAN + group * LANES
                lanes = pl.ds(pl.multiple_of(start, LANES), LANES)
                merged = gradient[0, :, lanes].astype(jnp.float32) + feedback[0, :, lanes]
                feedback_part[shard, :, place] = merged - part
                momentum_part[shard, :, place] = BETA * momentum[:, lanes] + part
        for shard in range(th * GROUP, (th + 1) * GROUP):
            lanes = columns(shard, half)
            copies += [
                pltpu.make_async_copy(
                    feedback_part.at[shard], new_feedback.at[0, :, lanes], sems.at[0, shard]
                ),
                pltpu.make_async_copy(
                    momentum_part.at[shard], new_momentum.at[:, lanes], sems.at[1, shard]
                ),
            ]
            copies[-2].start()
            copies[-1].start()
    for copy in copies:
        copy.wait()


def finish_own_kernel(half_ref, gradient, feedback, momentum, parts, *refs):
    finish_half(half_ref, gradient, feedback, momentum, parts, refs[:3], refs[3:6], refs[6])


def finish_other_kernel(half_ref, gradient, feedback, momentum, parts, *refs):
    finish_half(half_ref, gradient, feedback, momentum, parts, refs[3:6], refs[6:9], refs[9])


def local(kernel, *shapes, scalars=0, inputs=1, scratch=(), flops=100_000, far=(), far_out=False, alias=None, room=32):
    vmem, anywhere = pl.BlockSpec(memory_space=pltpu.VMEM), pl.BlockSpec(memory_space=pltpu.HBM)
    return pl.pallas_call(
        kernel,
        out_shape=[jax.ShapeDtypeStruct(shape, jnp.float32) for shape in shapes],
        in_specs=[pl.BlockSpec(memory_space=pltpu.SMEM)] * scalars
        + [anywhere if i in far else vmem for i in range(inputs)],
        out_specs=[anywhere if far_out else vmem] * len(shapes),
        scratch_shapes=list(scratch),
        input_output_aliases=alias or {},
        cost_estimate=pl.CostEstimate(flops=flops, bytes_accessed=100_000, transcendentals=0),
        compiler_params=pltpu.CompilerParams(vmem_limit_bytes=room * 1024 * 1024),
    )


def exchange(parts, axis, groups=None):
    return lax.all_to_all(parts, axis, 0, 0, tiled=True, axis_index_groups=groups)


def swap_cores(parts):
    return lax.ppermute(parts, "dp", [(d, d ^ 1) for d in range(DP)])


def permute(parts, target):
    pairs = []
    for d in range(DP):
        for t in range(TP):
            chip, plane = target(d // 2, d % 2, t)
            pairs.append((d * TP + t, (chip * 2 + d % 2) * TP + plane))
    return lax.ppermute(parts, ("dp", "tensor"), pairs)


def on_device(gradient, feedback, momentum, q_previous):
    d = lax.axis_index("dp").reshape(1)
    core, chip = d & 1, d >> 1
    t = lax.axis_index("tensor").reshape(1)
    chips = [list(range(c, DP, 2)) for c in range(2)]
    q_part = local(half_kernel, (RANK, SPAN), scalars=1)(core, q_previous)[0]
    q_part = permute(q_part, lambda chip, c, plane: (chip, (plane - chip - c * (TP // 2)) % TP))
    q_part = local(twice_kernel, (2 * RANK, SPAN), flops=100_000)(q_part)[0]
    merged = local(
        merge_kernel,
        (DP, ROWS, SPAN),
        scalars=1,
        inputs=2,
        far=(0, 1),
        far_out=True,
        room=60,
        scratch=[
            pltpu.VMEM(gradient.shape[1:], jnp.bfloat16),
            pltpu.VMEM(feedback.shape[1:], jnp.float32),
            pltpu.VMEM((DP, ROWS, SPAN), jnp.float32),
            pltpu.SemaphoreType.DMA((3, DP)),
        ],
    )(t, gradient, feedback)[0]
    merged = exchange(merged, "dp")
    factor = local(factor_kernel, (DP, HALF + 8, LANES), inputs=2)(merged, q_part)[0]
    factor = exchange(factor, "dp")
    parts = local(project_kernel, (HALF + 2 * ROWS, LANES), scalars=3)(core, chip, t, factor)[0]
    parts = lax.all_gather(parts, "tensor")
    own = local(solve_kernel, (CHIPS, 2 * ROWS + 8, LANES), scalars=1)(t, parts)[0]
    own = exchange(own, "dp", chips)
    other = swap_cores(own)
    shapes = (feedback.shape, momentum.shape, q_previous.shape)
    scratch = [
        pltpu.VMEM((TP, ROWS, SPAN), jnp.float32),
        pltpu.VMEM((TP, ROWS, SPAN), jnp.float32),
        pltpu.VMEM((RANK, SPAN), jnp.float32),
        pltpu.SemaphoreType.DMA((3, TP)),
    ]
    outs = local(
        finish_own_kernel, *shapes, scalars=1, inputs=4, scratch=scratch, far_out=True
    )(core, gradient, feedback, momentum, own)
    outs = local(
        finish_other_kernel,
        *shapes,
        scalars=1,
        inputs=7,
        scratch=scratch,
        far=(4, 5, 6),
        far_out=True,
        alias={5: 0, 6: 1, 7: 2},
    )(1 - core, gradient, feedback, momentum, other, *outs)
    return tuple(outs)


def solution(mesh):
    placed = (
        P("dp", "tensor", None),
        P("dp", "tensor", None),
        P("tensor", None),
        P(None, "tensor"),
    )
    return jax.shard_map(
        on_device,
        mesh=mesh,
        in_specs=placed,
        out_specs=(P("dp", "tensor", None), P("tensor", None), P(None, "tensor")),
        check_vma=False,
    )
```

```python
import functools

import jax
import jax.numpy as jnp
from jax import lax
from jax.experimental import pallas as pl
from jax.experimental.pallas import tpu as pltpu
from jax.sharding import PartitionSpec as P

BETA = 0.9
HIGH = lax.Precision.HIGHEST

DP = 32
TP = 16
ROWS = 32
RANK = 64
LANES = 128
BLOCK = 16
GROUP = LANES // BLOCK
SPAN = BLOCK * TP
CHUNKS = 4
SHARD = DP * BLOCK
CHIPS = DP // 2
HALF = ROWS // 2


def dot(left, right, left_dim, right_dim):
    return lax.dot_general(
        left,
        right,
        (((left_dim,), (right_dim,)), ((), ())),
        precision=HIGH,
        preferred_element_type=jnp.float32,
    )


def swap_blocks(parts):
    parts = list(parts)
    block = lax.broadcasted_iota(jnp.int32, parts[0].shape, 1) // BLOCK
    for step in (1, 2, 4):
        upper = (block & step) != 0
        for i in range(GROUP):
            if i & step:
                continue
            a, b = parts[i], parts[i | step]
            parts[i] = jnp.where(upper, pltpu.roll(b, step * BLOCK, 1), a)
            parts[i | step] = jnp.where(upper, b, pltpu.roll(a, LANES - step * BLOCK, 1))
    return parts


def gather_blocks(matrix, lane_block):
    block = lax.broadcasted_iota(jnp.int32, (8, LANES), 1) // BLOCK
    moved = pltpu.roll(matrix, (GROUP - lane_block) % GROUP * BLOCK, 1)
    out = jnp.zeros((8, LANES), jnp.float32)
    for kh in range(GROUP):
        piece = moved[kh * 8 : (kh + 1) * 8, :]
        if kh:
            piece = pltpu.roll(piece, kh * BLOCK, 1)
        out = jnp.where(block == kh, piece, out)
    return out


def columns(shard, half):
    return pl.ds(pl.multiple_of(shard * SHARD + half * SPAN, SPAN), SPAN)


def merge_kernel(t_ref, gradient, feedback, out, gradient_part, feedback_part, merged, sems):
    t = t_ref[0]
    wide = TP // CHUNKS * SHARD
    copies = []
    for chunk in range(CHUNKS):
        lanes = pl.ds(chunk * wide, wide)
        copies.append(
            [
                pltpu.make_async_copy(source.at[0, :, lanes], target.at[:, lanes], sems.at[i, chunk])
                for i, (source, target) in enumerate(
                    ((gradient, gradient_part), (feedback, feedback_part))
                )
            ]
        )
        for copy in copies[chunk]:
            copy.start()
    results = []
    for shard in range(TP):
        if shard % (TP // CHUNKS) == 0:
            for copy in copies[shard // (TP // CHUNKS)]:
                copy.wait()
        for half in range(2):
            start = shard * SHARD + half * SPAN
            lanes = slice(start, start + SPAN)
            place = shard * 2 + half
            merged[place] = gradient_part[:, lanes].astype(jnp.float32) + feedback_part[:, lanes]
            chip = (shard - t + (4 - half) * (TP // 2)) % TP
            results.append(
                pltpu.make_async_copy(
                    merged.at[place], out.at[chip * 2 + (half ^ (t & 1))], sems.at[2, place]
                )
            )
            results[place].start()
    for copy in results:
        copy.wait()


def half_kernel(half_ref, q_ref, out):
    out[...] = jnp.where(half_ref[0] == 0, q_ref[:, :SPAN], q_ref[:, SPAN:])


def twice_kernel(q_part, out):
    out[:RANK, :] = q_part[...]
    out[RANK:, :] = q_part[...]


def factor_kernel(merged, q_twice, out):
    total = merged[0]
    for d in range(1, DP):
        total = total + merged[d]
    factor = dot(total, q_twice[...], 1, 1)
    lane = lax.broadcasted_iota(jnp.int32, (HALF, LANES), 1)
    packed = jnp.where(lane < RANK, factor[:HALF], factor[HALF:])
    pieces = swap_blocks(
        [
            total[g * 8 : (g + 1) * 8, h * LANES : (h + 1) * LANES]
            for h in range(2)
            for g in range(ROWS // 8)
        ]
    )
    for d in range(DP):
        out[d, :HALF, :] = packed
        out[d, HALF:, :] = pieces[d // 2 % GROUP]


def unpack_rows(packed):
    return jnp.concatenate([packed[:, :RANK], packed[:, RANK:]], axis=0)


def project_kernel(core_ref, chip_ref, t_ref, parts, out):
    half = core_ref[0] ^ (t_ref[0] & 1)
    packed = parts[0, :HALF, :]
    for d in range(1, DP):
        packed = packed + parts[d, :HALF, :]
    out[:HALF, :] = packed
    low = chip_ref[0] < GROUP
    for th in range(TP // GROUP):
        pieces = []
        for tl in range(GROUP):
            source = (th * GROUP + tl - t_ref[0] + (4 - half) * (TP // 2)) % TP
            pieces.append(parts[source * 2 + core_ref[0], HALF:, :])
        pieces = swap_blocks(pieces)
        start = HALF + th * ROWS
        for g in range(ROWS // 8):
            out[start + g * 8 : start + (g + 1) * 8, :] = jnp.where(
                low, pieces[g], pieces[g + ROWS // 8]
            )


def inverse_triangle(gram):
    size = 8
    count = RANK // size
    row = lax.broadcasted_iota(jnp.int32, (RANK, LANES), 0)
    lane = lax.broadcasted_iota(jnp.int32, (RANK, LANES), 1)
    identity = jnp.where(lane == row + RANK, 1.0, 0.0)
    work = jnp.concatenate([gram, jnp.zeros_like(gram)], axis=1) + identity
    work = [work[g * size : (g + 1) * size, :] for g in range(count)]
    row = lax.broadcasted_iota(jnp.int32, (size, LANES), 0)
    for b in range(count):
        spread = {
            g: [
                jnp.broadcast_to(work[g][:, b * size + k : b * size + k + 1], (size, LANES))
                for k in range(size)
            ]
            for g in range(b, count)
        }
        pivots = jnp.zeros((size, LANES), jnp.float32)
        for k in range(size):
            pivot_row = work[b][k : k + 1, :]
            heads = [spread[b][j][k : k + 1, :] for j in range(size)]
            pivots = jnp.where(row == k, heads[k], pivots)
            reciprocal = 1.0 / heads[k]
            for g in range(b, count):
                factor = spread[g][k] * reciprocal
                if g == b:
                    factor = jnp.where(row > k, factor, 0.0)
                work[g] = work[g] - factor * pivot_row
                for j in range(k + 1, size):
                    spread[g][j] = spread[g][j] - factor * heads[j]
        work[b] = work[b] * lax.rsqrt(pivots)
    return jnp.concatenate(work, axis=0)[:, RANK:]


def solve_kernel(t_ref, parts, out):
    t = t_ref[0]
    whole = unpack_rows(parts[:, :HALF, :].reshape(TP * HALF, LANES))
    whole_t = whole.T
    inverse = inverse_triangle(dot(whole_t, whole, 1, 0))
    basis = dot(unpack_rows(parts[t, :HALF, :]), inverse, 1, 1)
    approx, q_tiles = [], []
    for th in range(TP // GROUP):
        start = HALF + th * ROWS
        sums = jnp.concatenate(
            [
                parts[:, start + h * HALF : start + (h + 1) * HALF, :].reshape(TP * HALF, LANES)
                for h in range(2)
            ],
            axis=0,
        )
        q_tiles.append(dot(inverse, dot(whole_t, sums, 1, 0), 1, 0) * (1.0 / DP))
        approx.append(dot(basis, q_tiles[th], 1, 0))
    mine = jnp.where(t // GROUP == 0, q_tiles[0], q_tiles[1])
    message = jnp.concatenate(approx + [gather_blocks(mine, t % GROUP)], axis=0)
    for chip in range(CHIPS):
        out[chip] = message


def finish_half(half_ref, gradient, feedback, momentum, parts, outs, scratch, sems):
    half = half_ref[0]
    new_feedback, new_momentum, q_out = outs
    feedback_part, momentum_part, q_part = scratch
    for group in range(CHIPS // GROUP):
        chips = range(group * GROUP, (group + 1) * GROUP)
        chunks = swap_blocks([parts[chip, 2 * ROWS :, :] for chip in chips])
        q_part[:, group * LANES : (group + 1) * LANES] = jnp.concatenate(chunks, axis=0)
    copies = [pltpu.make_async_copy(q_part, q_out.at[:, columns(0, half)], sems.at[2, 0])]
    copies[0].start()
    for th in range(TP // GROUP):
        rows = slice(th * ROWS, (th + 1) * ROWS)
        for group in range(CHIPS // GROUP):
            chips = range(group * GROUP, (group + 1) * GROUP)
            place = slice(group * LANES, (group + 1) * LANES)
            for tl, part in enumerate(swap_blocks([parts[chip, rows, :] for chip in chips])):
                shard = th * GROUP + tl
                start = shard * SHARD + half * SPAN + group * LANES
                lanes = pl.ds(pl.multiple_of(start, LANES), LANES)
                merged = gradient[0, :, lanes].astype(jnp.float32) + feedback[0, :, lanes]
                feedback_part[shard, :, place] = merged - part
                momentum_part[shard, :, place] = BETA * momentum[:, lanes] + part
        for shard in range(th * GROUP, (th + 1) * GROUP):
            lanes = columns(shard, half)
            copies += [
                pltpu.make_async_copy(
                    feedback_part.at[shard], new_feedback.at[0, :, lanes], sems.at[0, shard]
                ),
                pltpu.make_async_copy(
                    momentum_part.at[shard], new_momentum.at[:, lanes], sems.at[1, shard]
                ),
            ]
            copies[-2].start()
            copies[-1].start()
    for copy in copies:
        copy.wait()


def finish_own_kernel(half_ref, gradient, feedback, momentum, parts, *refs):
    finish_half(half_ref, gradient, feedback, momentum, parts, refs[:3], refs[3:6], refs[6])


def finish_other_kernel(half_ref, gradient, feedback, momentum, parts, *refs):
    finish_half(half_ref, gradient, feedback, momentum, parts, refs[3:6], refs[6:9], refs[9])


def local(kernel, *shapes, scalars=0, inputs=1, scratch=(), flops=100_000, far=(), far_out=False, alias=None, room=32):
    vmem, anywhere = pl.BlockSpec(memory_space=pltpu.VMEM), pl.BlockSpec(memory_space=pltpu.HBM)
    return pl.pallas_call(
        kernel,
        out_shape=[jax.ShapeDtypeStruct(shape, jnp.float32) for shape in shapes],
        in_specs=[pl.BlockSpec(memory_space=pltpu.SMEM)] * scalars
        + [anywhere if i in far else vmem for i in range(inputs)],
        out_specs=[anywhere if far_out else vmem] * len(shapes),
        scratch_shapes=list(scratch),
        input_output_aliases=alias or {},
        cost_estimate=pl.CostEstimate(flops=flops, bytes_accessed=100_000, transcendentals=0),
        compiler_params=pltpu.CompilerParams(vmem_limit_bytes=room * 1024 * 1024),
    )


def exchange(parts, axis, groups=None):
    return lax.all_to_all(parts, axis, 0, 0, tiled=True, axis_index_groups=groups)


def swap_cores(parts):
    return lax.ppermute(parts, "dp", [(d, d ^ 1) for d in range(DP)])


def fetch_shards(parts):
    pairs = []
    for d in range(DP):
        for t in range(TP):
            plane = (t + d // 2 + (d & 1 ^ t & 1) * (TP // 2)) % TP
            pairs.append((d * TP + plane, d * TP + t))
    return lax.ppermute(parts, ("dp", "tensor"), pairs)


def gather_lines(parts):
    lines = [
        [(chip * 2 + (t + v) % 2) * TP + t for t in range(TP)] for chip in range(CHIPS) for v in range(2)
    ]
    return lax.all_gather(parts, ("dp", "tensor"), axis_index_groups=lines)


def on_device(gradient, feedback, momentum, q_previous):
    d = lax.axis_index("dp").reshape(1)
    core, chip = d & 1, d >> 1
    t = lax.axis_index("tensor").reshape(1)
    chips = [list(range(c, DP, 2)) for c in range(2)]
    half = core ^ (t & 1)
    q_part = local(half_kernel, (RANK, SPAN), scalars=1)(core ^ ((t - chip) & 1), q_previous)[0]
    q_part = fetch_shards(q_part)
    q_part = local(twice_kernel, (2 * RANK, SPAN), flops=100_000)(q_part)[0]
    merged = local(
        merge_kernel,
        (DP, ROWS, SPAN),
        scalars=1,
        inputs=2,
        far=(0, 1),
        far_out=True,
        room=60,
        scratch=[
            pltpu.VMEM(gradient.shape[1:], jnp.bfloat16),
            pltpu.VMEM(feedback.shape[1:], jnp.float32),
            pltpu.VMEM((DP, ROWS, SPAN), jnp.float32),
            pltpu.SemaphoreType.DMA((3, DP)),
        ],
    )(t, gradient, feedback)[0]
    merged = exchange(merged, "dp")
    factor = local(factor_kernel, (DP, HALF + 8, LANES), inputs=2)(merged, q_part)[0]
    factor = exchange(factor, "dp")
    parts = local(project_kernel, (HALF + 2 * ROWS, LANES), scalars=3)(core, chip, t, factor)[0]
    parts = gather_lines(parts)
    own = local(solve_kernel, (CHIPS, 2 * ROWS + 8, LANES), scalars=1)(t, parts)[0]
    own = exchange(own, "dp", chips)
    other = swap_cores(own)
    shapes = (feedback.shape, momentum.shape, q_previous.shape)
    scratch = [
        pltpu.VMEM((TP, ROWS, SPAN), jnp.float32),
        pltpu.VMEM((TP, ROWS, SPAN), jnp.float32),
        pltpu.VMEM((RANK, SPAN), jnp.float32),
        pltpu.SemaphoreType.DMA((3, TP)),
    ]
    outs = local(
        finish_own_kernel, *shapes, scalars=1, inputs=4, scratch=scratch, far_out=True
    )(half, gradient, feedback, momentum, own)
    outs = local(
        finish_other_kernel,
        *shapes,
        scalars=1,
        inputs=7,
        scratch=scratch,
        far=(4, 5, 6),
        far_out=True,
        alias={5: 0, 6: 1, 7: 2},
    )(1 - half, gradient, feedback, momentum, other, *outs)
    return tuple(outs)


def solution(mesh):
    placed = (
        P("dp", "tensor", None),
        P("dp", "tensor", None),
        P("tensor", None),
        P(None, "tensor"),
    )
    return jax.shard_map(
        on_device,
        mesh=mesh,
        in_specs=placed,
        out_specs=(P("dp", "tensor", None), P("tensor", None), P(None, "tensor")),
        check_vma=False,
    )
```

```python
import functools

import jax
import jax.numpy as jnp
from jax import lax
from jax.experimental import pallas as pl
from jax.experimental.pallas import tpu as pltpu
from jax.sharding import PartitionSpec as P

BETA = 0.9
HIGH = lax.Precision.HIGHEST

DP = 32
TP = 16
ROWS = 32
RANK = 64
LANES = 128
BLOCK = 16
GROUP = LANES // BLOCK
SPAN = BLOCK * TP
SHARD = DP * BLOCK
CHIPS = DP // 2
HALF = ROWS // 2


def dot(left, right, left_dim, right_dim):
    return lax.dot_general(
        left,
        right,
        (((left_dim,), (right_dim,)), ((), ())),
        precision=HIGH,
        preferred_element_type=jnp.float32,
    )


def swap_blocks(parts):
    parts = list(parts)
    block = lax.broadcasted_iota(jnp.int32, parts[0].shape, 1) // BLOCK
    for step in (1, 2, 4):
        upper = (block & step) != 0
        for i in range(GROUP):
            if i & step:
                continue
            a, b = parts[i], parts[i | step]
            parts[i] = jnp.where(upper, pltpu.roll(b, step * BLOCK, 1), a)
            parts[i | step] = jnp.where(upper, b, pltpu.roll(a, LANES - step * BLOCK, 1))
    return parts


def gather_blocks(matrix, lane_block):
    block = lax.broadcasted_iota(jnp.int32, (8, LANES), 1) // BLOCK
    moved = pltpu.roll(matrix, (GROUP - lane_block) % GROUP * BLOCK, 1)
    out = jnp.zeros((8, LANES), jnp.float32)
    for kh in range(GROUP):
        piece = moved[kh * 8 : (kh + 1) * 8, :]
        if kh:
            piece = pltpu.roll(piece, kh * BLOCK, 1)
        out = jnp.where(block == kh, piece, out)
    return out


def columns(shard, half):
    return pl.ds(pl.multiple_of(shard * SHARD + half * SPAN, SPAN), SPAN)


def merge_kernel(t_ref, gradient, feedback, out):
    t = t_ref[0]
    for shard in range(TP):
        for half in range(2):
            start = shard * SHARD + half * SPAN
            lanes = slice(start, start + SPAN)
            chip = (shard - t + (4 - half) * (TP // 2)) % TP
            out[chip * 2 + (half ^ (t & 1))] = (
                gradient[0, :, lanes].astype(jnp.float32) + feedback[0, :, lanes]
            )


def half_kernel(half_ref, q_ref, out):
    out[...] = jnp.where(half_ref[0] == 0, q_ref[:, :SPAN], q_ref[:, SPAN:])


def twice_kernel(q_part, out):
    out[:RANK, :] = q_part[...]
    out[RANK:, :] = q_part[...]


def factor_kernel(merged, q_twice, out):
    total = merged[0]
    for d in range(1, DP):
        total = total + merged[d]
    factor = dot(total, q_twice[...], 1, 1)
    lane = lax.broadcasted_iota(jnp.int32, (HALF, LANES), 1)
    packed = jnp.where(lane < RANK, factor[:HALF], factor[HALF:])
    pieces = swap_blocks(
        [
            total[g * 8 : (g + 1) * 8, h * LANES : (h + 1) * LANES]
            for h in range(2)
            for g in range(ROWS // 8)
        ]
    )
    for d in range(DP):
        out[d, :HALF, :] = packed
        out[d, HALF:, :] = pieces[d // 2 % GROUP]


def unpack_rows(packed):
    return jnp.concatenate([packed[:, :RANK], packed[:, RANK:]], axis=0)


def project_kernel(core_ref, chip_ref, t_ref, parts, out):
    half = core_ref[0] ^ (t_ref[0] & 1)
    packed = parts[0, :HALF, :]
    for d in range(1, DP):
        packed = packed + parts[d, :HALF, :]
    out[:HALF, :] = packed
    low = chip_ref[0] < GROUP
    for th in range(TP // GROUP):
        pieces = []
        for tl in range(GROUP):
            source = (th * GROUP + tl - t_ref[0] + (4 - half) * (TP // 2)) % TP
            pieces.append(parts[source * 2 + core_ref[0], HALF:, :])
        pieces = swap_blocks(pieces)
        start = HALF + th * ROWS
        for g in range(ROWS // 8):
            out[start + g * 8 : start + (g + 1) * 8, :] = jnp.where(
                low, pieces[g], pieces[g + ROWS // 8]
            )


def inverse_triangle(gram):
    size = 8
    count = RANK // size
    row = lax.broadcasted_iota(jnp.int32, (RANK, LANES), 0)
    lane = lax.broadcasted_iota(jnp.int32, (RANK, LANES), 1)
    identity = jnp.where(lane == row + RANK, 1.0, 0.0)
    work = jnp.concatenate([gram, jnp.zeros_like(gram)], axis=1) + identity
    work = [work[g * size : (g + 1) * size, :] for g in range(count)]
    row = lax.broadcasted_iota(jnp.int32, (size, LANES), 0)
    for b in range(count):
        spread = {
            g: [
                jnp.broadcast_to(work[g][:, b * size + k : b * size + k + 1], (size, LANES))
                for k in range(size)
            ]
            for g in range(b, count)
        }
        pivots = jnp.zeros((size, LANES), jnp.float32)
        for k in range(size):
            pivot_row = work[b][k : k + 1, :]
            heads = [spread[b][j][k : k + 1, :] for j in range(size)]
            pivots = jnp.where(row == k, heads[k], pivots)
            reciprocal = 1.0 / heads[k]
            for g in range(b, count):
                factor = spread[g][k] * reciprocal
                if g == b:
                    factor = jnp.where(row > k, factor, 0.0)
                work[g] = work[g] - factor * pivot_row
                for j in range(k + 1, size):
                    spread[g][j] = spread[g][j] - factor * heads[j]
        work[b] = work[b] * lax.rsqrt(pivots)
    return jnp.concatenate(work, axis=0)[:, RANK:]


def solve_kernel(t_ref, parts, out):
    t = t_ref[0]
    whole = unpack_rows(parts[:, :HALF, :].reshape(TP * HALF, LANES))
    whole_t = whole.T
    inverse = inverse_triangle(dot(whole_t, whole, 1, 0))
    basis = dot(unpack_rows(parts[t, :HALF, :]), inverse, 1, 1)
    approx, q_tiles = [], []
    for th in range(TP // GROUP):
        start = HALF + th * ROWS
        sums = jnp.concatenate(
            [
                parts[:, start + h * HALF : start + (h + 1) * HALF, :].reshape(TP * HALF, LANES)
                for h in range(2)
            ],
            axis=0,
        )
        q_tiles.append(dot(inverse, dot(whole_t, sums, 1, 0), 1, 0) * (1.0 / DP))
        approx.append(dot(basis, q_tiles[th], 1, 0))
    mine = jnp.where(t // GROUP == 0, q_tiles[0], q_tiles[1])
    message = jnp.concatenate(approx + [gather_blocks(mine, t % GROUP)], axis=0)
    for chip in range(CHIPS):
        out[chip] = message


def finish_half(half_ref, gradient, feedback, momentum, parts, outs, scratch, sems):
    half = half_ref[0]
    new_feedback, new_momentum, q_out = outs
    feedback_part, momentum_part, q_part = scratch
    for group in range(CHIPS // GROUP):
        chips = range(group * GROUP, (group + 1) * GROUP)
        chunks = swap_blocks([parts[chip, 2 * ROWS :, :] for chip in chips])
        q_part[:, group * LANES : (group + 1) * LANES] = jnp.concatenate(chunks, axis=0)
    copies = [pltpu.make_async_copy(q_part, q_out.at[:, columns(0, half)], sems.at[2, 0])]
    copies[0].start()
    for th in range(TP // GROUP):
        rows = slice(th * ROWS, (th + 1) * ROWS)
        for group in range(CHIPS // GROUP):
            chips = range(group * GROUP, (group + 1) * GROUP)
            place = slice(group * LANES, (group + 1) * LANES)
            for tl, part in enumerate(swap_blocks([parts[chip, rows, :] for chip in chips])):
                shard = th * GROUP + tl
                start = shard * SHARD + half * SPAN + group * LANES
                lanes = pl.ds(pl.multiple_of(start, LANES), LANES)
                merged = gradient[0, :, lanes].astype(jnp.float32) + feedback[0, :, lanes]
                feedback_part[shard, :, place] = merged - part
                momentum_part[shard, :, place] = BETA * momentum[:, lanes] + part
        for shard in range(th * GROUP, (th + 1) * GROUP):
            lanes = columns(shard, half)
            copies += [
                pltpu.make_async_copy(
                    feedback_part.at[shard], new_feedback.at[0, :, lanes], sems.at[0, shard]
                ),
                pltpu.make_async_copy(
                    momentum_part.at[shard], new_momentum.at[:, lanes], sems.at[1, shard]
                ),
            ]
            copies[-2].start()
            copies[-1].start()
    for copy in copies:
        copy.wait()


def finish_own_kernel(half_ref, gradient, feedback, momentum, parts, *refs):
    finish_half(half_ref, gradient, feedback, momentum, parts, refs[:3], refs[3:6], refs[6])


def finish_other_kernel(half_ref, gradient, feedback, momentum, parts, *refs):
    finish_half(half_ref, gradient, feedback, momentum, parts, refs[3:6], refs[6:9], refs[9])


def local(kernel, *shapes, scalars=0, inputs=1, scratch=(), flops=100_000, far=(), far_out=False, alias=None, room=32):
    vmem, anywhere = pl.BlockSpec(memory_space=pltpu.VMEM), pl.BlockSpec(memory_space=pltpu.HBM)
    return pl.pallas_call(
        kernel,
        out_shape=[jax.ShapeDtypeStruct(shape, jnp.float32) for shape in shapes],
        in_specs=[pl.BlockSpec(memory_space=pltpu.SMEM)] * scalars
        + [anywhere if i in far else vmem for i in range(inputs)],
        out_specs=[anywhere if far_out else vmem] * len(shapes),
        scratch_shapes=list(scratch),
        input_output_aliases=alias or {},
        cost_estimate=pl.CostEstimate(flops=flops, bytes_accessed=100_000, transcendentals=0),
        compiler_params=pltpu.CompilerParams(vmem_limit_bytes=room * 1024 * 1024),
    )


def exchange(parts, axis, groups=None):
    return lax.all_to_all(parts, axis, 0, 0, tiled=True, axis_index_groups=groups)


def swap_cores(parts):
    return lax.ppermute(parts, "dp", [(d, d ^ 1) for d in range(DP)])


def fetch_shards(parts):
    pairs = []
    for d in range(DP):
        for t in range(TP):
            plane = (t + d // 2 + (d & 1 ^ t & 1) * (TP // 2)) % TP
            pairs.append((d * TP + plane, d * TP + t))
    return lax.ppermute(parts, ("dp", "tensor"), pairs)


def gather_lines(parts):
    lines = [
        [(chip * 2 + (t + v) % 2) * TP + t for t in range(TP)] for chip in range(CHIPS) for v in range(2)
    ]
    return lax.all_gather(parts, ("dp", "tensor"), axis_index_groups=lines)


def on_device(gradient, feedback, momentum, q_previous):
    d = lax.axis_index("dp").reshape(1)
    core, chip = d & 1, d >> 1
    t = lax.axis_index("tensor").reshape(1)
    chips = [list(range(c, DP, 2)) for c in range(2)]
    half = core ^ (t & 1)
    q_part = local(half_kernel, (RANK, SPAN), scalars=1)(core ^ ((t - chip) & 1), q_previous)[0]
    q_part = fetch_shards(q_part)
    q_part = local(twice_kernel, (2 * RANK, SPAN), flops=100_000)(q_part)[0]
    merged = local(merge_kernel, (DP, ROWS, SPAN), scalars=1, inputs=2, room=60)(
        t, gradient, feedback
    )[0]
    merged = exchange(merged, "dp")
    factor = local(factor_kernel, (DP, HALF + 8, LANES), inputs=2)(merged, q_part)[0]
    factor = exchange(factor, "dp")
    parts = local(project_kernel, (HALF + 2 * ROWS, LANES), scalars=3)(core, chip, t, factor)[0]
    parts = gather_lines(parts)
    own = local(solve_kernel, (CHIPS, 2 * ROWS + 8, LANES), scalars=1)(t, parts)[0]
    own = exchange(own, "dp", chips)
    other = swap_cores(own)
    shapes = (feedback.shape, momentum.shape, q_previous.shape)
    scratch = [
        pltpu.VMEM((TP, ROWS, SPAN), jnp.float32),
        pltpu.VMEM((TP, ROWS, SPAN), jnp.float32),
        pltpu.VMEM((RANK, SPAN), jnp.float32),
        pltpu.SemaphoreType.DMA((3, TP)),
    ]
    outs = local(
        finish_own_kernel, *shapes, scalars=1, inputs=4, scratch=scratch, far_out=True
    )(half, gradient, feedback, momentum, own)
    outs = local(
        finish_other_kernel,
        *shapes,
        scalars=1,
        inputs=7,
        scratch=scratch,
        far=(4, 5, 6),
        far_out=True,
        alias={5: 0, 6: 1, 7: 2},
    )(1 - half, gradient, feedback, momentum, other, *outs)
    return tuple(outs)


def solution(mesh):
    placed = (
        P("dp", "tensor", None),
        P("dp", "tensor", None),
        P("tensor", None),
        P(None, "tensor"),
    )
    return jax.shard_map(
        on_device,
        mesh=mesh,
        in_specs=placed,
        out_specs=(P("dp", "tensor", None), P("tensor", None), P(None, "tensor")),
        check_vma=False,
    )
```

```python
import functools

import jax
import jax.numpy as jnp
from jax import lax
from jax.experimental import pallas as pl
from jax.experimental.pallas import tpu as pltpu
from jax.sharding import PartitionSpec as P

BETA = 0.9
HIGH = lax.Precision.HIGHEST

DP = 32
TP = 16
ROWS = 32
RANK = 64
LANES = 128
BLOCK = 16
GROUP = LANES // BLOCK
SPAN = BLOCK * TP
SHARD = DP * BLOCK
CHIPS = DP // 2
HALF = ROWS // 2


def dot(left, right, left_dim, right_dim):
    return lax.dot_general(
        left,
        right,
        (((left_dim,), (right_dim,)), ((), ())),
        precision=HIGH,
        preferred_element_type=jnp.float32,
    )


def swap_blocks(parts):
    parts = list(parts)
    block = lax.broadcasted_iota(jnp.int32, parts[0].shape, 1) // BLOCK
    for step in (1, 2, 4):
        upper = (block & step) != 0
        for i in range(GROUP):
            if i & step:
                continue
            a, b = parts[i], parts[i | step]
            parts[i] = jnp.where(upper, pltpu.roll(b, step * BLOCK, 1), a)
            parts[i | step] = jnp.where(upper, b, pltpu.roll(a, LANES - step * BLOCK, 1))
    return parts


def merge_blocks(parts):
    block = lax.broadcasted_iota(jnp.int32, parts[0].shape, 1) // BLOCK
    at = [block == place for place in range(GROUP)]
    merged = []
    for tl in range(GROUP):
        part = parts[(GROUP - tl) % GROUP]
        for place in range(1, GROUP):
            part = jnp.where(at[place], parts[(place - tl) % GROUP], part)
        merged.append(pltpu.roll(part, (GROUP - tl) * BLOCK, 1) if tl else part)
    return merged


def gather_blocks(matrix, lane_block):
    block = lax.broadcasted_iota(jnp.int32, (8, LANES), 1) // BLOCK
    moved = pltpu.roll(matrix, (GROUP - lane_block) % GROUP * BLOCK, 1)
    out = jnp.zeros((8, LANES), jnp.float32)
    for kh in range(GROUP):
        piece = moved[kh * 8 : (kh + 1) * 8, :]
        if kh:
            piece = pltpu.roll(piece, kh * BLOCK, 1)
        out = jnp.where(block == kh, piece, out)
    return out


def columns(shard, half):
    return pl.ds(pl.multiple_of(shard * SHARD + half * SPAN, SPAN), SPAN)


def merge_kernel(t_ref, gradient, feedback, out):
    t = t_ref[0]
    for shard in range(TP):
        for half in range(2):
            start = shard * SHARD + half * SPAN
            lanes = slice(start, start + SPAN)
            chip = (shard - t + (4 - half) * (TP // 2)) % TP
            out[chip * 2 + (half ^ (t & 1))] = (
                gradient[0, :, lanes].astype(jnp.float32) + feedback[0, :, lanes]
            )


def half_kernel(half_ref, q_ref, out):
    out[...] = jnp.where(half_ref[0] == 0, q_ref[:, :SPAN], q_ref[:, SPAN:])


def twice_kernel(q_part, out):
    out[:RANK, :] = q_part[...]
    out[RANK:, :] = q_part[...]


def factor_kernel(merged, q_twice, out):
    total = merged[0]
    for d in range(1, DP):
        total = total + merged[d]
    factor = dot(total, q_twice[...], 1, 1)
    lane = lax.broadcasted_iota(jnp.int32, (HALF, LANES), 1)
    packed = jnp.where(lane < RANK, factor[:HALF], factor[HALF:])
    pieces = swap_blocks(
        [
            total[g * 8 : (g + 1) * 8, h * LANES : (h + 1) * LANES]
            for h in range(2)
            for g in range(ROWS // 8)
        ]
    )
    for d in range(DP):
        out[d, :HALF, :] = packed
        out[d, HALF:, :] = pieces[d // 2 % GROUP]


def unpack_rows(packed):
    return jnp.concatenate([packed[:, :RANK], packed[:, RANK:]], axis=0)


def project_kernel(core_ref, chip_ref, t_ref, parts, out):
    half = core_ref[0] ^ (t_ref[0] & 1)
    packed = parts[0, :HALF, :]
    for d in range(1, DP):
        packed = packed + parts[d, :HALF, :]
    out[:HALF, :] = packed
    low = chip_ref[0] < GROUP
    for th in range(TP // GROUP):
        pieces = []
        for tl in range(GROUP):
            source = (th * GROUP + tl - t_ref[0] + (4 - half) * (TP // 2)) % TP
            pieces.append(parts[source * 2 + core_ref[0], HALF:, :])
        pieces = swap_blocks(pieces)
        start = HALF + th * ROWS
        for g in range(ROWS // 8):
            out[start + g * 8 : start + (g + 1) * 8, :] = jnp.where(
                low, pieces[g], pieces[g + ROWS // 8]
            )


def inverse_triangle(gram):
    size = 8
    count = RANK // size
    row = lax.broadcasted_iota(jnp.int32, (RANK, LANES), 0)
    lane = lax.broadcasted_iota(jnp.int32, (RANK, LANES), 1)
    identity = jnp.where(lane == row + RANK, 1.0, 0.0)
    work = jnp.concatenate([gram, jnp.zeros_like(gram)], axis=1) + identity
    work = [work[g * size : (g + 1) * size, :] for g in range(count)]
    row = lax.broadcasted_iota(jnp.int32, (size, LANES), 0)
    for b in range(count):
        spread = {
            g: [
                jnp.broadcast_to(work[g][:, b * size + k : b * size + k + 1], (size, LANES))
                for k in range(size)
            ]
            for g in range(b, count)
        }
        pivots = jnp.zeros((size, LANES), jnp.float32)
        for k in range(size):
            pivot_row = work[b][k : k + 1, :]
            heads = [spread[b][j][k : k + 1, :] for j in range(size)]
            pivots = jnp.where(row == k, heads[k], pivots)
            reciprocal = 1.0 / heads[k]
            for g in range(b, count):
                factor = spread[g][k] * reciprocal
                if g == b:
                    factor = jnp.where(row > k, factor, 0.0)
                work[g] = work[g] - factor * pivot_row
                for j in range(k + 1, size):
                    spread[g][j] = spread[g][j] - factor * heads[j]
        work[b] = work[b] * lax.rsqrt(pivots)
    return jnp.concatenate(work, axis=0)[:, RANK:]


def solve_kernel(chip_ref, t_ref, parts, out):
    t = t_ref[0]
    whole = unpack_rows(parts[:, :HALF, :].reshape(TP * HALF, LANES))
    whole_t = whole.T
    inverse = inverse_triangle(dot(whole_t, whole, 1, 0))
    basis = dot(unpack_rows(parts[t, :HALF, :]), inverse, 1, 1)
    tiles = []
    for th in range(TP // GROUP):
        start = HALF + th * ROWS
        halves = [parts[:, start + h * HALF : start + (h + 1) * HALF, :] for h in range(2)]
        tiles.append(
            jnp.concatenate([half.reshape(TP * HALF, LANES) for half in halves], axis=0)
        )
    sums = jnp.concatenate(tiles, axis=1)
    q_tile = dot(inverse, dot(whole_t, sums, 1, 0), 1, 0) * (1.0 / DP)
    approx = dot(basis, q_tile, 1, 0)
    mine = jnp.where(t // GROUP == 0, q_tile[:, :LANES], q_tile[:, LANES:])
    message = jnp.concatenate(
        [approx[:, :LANES], approx[:, LANES:], gather_blocks(mine, t % GROUP)], axis=0
    )
    message = pltpu.roll(message, chip_ref[0] % GROUP * BLOCK, 1)
    for chip in range(CHIPS):
        out[chip] = message


def finish_half(half_ref, gradient, feedback, momentum, parts, outs, scratch, sems):
    half = half_ref[0]
    new_feedback, new_momentum, q_out = outs
    feedback_part, momentum_part, q_part = scratch
    for group in range(CHIPS // GROUP):
        chips = range(group * GROUP, (group + 1) * GROUP)
        chunks = merge_blocks([parts[chip, 2 * ROWS :, :] for chip in chips])
        q_part[:, group * LANES : (group + 1) * LANES] = jnp.concatenate(chunks, axis=0)
    copies = [pltpu.make_async_copy(q_part, q_out.at[:, columns(0, half)], sems.at[2, 0])]
    copies[0].start()
    for th in range(TP // GROUP):
        rows = slice(th * ROWS, (th + 1) * ROWS)
        for group in range(CHIPS // GROUP):
            chips = range(group * GROUP, (group + 1) * GROUP)
            place = slice(group * LANES, (group + 1) * LANES)
            for tl, part in enumerate(merge_blocks([parts[chip, rows, :] for chip in chips])):
                shard = th * GROUP + tl
                start = shard * SHARD + half * SPAN + group * LANES
                lanes = pl.ds(pl.multiple_of(start, LANES), LANES)
                merged = gradient[0, :, lanes].astype(jnp.float32) + feedback[0, :, lanes]
                feedback_part[shard, :, place] = merged - part
                momentum_part[shard, :, place] = BETA * momentum[:, lanes] + part
        for shard in range(th * GROUP, (th + 1) * GROUP):
            lanes = columns(shard, half)
            copies += [
                pltpu.make_async_copy(
                    feedback_part.at[shard], new_feedback.at[0, :, lanes], sems.at[0, shard]
                ),
                pltpu.make_async_copy(
                    momentum_part.at[shard], new_momentum.at[:, lanes], sems.at[1, shard]
                ),
            ]
            copies[-2].start()
            copies[-1].start()
    for copy in copies:
        copy.wait()


def finish_own_kernel(half_ref, gradient, feedback, momentum, parts, *refs):
    finish_half(half_ref, gradient, feedback, momentum, parts, refs[:3], refs[3:6], refs[6])


def finish_other_kernel(half_ref, gradient, feedback, momentum, parts, *refs):
    finish_half(half_ref, gradient, feedback, momentum, parts, refs[3:6], refs[6:9], refs[9])


def local(kernel, *shapes, scalars=0, inputs=1, scratch=(), flops=100_000, far=(), far_out=False, alias=None, room=32):
    vmem, anywhere = pl.BlockSpec(memory_space=pltpu.VMEM), pl.BlockSpec(memory_space=pltpu.HBM)
    return pl.pallas_call(
        kernel,
        out_shape=[jax.ShapeDtypeStruct(shape, jnp.float32) for shape in shapes],
        in_specs=[pl.BlockSpec(memory_space=pltpu.SMEM)] * scalars
        + [anywhere if i in far else vmem for i in range(inputs)],
        out_specs=[anywhere if far_out else vmem] * len(shapes),
        scratch_shapes=list(scratch),
        input_output_aliases=alias or {},
        cost_estimate=pl.CostEstimate(flops=flops, bytes_accessed=100_000, transcendentals=0),
        compiler_params=pltpu.CompilerParams(vmem_limit_bytes=room * 1024 * 1024),
    )


def exchange(parts, axis, groups=None):
    return lax.all_to_all(parts, axis, 0, 0, tiled=True, axis_index_groups=groups)


def swap_cores(parts):
    return lax.ppermute(parts, "dp", [(d, d ^ 1) for d in range(DP)])


def fetch_shards(parts):
    pairs = []
    for d in range(DP):
        for t in range(TP):
            plane = (t + d // 2 + (d & 1 ^ t & 1) * (TP // 2)) % TP
            pairs.append((d * TP + plane, d * TP + t))
    return lax.ppermute(parts, ("dp", "tensor"), pairs)


def gather_lines(parts):
    lines = [
        [(chip * 2 + (t + v) % 2) * TP + t for t in range(TP)] for chip in range(CHIPS) for v in range(2)
    ]
    return lax.all_gather(parts, ("dp", "tensor"), axis_index_groups=lines)


def on_device(gradient, feedback, momentum, q_previous):
    d = lax.axis_index("dp").reshape(1)
    core, chip = d & 1, d >> 1
    t = lax.axis_index("tensor").reshape(1)
    chips = [list(range(c, DP, 2)) for c in range(2)]
    half = core ^ (t & 1)
    q_part = local(half_kernel, (RANK, SPAN), scalars=1)(core ^ ((t - chip) & 1), q_previous)[0]
    q_part = fetch_shards(q_part)
    q_part = local(twice_kernel, (2 * RANK, SPAN), flops=100_000)(q_part)[0]
    merged = local(merge_kernel, (DP, ROWS, SPAN), scalars=1, inputs=2, room=60)(
        t, gradient, feedback
    )[0]
    merged = exchange(merged, "dp")
    factor = local(factor_kernel, (DP, HALF + 8, LANES), inputs=2)(merged, q_part)[0]
    factor = exchange(factor, "dp")
    parts = local(project_kernel, (HALF + 2 * ROWS, LANES), scalars=3)(core, chip, t, factor)[0]
    parts = gather_lines(parts)
    own = local(solve_kernel, (CHIPS, 2 * ROWS + 8, LANES), scalars=2)(chip, t, parts)[0]
    own = exchange(own, "dp", chips)
    other = swap_cores(own)
    shapes = (feedback.shape, momentum.shape, q_previous.shape)
    scratch = [
        pltpu.VMEM((TP, ROWS, SPAN), jnp.float32),
        pltpu.VMEM((TP, ROWS, SPAN), jnp.float32),
        pltpu.VMEM((RANK, SPAN), jnp.float32),
        pltpu.SemaphoreType.DMA((3, TP)),
    ]
    outs = local(
        finish_own_kernel, *shapes, scalars=1, inputs=4, scratch=scratch, far_out=True
    )(half, gradient, feedback, momentum, own)
    outs = local(
        finish_other_kernel,
        *shapes,
        scalars=1,
        inputs=7,
        scratch=scratch,
        far=(4, 5, 6),
        far_out=True,
        alias={5: 0, 6: 1, 7: 2},
    )(1 - half, gradient, feedback, momentum, other, *outs)
    return tuple(outs)


def solution(mesh):
    placed = (
        P("dp", "tensor", None),
        P("dp", "tensor", None),
        P("tensor", None),
        P(None, "tensor"),
    )
    return jax.shard_map(
        on_device,
        mesh=mesh,
        in_specs=placed,
        out_specs=(P("dp", "tensor", None), P("tensor", None), P(None, "tensor")),
        check_vma=False,
    )
```

```python
import functools

import jax
import jax.numpy as jnp
from jax import lax
from jax.experimental import pallas as pl
from jax.experimental.pallas import tpu as pltpu
from jax.sharding import PartitionSpec as P

BETA = 0.9
HIGH = lax.Precision.HIGHEST

DP = 32
TP = 16
ROWS = 32
RANK = 64
LANES = 128
BLOCK = 16
GROUP = LANES // BLOCK
SPAN = BLOCK * TP
SHARD = DP * BLOCK
CHIPS = DP // 2
HALF = ROWS // 2


def dot(left, right, left_dim, right_dim):
    return lax.dot_general(
        left,
        right,
        (((left_dim,), (right_dim,)), ((), ())),
        precision=HIGH,
        preferred_element_type=jnp.float32,
    )


def swap_blocks(parts):
    parts = list(parts)
    block = lax.broadcasted_iota(jnp.int32, parts[0].shape, 1) // BLOCK
    for step in (1, 2, 4):
        upper = (block & step) != 0
        for i in range(GROUP):
            if i & step:
                continue
            a, b = parts[i], parts[i | step]
            parts[i] = jnp.where(upper, pltpu.roll(b, step * BLOCK, 1), a)
            parts[i | step] = jnp.where(upper, b, pltpu.roll(a, LANES - step * BLOCK, 1))
    return parts


def merge_blocks(parts):
    block = lax.broadcasted_iota(jnp.int32, parts[0].shape, 1) // BLOCK
    at = [block == place for place in range(GROUP)]
    merged = []
    for tl in range(GROUP):
        part = parts[(GROUP - tl) % GROUP]
        for place in range(1, GROUP):
            part = jnp.where(at[place], parts[(place - tl) % GROUP], part)
        merged.append(pltpu.roll(part, (GROUP - tl) * BLOCK, 1) if tl else part)
    return merged


def gather_blocks(matrix, lane_block):
    block = lax.broadcasted_iota(jnp.int32, (8, LANES), 1) // BLOCK
    moved = pltpu.roll(matrix, (GROUP - lane_block) % GROUP * BLOCK, 1)
    out = jnp.zeros((8, LANES), jnp.float32)
    for kh in range(GROUP):
        piece = moved[kh * 8 : (kh + 1) * 8, :]
        if kh:
            piece = pltpu.roll(piece, kh * BLOCK, 1)
        out = jnp.where(block == kh, piece, out)
    return out


def columns(shard, half):
    return pl.ds(pl.multiple_of(shard * SHARD + half * SPAN, SPAN), SPAN)


def merge_kernel(t_ref, gradient, feedback, out):
    t = t_ref[0]
    for shard in range(TP):
        for half in range(2):
            start = shard * SHARD + half * SPAN
            lanes = slice(start, start + SPAN)
            chip = (shard - t + (4 - half) * (TP // 2)) % TP
            out[chip * 2 + (half ^ (t & 1))] = (
                gradient[0, :, lanes].astype(jnp.float32) + feedback[0, :, lanes]
            )


def half_kernel(half_ref, q_ref, out):
    out[...] = jnp.where(half_ref[0] == 0, q_ref[:, :SPAN], q_ref[:, SPAN:])


def twice_kernel(q_part, out):
    out[:RANK, :] = q_part[...]
    out[RANK:, :] = q_part[...]


def factor_kernel(merged, q_twice, out):
    total = merged[0]
    for d in range(1, DP):
        total = total + merged[d]
    factor = dot(total, q_twice[...], 1, 1)
    lane = lax.broadcasted_iota(jnp.int32, (HALF, LANES), 1)
    packed = jnp.where(lane < RANK, factor[:HALF], factor[HALF:])
    pieces = swap_blocks(
        [
            total[g * 8 : (g + 1) * 8, h * LANES : (h + 1) * LANES]
            for h in range(2)
            for g in range(ROWS // 8)
        ]
    )
    for d in range(DP):
        out[d, :HALF, :] = packed
        out[d, HALF:, :] = pieces[d // 2 % GROUP]


def unpack_rows(packed):
    return jnp.concatenate([packed[:, :RANK], packed[:, RANK:]], axis=0)


def project_kernel(core_ref, chip_ref, t_ref, parts, out):
    half = core_ref[0] ^ (t_ref[0] & 1)
    packed = parts[0, :HALF, :]
    for d in range(1, DP):
        packed = packed + parts[d, :HALF, :]
    out[:HALF, :] = packed
    low = chip_ref[0] < GROUP
    for th in range(TP // GROUP):
        pieces = []
        for tl in range(GROUP):
            source = (th * GROUP + tl - t_ref[0] + (4 - half) * (TP // 2)) % TP
            pieces.append(parts[source * 2 + core_ref[0], HALF:, :])
        pieces = swap_blocks(pieces)
        start = HALF + th * ROWS
        for g in range(ROWS // 8):
            out[start + g * 8 : start + (g + 1) * 8, :] = jnp.where(
                low, pieces[g], pieces[g + ROWS // 8]
            )


def inverse_triangle(gram):
    size = 8
    count = RANK // size
    row = lax.broadcasted_iota(jnp.int32, (RANK, LANES), 0)
    lane = lax.broadcasted_iota(jnp.int32, (RANK, LANES), 1)
    identity = jnp.where(lane == row + RANK, 1.0, 0.0)
    work = jnp.concatenate([gram, jnp.zeros_like(gram)], axis=1) + identity
    work = [work[g * size : (g + 1) * size, :] for g in range(count)]
    row = lax.broadcasted_iota(jnp.int32, (size, LANES), 0)
    for b in range(count):
        spread = {
            g: [
                jnp.broadcast_to(work[g][:, b * size + k : b * size + k + 1], (size, LANES))
                for k in range(size)
            ]
            for g in range(b, count)
        }
        pivots = jnp.zeros((size, LANES), jnp.float32)
        for k in range(size):
            pivot_row = work[b][k : k + 1, :]
            heads = [spread[b][j][k : k + 1, :] for j in range(size)]
            pivots = jnp.where(row == k, heads[k], pivots)
            reciprocal = 1.0 / heads[k]
            for g in range(b, count):
                factor = spread[g][k] * reciprocal
                if g == b:
                    factor = jnp.where(row > k, factor, 0.0)
                work[g] = work[g] - factor * pivot_row
                for j in range(k + 1, size):
                    spread[g][j] = spread[g][j] - factor * heads[j]
        work[b] = work[b] * lax.rsqrt(pivots)
    return jnp.concatenate(work, axis=0)[:, RANK:]


def solve_kernel(chip_ref, t_ref, parts, out):
    t = t_ref[0]
    whole = unpack_rows(parts[:, :HALF, :].reshape(TP * HALF, LANES))
    whole_t = whole.T
    inverse = inverse_triangle(dot(whole_t, whole, 1, 0))
    basis = dot(unpack_rows(parts[t, :HALF, :]), inverse, 1, 1)
    tiles = []
    for th in range(TP // GROUP):
        start = HALF + th * ROWS
        halves = [parts[:, start + h * HALF : start + (h + 1) * HALF, :] for h in range(2)]
        tiles.append(
            jnp.concatenate([half.reshape(TP * HALF, LANES) for half in halves], axis=0)
        )
    sums = jnp.concatenate(tiles, axis=1)
    q_tile = dot(inverse, dot(whole_t, sums, 1, 0), 1, 0) * (1.0 / DP)
    approx = dot(basis, q_tile, 1, 0)
    mine = jnp.where(t // GROUP == 0, q_tile[:, :LANES], q_tile[:, LANES:])
    message = jnp.concatenate(
        [approx[:, :LANES], approx[:, LANES:], gather_blocks(mine, t % GROUP)], axis=0
    )
    message = pltpu.roll(message, chip_ref[0] % GROUP * BLOCK, 1)
    for chip in range(CHIPS):
        out[chip] = message


def finish_half(half_ref, gradient, feedback, momentum, parts, outs, scratch, sems):
    half = half_ref[0]
    new_feedback, new_momentum, q_out = outs
    feedback_part, momentum_part, q_part = scratch
    for group in range(CHIPS // GROUP):
        chips = range(group * GROUP, (group + 1) * GROUP)
        chunks = merge_blocks([parts[chip, 2 * ROWS :, :] for chip in chips])
        q_part[:, group * LANES : (group + 1) * LANES] = jnp.concatenate(chunks, axis=0)
    copies = [pltpu.make_async_copy(q_part, q_out.at[:, columns(0, half)], sems.at[2, 0])]
    copies[0].start()
    for th in range(TP // GROUP):
        rows = slice(th * ROWS, (th + 1) * ROWS)
        for group in range(CHIPS // GROUP):
            chips = range(group * GROUP, (group + 1) * GROUP)
            place = slice(group * LANES, (group + 1) * LANES)
            for tl, part in enumerate(merge_blocks([parts[chip, rows, :] for chip in chips])):
                shard = th * GROUP + tl
                start = shard * SHARD + half * SPAN + group * LANES
                lanes = pl.ds(pl.multiple_of(start, LANES), LANES)
                merged = gradient[0, :, lanes].astype(jnp.float32) + feedback[0, :, lanes]
                feedback_part[shard, :, place] = merged - part
                momentum_part[shard, :, place] = BETA * momentum[:, lanes] + part
        for shard in range(th * GROUP, (th + 1) * GROUP):
            lanes = columns(shard, half)
            copies += [
                pltpu.make_async_copy(
                    feedback_part.at[shard], new_feedback.at[0, :, lanes], sems.at[0, shard]
                ),
                pltpu.make_async_copy(
                    momentum_part.at[shard], new_momentum.at[:, lanes], sems.at[1, shard]
                ),
            ]
            copies[-2].start()
            copies[-1].start()
    for copy in copies:
        copy.wait()


def finish_own_kernel(half_ref, gradient, feedback, momentum, parts, *refs):
    finish_half(half_ref, gradient, feedback, momentum, parts, refs[:3], refs[3:6], refs[6])


def finish_other_kernel(half_ref, gradient, feedback, momentum, parts, *refs):
    finish_half(half_ref, gradient, feedback, momentum, parts, refs[3:6], refs[6:9], refs[9])


def local(kernel, *shapes, scalars=0, inputs=1, scratch=(), flops=100_000, far=(), far_out=False, alias=None, room=32):
    vmem, anywhere = pl.BlockSpec(memory_space=pltpu.VMEM), pl.BlockSpec(memory_space=pltpu.HBM)
    return pl.pallas_call(
        kernel,
        out_shape=[jax.ShapeDtypeStruct(shape, jnp.float32) for shape in shapes],
        in_specs=[pl.BlockSpec(memory_space=pltpu.SMEM)] * scalars
        + [anywhere if i in far else vmem for i in range(inputs)],
        out_specs=[anywhere if far_out else vmem] * len(shapes),
        scratch_shapes=list(scratch),
        input_output_aliases=alias or {},
        cost_estimate=pl.CostEstimate(flops=flops, bytes_accessed=100_000, transcendentals=0),
        compiler_params=pltpu.CompilerParams(vmem_limit_bytes=room * 1024 * 1024),
    )


def exchange(parts, axis, groups=None):
    return lax.all_to_all(parts, axis, 0, 0, tiled=True, axis_index_groups=groups)


def swap_cores(parts):
    return lax.ppermute(parts, "dp", [(d, d ^ 1) for d in range(DP)])


def fetch_shards(parts):
    pairs = []
    for d in range(DP):
        for t in range(TP):
            plane = (t + d // 2 + (d & 1 ^ t & 1) * (TP // 2)) % TP
            pairs.append(((d ^ 1) * TP + plane, d * TP + t))
    return lax.ppermute(parts, ("dp", "tensor"), pairs)


def gather_lines(parts):
    lines = [
        [(chip * 2 + (t + v) % 2) * TP + t for t in range(TP)] for chip in range(CHIPS) for v in range(2)
    ]
    return lax.all_gather(parts, ("dp", "tensor"), axis_index_groups=lines)


def on_device(gradient, feedback, momentum, q_previous):
    d = lax.axis_index("dp").reshape(1)
    core, chip = d & 1, d >> 1
    t = lax.axis_index("tensor").reshape(1)
    chips = [list(range(c, DP, 2)) for c in range(2)]
    half = core ^ (t & 1)
    q_part = local(half_kernel, (RANK, SPAN), scalars=1)(core ^ ((t - chip + 1) & 1), q_previous)[0]
    q_part = fetch_shards(q_part)
    q_part = local(twice_kernel, (2 * RANK, SPAN), flops=100_000)(q_part)[0]
    merged = local(merge_kernel, (DP, ROWS, SPAN), scalars=1, inputs=2, room=60)(
        t, gradient, feedback
    )[0]
    merged = exchange(merged, "dp")
    factor = local(factor_kernel, (DP, HALF + 8, LANES), inputs=2)(merged, q_part)[0]
    factor = exchange(factor, "dp")
    parts = local(project_kernel, (HALF + 2 * ROWS, LANES), scalars=3)(core, chip, t, factor)[0]
    parts = gather_lines(parts)
    own = local(solve_kernel, (CHIPS, 2 * ROWS + 8, LANES), scalars=2)(chip, t, parts)[0]
    own = exchange(own, "dp", chips)
    other = swap_cores(own)
    shapes = (feedback.shape, momentum.shape, q_previous.shape)
    scratch = [
        pltpu.VMEM((TP, ROWS, SPAN), jnp.float32),
        pltpu.VMEM((TP, ROWS, SPAN), jnp.float32),
        pltpu.VMEM((RANK, SPAN), jnp.float32),
        pltpu.SemaphoreType.DMA((3, TP)),
    ]
    outs = local(
        finish_own_kernel, *shapes, scalars=1, inputs=4, scratch=scratch, far_out=True
    )(half, gradient, feedback, momentum, own)
    outs = local(
        finish_other_kernel,
        *shapes,
        scalars=1,
        inputs=7,
        scratch=scratch,
        far=(4, 5, 6),
        far_out=True,
        alias={5: 0, 6: 1, 7: 2},
    )(1 - half, gradient, feedback, momentum, other, *outs)
    return tuple(outs)


def solution(mesh):
    placed = (
        P("dp", "tensor", None),
        P("dp", "tensor", None),
        P("tensor", None),
        P(None, "tensor"),
    )
    return jax.shard_map(
        on_device,
        mesh=mesh,
        in_specs=placed,
        out_specs=(P("dp", "tensor", None), P("tensor", None), P(None, "tensor")),
        check_vma=False,
    )
```

```python
import functools

import jax
import jax.numpy as jnp
from jax import lax
from jax.experimental import pallas as pl
from jax.experimental.pallas import tpu as pltpu
from jax.sharding import PartitionSpec as P

BETA = 0.9
HIGH = lax.Precision.HIGHEST

DP = 32
TP = 16
ROWS = 32
RANK = 64
LANES = 128
BLOCK = 16
GROUP = LANES // BLOCK
SPAN = BLOCK * TP
SHARD = DP * BLOCK
CHIPS = DP // 2
HALF = ROWS // 2
PART = ROWS // GROUP


def dot(left, right, left_dim, right_dim):
    return lax.dot_general(
        left,
        right,
        (((left_dim,), (right_dim,)), ((), ())),
        precision=HIGH,
        preferred_element_type=jnp.float32,
    )


def swap_blocks(parts):
    parts = list(parts)
    block = lax.broadcasted_iota(jnp.int32, parts[0].shape, 1) // BLOCK
    for step in (1, 2, 4):
        upper = (block & step) != 0
        for i in range(GROUP):
            if i & step:
                continue
            a, b = parts[i], parts[i | step]
            parts[i] = jnp.where(upper, pltpu.roll(b, step * BLOCK, 1), a)
            parts[i | step] = jnp.where(upper, b, pltpu.roll(a, LANES - step * BLOCK, 1))
    return parts


def merge_blocks(parts):
    block = lax.broadcasted_iota(jnp.int32, parts[0].shape, 1) // BLOCK
    at = [block == place for place in range(GROUP)]
    merged = []
    for tl in range(GROUP):
        part = parts[(GROUP - tl) % GROUP]
        for place in range(1, GROUP):
            part = jnp.where(at[place], parts[(place - tl) % GROUP], part)
        merged.append(pltpu.roll(part, (GROUP - tl) * BLOCK, 1) if tl else part)
    return merged


def gather_blocks(matrix, lane_block):
    block = lax.broadcasted_iota(jnp.int32, (8, LANES), 1) // BLOCK
    moved = pltpu.roll(matrix, (GROUP - lane_block) % GROUP * BLOCK, 1)
    out = jnp.zeros((8, LANES), jnp.float32)
    for kh in range(GROUP):
        piece = moved[kh * 8 : (kh + 1) * 8, :]
        if kh:
            piece = pltpu.roll(piece, kh * BLOCK, 1)
        out = jnp.where(block == kh, piece, out)
    return out


def columns(shard, half):
    return pl.ds(pl.multiple_of(shard * SHARD + half * SPAN, SPAN), SPAN)


def merge_kernel(t_ref, gradient, feedback, out):
    t = t_ref[0]
    for shard in range(TP):
        for half in range(2):
            start = shard * SHARD + half * SPAN
            lanes = slice(start, start + SPAN)
            chip = (shard - t + (4 - half) * (TP // 2)) % TP
            out[chip * 2 + (half ^ (t & 1))] = (
                gradient[0, :, lanes].astype(jnp.float32) + feedback[0, :, lanes]
            )


def half_kernel(half_ref, q_ref, out):
    out[...] = jnp.where(half_ref[0] == 0, q_ref[:, :SPAN], q_ref[:, SPAN:])


def twice_kernel(q_part, out):
    out[:RANK, :] = q_part[...]
    out[RANK:, :] = q_part[...]


def factor_kernel(merged, q_twice, out):
    total = merged[0]
    for d in range(1, DP):
        total = total + merged[d]
    factor = dot(total, q_twice[...], 1, 1)
    lane = lax.broadcasted_iota(jnp.int32, (HALF, LANES), 1)
    packed = jnp.where(lane < RANK, factor[:HALF], factor[HALF:])
    pieces = []
    for h in range(2):
        lanes = slice(h * LANES, (h + 1) * LANES)
        pieces += swap_blocks([total[g * PART : (g + 1) * PART, lanes] for g in range(GROUP)])
    for d in range(DP):
        for i in range(HALF // PART):
            out[d, i] = packed[i * PART : (i + 1) * PART]
        out[d, HALF // PART] = pieces[d // 2]


def unpack_rows(packed):
    return jnp.concatenate([packed[:, :RANK], packed[:, RANK:]], axis=0)


def project_kernel(core_ref, t_ref, parts, out):
    half = core_ref[0] ^ (t_ref[0] & 1)
    for i in range(HALF // PART):
        packed = parts[0, i]
        for d in range(1, DP):
            packed = packed + parts[d, i]
        out[i * PART : (i + 1) * PART, :] = packed
    for th in range(TP // GROUP):
        pieces = []
        for tl in range(GROUP):
            source = (th * GROUP + tl - t_ref[0] + (4 - half) * (TP // 2)) % TP
            pieces.append(parts[source * 2 + core_ref[0], HALF // PART])
        for g, piece in enumerate(swap_blocks(pieces)):
            start = HALF + th * ROWS + g * PART
            out[start : start + PART, :] = piece


def inverse_triangle(gram):
    size = 8
    count = RANK // size
    row = lax.broadcasted_iota(jnp.int32, (RANK, LANES), 0)
    lane = lax.broadcasted_iota(jnp.int32, (RANK, LANES), 1)
    identity = jnp.where(lane == row + RANK, 1.0, 0.0)
    work = jnp.concatenate([gram, jnp.zeros_like(gram)], axis=1) + identity
    work = [work[g * size : (g + 1) * size, :] for g in range(count)]
    row = lax.broadcasted_iota(jnp.int32, (size, LANES), 0)
    for b in range(count):
        spread = {
            g: [
                jnp.broadcast_to(work[g][:, b * size + k : b * size + k + 1], (size, LANES))
                for k in range(size)
            ]
            for g in range(b, count)
        }
        pivots = jnp.zeros((size, LANES), jnp.float32)
        for k in range(size):
            pivot_row = work[b][k : k + 1, :]
            heads = [spread[b][j][k : k + 1, :] for j in range(size)]
            pivots = jnp.where(row == k, heads[k], pivots)
            reciprocal = 1.0 / heads[k]
            for g in range(b, count):
                factor = spread[g][k] * reciprocal
                if g == b:
                    factor = jnp.where(row > k, factor, 0.0)
                work[g] = work[g] - factor * pivot_row
                for j in range(k + 1, size):
                    spread[g][j] = spread[g][j] - factor * heads[j]
        work[b] = work[b] * lax.rsqrt(pivots)
    return jnp.concatenate(work, axis=0)[:, RANK:]


def solve_kernel(chip_ref, t_ref, parts, out):
    t = t_ref[0]
    whole = unpack_rows(parts[:, :HALF, :].reshape(TP * HALF, LANES))
    whole_t = whole.T
    inverse = inverse_triangle(dot(whole_t, whole, 1, 0))
    basis = dot(unpack_rows(parts[t, :HALF, :]), inverse, 1, 1)
    tiles = []
    for th in range(TP // GROUP):
        start = HALF + th * ROWS
        halves = [parts[:, start + h * HALF : start + (h + 1) * HALF, :] for h in range(2)]
        tiles.append(
            jnp.concatenate([half.reshape(TP * HALF, LANES) for half in halves], axis=0)
        )
    sums = jnp.concatenate(tiles, axis=1)
    q_tile = dot(inverse, dot(whole_t, sums, 1, 0), 1, 0) * (1.0 / DP)
    approx = dot(basis, q_tile, 1, 0)
    mine = jnp.where(t // GROUP == 0, q_tile[:, :LANES], q_tile[:, LANES:])
    message = jnp.concatenate(
        [approx[:, :LANES], approx[:, LANES:], gather_blocks(mine, t % GROUP)], axis=0
    )
    message = pltpu.roll(message, chip_ref[0] % GROUP * BLOCK, 1)
    for chip in range(CHIPS):
        out[chip] = message


def finish_half(half_ref, gradient, feedback, momentum, parts, outs, scratch, sems):
    half = half_ref[0]
    new_feedback, new_momentum, q_out = outs
    feedback_part, momentum_part, q_part = scratch
    for group in range(CHIPS // GROUP):
        chips = range(group * GROUP, (group + 1) * GROUP)
        chunks = merge_blocks([parts[chip, 2 * ROWS :, :] for chip in chips])
        q_part[:, group * LANES : (group + 1) * LANES] = jnp.concatenate(chunks, axis=0)
    copies = [pltpu.make_async_copy(q_part, q_out.at[:, columns(0, half)], sems.at[2, 0])]
    copies[0].start()
    for th in range(TP // GROUP):
        rows = slice(th * ROWS, (th + 1) * ROWS)
        for group in range(CHIPS // GROUP):
            chips = range(group * GROUP, (group + 1) * GROUP)
            place = slice(group * LANES, (group + 1) * LANES)
            for tl, part in enumerate(merge_blocks([parts[chip, rows, :] for chip in chips])):
                shard = th * GROUP + tl
                start = shard * SHARD + half * SPAN + group * LANES
                lanes = pl.ds(pl.multiple_of(start, LANES), LANES)
                merged = gradient[0, :, lanes].astype(jnp.float32) + feedback[0, :, lanes]
                feedback_part[shard, :, place] = merged - part
                momentum_part[shard, :, place] = BETA * momentum[:, lanes] + part
        for shard in range(th * GROUP, (th + 1) * GROUP):
            lanes = columns(shard, half)
            copies += [
                pltpu.make_async_copy(
                    feedback_part.at[shard], new_feedback.at[0, :, lanes], sems.at[0, shard]
                ),
                pltpu.make_async_copy(
                    momentum_part.at[shard], new_momentum.at[:, lanes], sems.at[1, shard]
                ),
            ]
            copies[-2].start()
            copies[-1].start()
    for copy in copies:
        copy.wait()


def finish_own_kernel(half_ref, gradient, feedback, momentum, parts, *refs):
    finish_half(half_ref, gradient, feedback, momentum, parts, refs[:3], refs[3:6], refs[6])


def finish_other_kernel(half_ref, gradient, feedback, momentum, parts, *refs):
    finish_half(half_ref, gradient, feedback, momentum, parts, refs[3:6], refs[6:9], refs[9])


def local(kernel, *shapes, scalars=0, inputs=1, scratch=(), flops=100_000, far=(), far_out=False, alias=None, room=32):
    vmem, anywhere = pl.BlockSpec(memory_space=pltpu.VMEM), pl.BlockSpec(memory_space=pltpu.HBM)
    return pl.pallas_call(
        kernel,
        out_shape=[jax.ShapeDtypeStruct(shape, jnp.float32) for shape in shapes],
        in_specs=[pl.BlockSpec(memory_space=pltpu.SMEM)] * scalars
        + [anywhere if i in far else vmem for i in range(inputs)],
        out_specs=[anywhere if far_out else vmem] * len(shapes),
        scratch_shapes=list(scratch),
        input_output_aliases=alias or {},
        cost_estimate=pl.CostEstimate(flops=flops, bytes_accessed=100_000, transcendentals=0),
        compiler_params=pltpu.CompilerParams(vmem_limit_bytes=room * 1024 * 1024),
    )


def exchange(parts, axis, groups=None):
    return lax.all_to_all(parts, axis, 0, 0, tiled=True, axis_index_groups=groups)


def swap_cores(parts):
    return lax.ppermute(parts, "dp", [(d, d ^ 1) for d in range(DP)])


def fetch_shards(parts):
    pairs = []
    for d in range(DP):
        for t in range(TP):
            plane = (t + d // 2 + (d & 1 ^ t & 1) * (TP // 2)) % TP
            pairs.append(((d ^ 1) * TP + plane, d * TP + t))
    return lax.ppermute(parts, ("dp", "tensor"), pairs)


def gather_lines(parts):
    lines = [
        [(chip * 2 + (t + v) % 2) * TP + t for t in range(TP)] for chip in range(CHIPS) for v in range(2)
    ]
    return lax.all_gather(parts, ("dp", "tensor"), axis_index_groups=lines)


def on_device(gradient, feedback, momentum, q_previous):
    d = lax.axis_index("dp").reshape(1)
    core, chip = d & 1, d >> 1
    t = lax.axis_index("tensor").reshape(1)
    chips = [list(range(c, DP, 2)) for c in range(2)]
    half = core ^ (t & 1)
    q_part = local(half_kernel, (RANK, SPAN), scalars=1)(core ^ ((t - chip + 1) & 1), q_previous)[0]
    q_part = fetch_shards(q_part)
    q_part = local(twice_kernel, (2 * RANK, SPAN), flops=100_000)(q_part)[0]
    merged = local(merge_kernel, (DP, ROWS, SPAN), scalars=1, inputs=2, room=60)(
        t, gradient, feedback
    )[0]
    merged = exchange(merged, "dp")
    factor = local(factor_kernel, (DP, HALF // PART + 1, PART, LANES), inputs=2)(merged, q_part)[0]
    factor = exchange(factor, "dp")
    parts = local(project_kernel, (HALF + 2 * ROWS, LANES), scalars=2)(core, t, factor)[0]
    parts = gather_lines(parts)
    own = local(solve_kernel, (CHIPS, 2 * ROWS + 8, LANES), scalars=2)(chip, t, parts)[0]
    own = exchange(own, "dp", chips)
    other = swap_cores(own)
    shapes = (feedback.shape, momentum.shape, q_previous.shape)
    scratch = [
        pltpu.VMEM((TP, ROWS, SPAN), jnp.float32),
        pltpu.VMEM((TP, ROWS, SPAN), jnp.float32),
        pltpu.VMEM((RANK, SPAN), jnp.float32),
        pltpu.SemaphoreType.DMA((3, TP)),
    ]
    outs = local(
        finish_own_kernel, *shapes, scalars=1, inputs=4, scratch=scratch, far_out=True
    )(half, gradient, feedback, momentum, own)
    outs = local(
        finish_other_kernel,
        *shapes,
        scalars=1,
        inputs=7,
        scratch=scratch,
        far=(4, 5, 6),
        far_out=True,
        alias={5: 0, 6: 1, 7: 2},
    )(1 - half, gradient, feedback, momentum, other, *outs)
    return tuple(outs)


def solution(mesh):
    placed = (
        P("dp", "tensor", None),
        P("dp", "tensor", None),
        P("tensor", None),
        P(None, "tensor"),
    )
    return jax.shard_map(
        on_device,
        mesh=mesh,
        in_specs=placed,
        out_specs=(P("dp", "tensor", None), P("tensor", None), P(None, "tensor")),
        check_vma=False,
    )
```

```python
import functools

import jax
import jax.numpy as jnp
from jax import lax
from jax.experimental import pallas as pl
from jax.experimental.pallas import tpu as pltpu
from jax.sharding import PartitionSpec as P

BETA = 0.9
HIGH = lax.Precision.HIGHEST

DP = 32
TP = 16
ROWS = 32
RANK = 64
LANES = 128
BLOCK = 16
GROUP = LANES // BLOCK
SPAN = BLOCK * TP
SHARD = DP * BLOCK
CHIPS = DP // 2
HALF = ROWS // 2
PART = ROWS // GROUP


def dot(left, right, left_dim, right_dim):
    return lax.dot_general(
        left,
        right,
        (((left_dim,), (right_dim,)), ((), ())),
        precision=HIGH,
        preferred_element_type=jnp.float32,
    )


def swap_blocks(parts):
    parts = list(parts)
    block = lax.broadcasted_iota(jnp.int32, parts[0].shape, 1) // BLOCK
    for step in (1, 2, 4):
        upper = (block & step) != 0
        for i in range(GROUP):
            if i & step:
                continue
            a, b = parts[i], parts[i | step]
            parts[i] = jnp.where(upper, pltpu.roll(b, step * BLOCK, 1), a)
            parts[i | step] = jnp.where(upper, b, pltpu.roll(a, LANES - step * BLOCK, 1))
    return parts


def merge_blocks(parts):
    block = lax.broadcasted_iota(jnp.int32, parts[0].shape, 1) // BLOCK
    at = [block == place for place in range(GROUP)]
    merged = []
    for tl in range(GROUP):
        part = parts[(GROUP - tl) % GROUP]
        for place in range(1, GROUP):
            part = jnp.where(at[place], parts[(place - tl) % GROUP], part)
        merged.append(pltpu.roll(part, (GROUP - tl) * BLOCK, 1) if tl else part)
    return merged


def gather_blocks(matrix, lane_block):
    block = lax.broadcasted_iota(jnp.int32, (8, LANES), 1) // BLOCK
    moved = pltpu.roll(matrix, (GROUP - lane_block) % GROUP * BLOCK, 1)
    out = jnp.zeros((8, LANES), jnp.float32)
    for kh in range(GROUP):
        piece = moved[kh * 8 : (kh + 1) * 8, :]
        if kh:
            piece = pltpu.roll(piece, kh * BLOCK, 1)
        out = jnp.where(block == kh, piece, out)
    return out


def columns(shard, half):
    return pl.ds(pl.multiple_of(shard * SHARD + half * SPAN, SPAN), SPAN)


def merge_kernel(t_ref, gradient, feedback, out):
    t = t_ref[0]
    for shard in range(TP):
        for half in range(2):
            start = shard * SHARD + half * SPAN
            lanes = slice(start, start + SPAN)
            chip = (shard - t + (4 - half) * (TP // 2)) % TP
            out[chip * 2 + (half ^ (t & 1))] = (
                gradient[0, :, lanes].astype(jnp.float32) + feedback[0, :, lanes]
            )


def half_kernel(half_ref, q_ref, out):
    out[...] = jnp.where(half_ref[0] == 0, q_ref[:, :SPAN], q_ref[:, SPAN:])


def factor_kernel(merged, q_part, out):
    total = merged[0]
    for d in range(1, DP):
        total = total + merged[d]
    q_twice = jnp.concatenate([q_part[...], q_part[...]], axis=0)
    factor = dot(total, q_twice, 1, 1)
    lane = lax.broadcasted_iota(jnp.int32, (HALF, LANES), 1)
    packed = jnp.where(lane < RANK, factor[:HALF], factor[HALF:])
    pieces = []
    for h in range(2):
        lanes = slice(h * LANES, (h + 1) * LANES)
        pieces += swap_blocks([total[g * PART : (g + 1) * PART, lanes] for g in range(GROUP)])
    for d in range(DP):
        for i in range(HALF // PART):
            out[d, i] = packed[i * PART : (i + 1) * PART]
        out[d, HALF // PART] = pieces[d // 2]


def unpack_rows(packed):
    return jnp.concatenate([packed[:, :RANK], packed[:, RANK:]], axis=0)


def project_kernel(core_ref, t_ref, parts, out):
    half = core_ref[0] ^ (t_ref[0] & 1)
    for i in range(HALF // PART):
        packed = parts[0, i]
        for d in range(1, DP):
            packed = packed + parts[d, i]
        out[i * PART : (i + 1) * PART, :] = packed
    for th in range(TP // GROUP):
        pieces = []
        for tl in range(GROUP):
            source = (th * GROUP + tl - t_ref[0] + (4 - half) * (TP // 2)) % TP
            pieces.append(parts[source * 2 + core_ref[0], HALF // PART])
        for g, piece in enumerate(swap_blocks(pieces)):
            start = HALF + th * ROWS + g * PART
            out[start : start + PART, :] = piece


def inverse_triangle(gram):
    size = 8
    count = RANK // size
    row = lax.broadcasted_iota(jnp.int32, (RANK, LANES), 0)
    lane = lax.broadcasted_iota(jnp.int32, (RANK, LANES), 1)
    identity = jnp.where(lane == row + RANK, 1.0, 0.0)
    work = jnp.concatenate([gram, jnp.zeros_like(gram)], axis=1) + identity
    work = [work[g * size : (g + 1) * size, :] for g in range(count)]
    row = lax.broadcasted_iota(jnp.int32, (size, LANES), 0)
    for b in range(count):
        spread = {
            g: [
                jnp.broadcast_to(work[g][:, b * size + k : b * size + k + 1], (size, LANES))
                for k in range(size)
            ]
            for g in range(b, count)
        }
        pivots = jnp.zeros((size, LANES), jnp.float32)
        for k in range(size):
            pivot_row = work[b][k : k + 1, :]
            heads = [spread[b][j][k : k + 1, :] for j in range(size)]
            pivots = jnp.where(row == k, heads[k], pivots)
            reciprocal = 1.0 / heads[k]
            for g in range(b, count):
                factor = spread[g][k] * reciprocal
                if g == b:
                    factor = jnp.where(row > k, factor, 0.0)
                work[g] = work[g] - factor * pivot_row
                for j in range(k + 1, size):
                    spread[g][j] = spread[g][j] - factor * heads[j]
        work[b] = work[b] * lax.rsqrt(pivots)
    return jnp.concatenate(work, axis=0)[:, RANK:]


def solve_kernel(chip_ref, t_ref, parts, out):
    t = t_ref[0]
    whole = unpack_rows(parts[:, :HALF, :].reshape(TP * HALF, LANES))
    whole_t = whole.T
    inverse = inverse_triangle(dot(whole_t, whole, 1, 0))
    basis = dot(unpack_rows(parts[t, :HALF, :]), inverse, 1, 1)
    tiles = []
    for th in range(TP // GROUP):
        start = HALF + th * ROWS
        halves = [parts[:, start + h * HALF : start + (h + 1) * HALF, :] for h in range(2)]
        tiles.append(
            jnp.concatenate([half.reshape(TP * HALF, LANES) for half in halves], axis=0)
        )
    sums = jnp.concatenate(tiles, axis=1)
    q_tile = dot(inverse, dot(whole_t, sums, 1, 0), 1, 0) * (1.0 / DP)
    approx = dot(basis, q_tile, 1, 0)
    mine = jnp.where(t // GROUP == 0, q_tile[:, :LANES], q_tile[:, LANES:])
    message = jnp.concatenate(
        [approx[:, :LANES], approx[:, LANES:], gather_blocks(mine, t % GROUP)], axis=0
    )
    message = pltpu.roll(message, chip_ref[0] % GROUP * BLOCK, 1)
    for chip in range(CHIPS):
        out[chip] = message


def finish_half(half_ref, gradient, feedback, momentum, parts, outs, scratch, sems):
    half = half_ref[0]
    new_feedback, new_momentum, q_out = outs
    feedback_part, momentum_part, q_part = scratch
    for group in range(CHIPS // GROUP):
        chips = range(group * GROUP, (group + 1) * GROUP)
        chunks = merge_blocks([parts[chip, 2 * ROWS :, :] for chip in chips])
        q_part[:, group * LANES : (group + 1) * LANES] = jnp.concatenate(chunks, axis=0)
    copies = [pltpu.make_async_copy(q_part, q_out.at[:, columns(0, half)], sems.at[2, 0])]
    copies[0].start()
    for th in range(TP // GROUP):
        rows = slice(th * ROWS, (th + 1) * ROWS)
        for group in range(CHIPS // GROUP):
            chips = range(group * GROUP, (group + 1) * GROUP)
            place = slice(group * LANES, (group + 1) * LANES)
            for tl, part in enumerate(merge_blocks([parts[chip, rows, :] for chip in chips])):
                shard = th * GROUP + tl
                start = shard * SHARD + half * SPAN + group * LANES
                lanes = pl.ds(pl.multiple_of(start, LANES), LANES)
                merged = gradient[0, :, lanes].astype(jnp.float32) + feedback[0, :, lanes]
                feedback_part[shard, :, place] = merged - part
                momentum_part[shard, :, place] = BETA * momentum[:, lanes] + part
        for shard in range(th * GROUP, (th + 1) * GROUP):
            lanes = columns(shard, half)
            copies += [
                pltpu.make_async_copy(
                    feedback_part.at[shard], new_feedback.at[0, :, lanes], sems.at[0, shard]
                ),
                pltpu.make_async_copy(
                    momentum_part.at[shard], new_momentum.at[:, lanes], sems.at[1, shard]
                ),
            ]
            copies[-2].start()
            copies[-1].start()
    for copy in copies:
        copy.wait()


def finish_own_kernel(half_ref, gradient, feedback, momentum, parts, *refs):
    finish_half(half_ref, gradient, feedback, momentum, parts, refs[:3], refs[3:6], refs[6])


def finish_other_kernel(half_ref, gradient, feedback, momentum, parts, *refs):
    finish_half(half_ref, gradient, feedback, momentum, parts, refs[3:6], refs[6:9], refs[9])


def local(kernel, *shapes, scalars=0, inputs=1, scratch=(), flops=100_000, far=(), far_out=False, alias=None, room=32):
    vmem, anywhere = pl.BlockSpec(memory_space=pltpu.VMEM), pl.BlockSpec(memory_space=pltpu.HBM)
    return pl.pallas_call(
        kernel,
        out_shape=[jax.ShapeDtypeStruct(shape, jnp.float32) for shape in shapes],
        in_specs=[pl.BlockSpec(memory_space=pltpu.SMEM)] * scalars
        + [anywhere if i in far else vmem for i in range(inputs)],
        out_specs=[anywhere if far_out else vmem] * len(shapes),
        scratch_shapes=list(scratch),
        input_output_aliases=alias or {},
        cost_estimate=pl.CostEstimate(flops=flops, bytes_accessed=100_000, transcendentals=0),
        compiler_params=pltpu.CompilerParams(vmem_limit_bytes=room * 1024 * 1024),
    )


def exchange(parts, axis, groups=None):
    return lax.all_to_all(parts, axis, 0, 0, tiled=True, axis_index_groups=groups)


def swap_cores(parts):
    return lax.ppermute(parts, "dp", [(d, d ^ 1) for d in range(DP)])


def fetch_shards(parts):
    pairs = []
    for d in range(DP):
        for t in range(TP):
            plane = (t + d // 2 + (d & 1 ^ t & 1) * (TP // 2)) % TP
            pairs.append(((d ^ 1) * TP + plane, d * TP + t))
    return lax.ppermute(parts, ("dp", "tensor"), pairs)


def gather_lines(parts):
    lines = [
        [(chip * 2 + (t + v) % 2) * TP + t for t in range(TP)] for chip in range(CHIPS) for v in range(2)
    ]
    return lax.all_gather(parts, ("dp", "tensor"), axis_index_groups=lines)


def on_device(gradient, feedback, momentum, q_previous):
    d = lax.axis_index("dp").reshape(1)
    core, chip = d & 1, d >> 1
    t = lax.axis_index("tensor").reshape(1)
    chips = [list(range(c, DP, 2)) for c in range(2)]
    half = core ^ (t & 1)
    q_part = local(half_kernel, (RANK, SPAN), scalars=1)(core ^ ((t - chip + 1) & 1), q_previous)[0]
    q_part = fetch_shards(q_part)
    merged = local(merge_kernel, (DP, ROWS, SPAN), scalars=1, inputs=2, room=60)(
        t, gradient, feedback
    )[0]
    merged = exchange(merged, "dp")
    factor = local(factor_kernel, (DP, HALF // PART + 1, PART, LANES), inputs=2)(merged, q_part)[0]
    factor = exchange(factor, "dp")
    parts = local(project_kernel, (HALF + 2 * ROWS, LANES), scalars=2)(core, t, factor)[0]
    parts = gather_lines(parts)
    own = local(solve_kernel, (CHIPS, 2 * ROWS + 8, LANES), scalars=2)(chip, t, parts)[0]
    own = exchange(own, "dp", chips)
    other = swap_cores(own)
    shapes = (feedback.shape, momentum.shape, q_previous.shape)
    scratch = [
        pltpu.VMEM((TP, ROWS, SPAN), jnp.float32),
        pltpu.VMEM((TP, ROWS, SPAN), jnp.float32),
        pltpu.VMEM((RANK, SPAN), jnp.float32),
        pltpu.SemaphoreType.DMA((3, TP)),
    ]
    outs = local(
        finish_own_kernel, *shapes, scalars=1, inputs=4, scratch=scratch, far_out=True
    )(half, gradient, feedback, momentum, own)
    outs = local(
        finish_other_kernel,
        *shapes,
        scalars=1,
        inputs=7,
        scratch=scratch,
        far=(4, 5, 6),
        far_out=True,
        alias={5: 0, 6: 1, 7: 2},
    )(1 - half, gradient, feedback, momentum, other, *outs)
    return tuple(outs)


def solution(mesh):
    placed = (
        P("dp", "tensor", None),
        P("dp", "tensor", None),
        P("tensor", None),
        P(None, "tensor"),
    )
    return jax.shard_map(
        on_device,
        mesh=mesh,
        in_specs=placed,
        out_specs=(P("dp", "tensor", None), P("tensor", None), P(None, "tensor")),
        check_vma=False,
    )
```

```python
import functools

import jax
import jax.numpy as jnp
from jax import lax
from jax.experimental import pallas as pl
from jax.experimental.pallas import tpu as pltpu
from jax.sharding import PartitionSpec as P

BETA = 0.9
HIGH = lax.Precision.HIGHEST

DP = 32
TP = 16
ROWS = 32
RANK = 64
LANES = 128
BLOCK = 16
GROUP = LANES // BLOCK
SPAN = BLOCK * TP
SHARD = DP * BLOCK
CHIPS = DP // 2
HALF = ROWS // 2
PART = ROWS // GROUP


def dot(left, right, left_dim, right_dim):
    return lax.dot_general(
        left,
        right,
        (((left_dim,), (right_dim,)), ((), ())),
        precision=HIGH,
        preferred_element_type=jnp.float32,
    )


def swap_blocks(parts):
    parts = list(parts)
    block = lax.broadcasted_iota(jnp.int32, parts[0].shape, 1) // BLOCK
    for step in (1, 2, 4):
        upper = (block & step) != 0
        for i in range(GROUP):
            if i & step:
                continue
            a, b = parts[i], parts[i | step]
            parts[i] = jnp.where(upper, pltpu.roll(b, step * BLOCK, 1), a)
            parts[i | step] = jnp.where(upper, b, pltpu.roll(a, LANES - step * BLOCK, 1))
    return parts


def merge_blocks(parts):
    block = lax.broadcasted_iota(jnp.int32, parts[0].shape, 1) // BLOCK
    at = [block == place for place in range(GROUP)]
    merged = []
    for tl in range(GROUP):
        part = parts[(GROUP - tl) % GROUP]
        for place in range(1, GROUP):
            part = jnp.where(at[place], parts[(place - tl) % GROUP], part)
        merged.append(pltpu.roll(part, (GROUP - tl) * BLOCK, 1) if tl else part)
    return merged


def gather_blocks(matrix, lane_block):
    block = lax.broadcasted_iota(jnp.int32, (8, LANES), 1) // BLOCK
    moved = pltpu.roll(matrix, (GROUP - lane_block) % GROUP * BLOCK, 1)
    out = jnp.zeros((8, LANES), jnp.float32)
    for kh in range(GROUP):
        piece = moved[kh * 8 : (kh + 1) * 8, :]
        if kh:
            piece = pltpu.roll(piece, kh * BLOCK, 1)
        out = jnp.where(block == kh, piece, out)
    return out


def columns(shard, half):
    return pl.ds(pl.multiple_of(shard * SHARD + half * SPAN, SPAN), SPAN)


def merge_kernel(t_ref, gradient, feedback, out):
    t = t_ref[0]
    for shard in range(TP):
        for half in range(2):
            start = shard * SHARD + half * SPAN
            lanes = slice(start, start + SPAN)
            chip = (shard - t + (4 - half) * (TP // 2)) % TP
            out[chip * 2 + (half ^ (t & 1))] = (
                gradient[0, :, lanes].astype(jnp.float32) + feedback[0, :, lanes]
            )


def half_kernel(half_ref, q_ref, out):
    out[...] = jnp.where(half_ref[0] == 0, q_ref[:, :SPAN], q_ref[:, SPAN:])


def factor_kernel(merged, q_part, out):
    total = merged[0]
    for d in range(1, DP):
        total = total + merged[d]
    q_twice = jnp.concatenate([q_part[...], q_part[...]], axis=0)
    factor = dot(total, q_twice, 1, 1)
    lane = lax.broadcasted_iota(jnp.int32, (HALF, LANES), 1)
    packed = jnp.where(lane < RANK, factor[:HALF], factor[HALF:])
    pieces = []
    for h in range(2):
        lanes = slice(h * LANES, (h + 1) * LANES)
        pieces += swap_blocks([total[g * PART : (g + 1) * PART, lanes] for g in range(GROUP)])
    for d in range(DP):
        for i in range(HALF // PART):
            out[d, i] = packed[i * PART : (i + 1) * PART]
        out[d, HALF // PART] = pieces[d // 2]


def unpack_rows(packed):
    return jnp.concatenate([packed[:, :RANK], packed[:, RANK:]], axis=0)


def project_kernel(core_ref, t_ref, parts, out):
    half = core_ref[0] ^ (t_ref[0] & 1)
    for i in range(HALF // PART):
        packed = parts[0, i]
        for d in range(1, DP):
            packed = packed + parts[d, i]
        out[i * PART : (i + 1) * PART, :] = packed
    for th in range(TP // GROUP):
        pieces = []
        for tl in range(GROUP):
            source = (th * GROUP + tl - t_ref[0] + (4 - half) * (TP // 2)) % TP
            pieces.append(parts[source * 2 + core_ref[0], HALF // PART])
        for g, piece in enumerate(swap_blocks(pieces)):
            start = HALF + th * ROWS + g * PART
            out[start : start + PART, :] = piece


def inverse_triangle(gram):
    size = 8
    count = RANK // size
    row = lax.broadcasted_iota(jnp.int32, (RANK, LANES), 0)
    lane = lax.broadcasted_iota(jnp.int32, (RANK, LANES), 1)
    identity = jnp.where(lane == row + RANK, 1.0, 0.0)
    work = jnp.concatenate([gram, jnp.zeros_like(gram)], axis=1) + identity
    work = [work[g * size : (g + 1) * size, :] for g in range(count)]
    row = lax.broadcasted_iota(jnp.int32, (size, LANES), 0)
    for b in range(count):
        spread = {
            g: [
                jnp.broadcast_to(work[g][:, b * size + k : b * size + k + 1], (size, LANES))
                for k in range(size)
            ]
            for g in range(b, count)
        }
        pivots = jnp.zeros((size, LANES), jnp.float32)
        for k in range(size):
            pivot_row = work[b][k : k + 1, :]
            heads = [spread[b][j][k : k + 1, :] for j in range(size)]
            pivots = jnp.where(row == k, heads[k], pivots)
            reciprocal = 1.0 / heads[k]
            for g in range(b, count):
                factor = spread[g][k] * reciprocal
                if g == b:
                    factor = jnp.where(row > k, factor, 0.0)
                work[g] = work[g] - factor * pivot_row
                for j in range(k + 1, size):
                    spread[g][j] = spread[g][j] - factor * heads[j]
        work[b] = work[b] * lax.rsqrt(pivots)
    return jnp.concatenate(work, axis=0)[:, RANK:]


def solve_kernel(chip_ref, t_ref, parts, out):
    t = t_ref[0]
    whole = unpack_rows(parts[:, :HALF, :].reshape(TP * HALF, LANES))
    whole_t = whole.T
    inverse = inverse_triangle(dot(whole_t, whole, 1, 0))
    basis = dot(unpack_rows(parts[t, :HALF, :]), inverse, 1, 1)
    tiles = []
    for th in range(TP // GROUP):
        start = HALF + th * ROWS
        halves = [parts[:, start + h * HALF : start + (h + 1) * HALF, :] for h in range(2)]
        tiles.append(
            jnp.concatenate([half.reshape(TP * HALF, LANES) for half in halves], axis=0)
        )
    sums = jnp.concatenate(tiles, axis=1)
    q_tile = dot(inverse, dot(whole_t, sums, 1, 0), 1, 0) * (1.0 / DP)
    approx = dot(basis, q_tile, 1, 0)
    mine = jnp.where(t // GROUP == 0, q_tile[:, :LANES], q_tile[:, LANES:])
    message = jnp.concatenate(
        [approx[:, :LANES], approx[:, LANES:], gather_blocks(mine, t % GROUP)], axis=0
    )
    message = pltpu.roll(message, chip_ref[0] % GROUP * BLOCK, 1)
    for chip in range(CHIPS):
        out[chip] = message


def finish_half(half_ref, gradient, feedback, momentum, parts, outs, scratch, sems):
    half = half_ref[0]
    new_feedback, new_momentum, q_out = outs
    feedback_part, momentum_part, q_part = scratch
    for group in range(CHIPS // GROUP):
        chips = range(group * GROUP, (group + 1) * GROUP)
        chunks = merge_blocks([parts[chip, 2 * ROWS :, :] for chip in chips])
        q_part[:, group * LANES : (group + 1) * LANES] = jnp.concatenate(chunks, axis=0)
    copies = [pltpu.make_async_copy(q_part, q_out.at[:, columns(0, half)], sems.at[2, 0])]
    copies[0].start()
    for th in range(TP // GROUP):
        rows = slice(th * ROWS, (th + 1) * ROWS)
        for group in range(CHIPS // GROUP):
            chips = range(group * GROUP, (group + 1) * GROUP)
            place = slice(group * LANES, (group + 1) * LANES)
            for tl, part in enumerate(merge_blocks([parts[chip, rows, :] for chip in chips])):
                shard = th * GROUP + tl
                start = shard * SHARD + half * SPAN + group * LANES
                lanes = pl.ds(pl.multiple_of(start, LANES), LANES)
                merged = gradient[0, :, lanes].astype(jnp.float32) + feedback[0, :, lanes]
                feedback_part[shard, :, place] = merged - part
                momentum_part[shard, :, place] = BETA * momentum[:, lanes] + part
                if group == CHIPS // GROUP - 1:
                    lanes = columns(shard, half)
                    copies += [
                        pltpu.make_async_copy(
                            feedback_part.at[shard], new_feedback.at[0, :, lanes], sems.at[0, shard]
                        ),
                        pltpu.make_async_copy(
                            momentum_part.at[shard], new_momentum.at[:, lanes], sems.at[1, shard]
                        ),
                    ]
                    copies[-2].start()
                    copies[-1].start()
    for copy in copies:
        copy.wait()


def finish_own_kernel(half_ref, gradient, feedback, momentum, parts, *refs):
    finish_half(half_ref, gradient, feedback, momentum, parts, refs[:3], refs[3:6], refs[6])


def finish_other_kernel(half_ref, gradient, feedback, momentum, parts, *refs):
    finish_half(half_ref, gradient, feedback, momentum, parts, refs[3:6], refs[6:9], refs[9])


def local(kernel, *shapes, scalars=0, inputs=1, scratch=(), flops=100_000, far=(), far_out=False, alias=None, room=32):
    vmem, anywhere = pl.BlockSpec(memory_space=pltpu.VMEM), pl.BlockSpec(memory_space=pltpu.HBM)
    return pl.pallas_call(
        kernel,
        out_shape=[jax.ShapeDtypeStruct(shape, jnp.float32) for shape in shapes],
        in_specs=[pl.BlockSpec(memory_space=pltpu.SMEM)] * scalars
        + [anywhere if i in far else vmem for i in range(inputs)],
        out_specs=[anywhere if far_out else vmem] * len(shapes),
        scratch_shapes=list(scratch),
        input_output_aliases=alias or {},
        cost_estimate=pl.CostEstimate(flops=flops, bytes_accessed=100_000, transcendentals=0),
        compiler_params=pltpu.CompilerParams(vmem_limit_bytes=room * 1024 * 1024),
    )


def exchange(parts, axis, groups=None):
    return lax.all_to_all(parts, axis, 0, 0, tiled=True, axis_index_groups=groups)


def swap_cores(parts):
    return lax.ppermute(parts, "dp", [(d, d ^ 1) for d in range(DP)])


def fetch_shards(parts):
    pairs = []
    for d in range(DP):
        for t in range(TP):
            plane = (t + d // 2 + (d & 1 ^ t & 1) * (TP // 2)) % TP
            pairs.append(((d ^ 1) * TP + plane, d * TP + t))
    return lax.ppermute(parts, ("dp", "tensor"), pairs)


def gather_lines(parts):
    lines = [
        [(chip * 2 + (t + v) % 2) * TP + t for t in range(TP)] for chip in range(CHIPS) for v in range(2)
    ]
    return lax.all_gather(parts, ("dp", "tensor"), axis_index_groups=lines)


def on_device(gradient, feedback, momentum, q_previous):
    d = lax.axis_index("dp").reshape(1)
    core, chip = d & 1, d >> 1
    t = lax.axis_index("tensor").reshape(1)
    chips = [list(range(c, DP, 2)) for c in range(2)]
    half = core ^ (t & 1)
    q_part = local(half_kernel, (RANK, SPAN), scalars=1)(core ^ ((t - chip + 1) & 1), q_previous)[0]
    q_part = fetch_shards(q_part)
    merged = local(merge_kernel, (DP, ROWS, SPAN), scalars=1, inputs=2, room=60)(
        t, gradient, feedback
    )[0]
    merged = exchange(merged, "dp")
    factor = local(factor_kernel, (DP, HALF // PART + 1, PART, LANES), inputs=2)(merged, q_part)[0]
    factor = exchange(factor, "dp")
    parts = local(project_kernel, (HALF + 2 * ROWS, LANES), scalars=2)(core, t, factor)[0]
    parts = gather_lines(parts)
    own = local(solve_kernel, (CHIPS, 2 * ROWS + 8, LANES), scalars=2)(chip, t, parts)[0]
    own = exchange(own, "dp", chips)
    other = swap_cores(own)
    shapes = (feedback.shape, momentum.shape, q_previous.shape)
    scratch = [
        pltpu.VMEM((TP, ROWS, SPAN), jnp.float32),
        pltpu.VMEM((TP, ROWS, SPAN), jnp.float32),
        pltpu.VMEM((RANK, SPAN), jnp.float32),
        pltpu.SemaphoreType.DMA((3, TP)),
    ]
    outs = local(
        finish_own_kernel, *shapes, scalars=1, inputs=4, scratch=scratch, far_out=True
    )(half, gradient, feedback, momentum, own)
    outs = local(
        finish_other_kernel,
        *shapes,
        scalars=1,
        inputs=7,
        scratch=scratch,
        far=(4, 5, 6),
        far_out=True,
        alias={5: 0, 6: 1, 7: 2},
    )(1 - half, gradient, feedback, momentum, other, *outs)
    return tuple(outs)


def solution(mesh):
    placed = (
        P("dp", "tensor", None),
        P("dp", "tensor", None),
        P("tensor", None),
        P(None, "tensor"),
    )
    return jax.shard_map(
        on_device,
        mesh=mesh,
        in_specs=placed,
        out_specs=(P("dp", "tensor", None), P("tensor", None), P(None, "tensor")),
        check_vma=False,
    )
```
